256 devices in a mesh: member: 16 (over y_lo, z), lat: 4 (over x), lon: 4 (over y_hi, core).
Axes of the slice: x: 4, y: 4 (y_hi: 2, y_lo: 2; y = y_hi * 2 + y_lo), z: 8, core: 2. Of those that a mesh axis runs over, the one named last changes fastest.
Arguments:
- embeddings: bfloat16 [16, 83, 32, 512], P('member', None, 'lat', 'lon'), may hold values from -6 to 6
- entry_perturbation: bfloat16 [16, 83, 32, 512], P('member', None, 'lat', 'lon'), may hold values from -6 to 6
- target: bfloat16 [83, 32, 512], P(None, 'lat', 'lon'), may hold values from -9 to 9
- feature_scale_factor: float32 [83], replicated, may hold values from 0.5 to 1.5
- first_stencil_kernel: bfloat16 [9, 192, 83], replicated, may hold values from -0.21875 to 0.21875
- second_stencil_kernel: bfloat16 [9, 83, 192], replicated, may hold values from -0.15625 to 0.15625
Outputs:
- embedding_sensitivities: bfloat16 [16, 83, 32, 512], P('member', None, 'lat', 'lon')
- grad_weight_in: float32 [9, 192, 83], replicated
- grad_weight_out: float32 [9, 83, 192], replicated
The draws below stay inside these ranges and needn't reach their ends.
All inputs are finite; a program needn't handle non-finite values.
Results may differ from the reference program's by a relative error of at most 0.0069.
Values may be sent and summed in bfloat16 or wider, within the bound.
No kernel may reach another device: no remote copies, remote signals or barrier semaphores. Data moves between devices by JAX's collectives and lax.ppermute only.
A program may use at most 64 MiB of HBM per device.

```python
import jax
import jax.numpy as jnp
from jax import lax

C = 83
HID = 192
ENSEMBLE_SIZE = 16
MERIDIAN_LINES = 32
PARALLEL_POINTS = 512


def block_levels(key, dims, pieces, least, top_value):
    factor_of, own = 1.0, jax.random.fold_in(key, 6)
    for dim, shards_of in pieces:
        steps = jnp.exp(jax.random.uniform(jax.random.fold_in(own, dim), (shards_of,), jnp.float32, least / len(pieces), top_value / len(pieces)))
        factor_of = factor_of * jnp.repeat(steps, dims[dim] // shards_of).reshape([-1 if axis == dim else 1 for axis in range(len(dims))])
    return factor_of


def noise(own_key, dims, scale, reach, shards=(), kind=jnp.bfloat16):
    level = block_levels(own_key, dims, shards, -0.22, 0.18) if shards else 1.0
    values = jax.random.normal(own_key, dims, jnp.float32) * scale * level
    return jnp.minimum(jnp.maximum(values, -reach), reach).astype(kind)


def setup_inputs(seed: int = 0) -> dict:
    arg_keys = jax.random.split(jax.random.key(seed), 7)
    return {
        "embeddings": noise(arg_keys[0], (ENSEMBLE_SIZE, C, MERIDIAN_LINES, PARALLEL_POINTS), 1.0, 6.0, ((0, 16), (2, 4), (3, 4))),
        "entry_perturbation": noise(arg_keys[1], (ENSEMBLE_SIZE, C, MERIDIAN_LINES, PARALLEL_POINTS), 1.0, 6.0, ((0, 16), (2, 4), (3, 4))),
        "target": noise(arg_keys[2], (C, MERIDIAN_LINES, PARALLEL_POINTS), 1.5, 9.0, ((1, 4), (2, 4))),
        "feature_scale_factor": jnp.clip(1.0 + 0.1 * jax.random.normal(arg_keys[3], (C,), jnp.float32), 0.5, 1.5),
        "first_stencil_kernel": noise(arg_keys[4], (9, HID, C), (9 * C) ** -0.5, 0.21875),
        "second_stencil_kernel": noise(arg_keys[5], (9, C, HID), (9 * HID) ** -0.5, 0.15625),
    }


soft_eps = 0.01

def differentiable_derivative(values):
    return values / jnp.sqrt(values * values + soft_eps)

def normalize(embedded_map, feature_scale_factor):
    average = lax.optimization_barrier(jnp.mean(embedded_map, axis=0, keepdims=True))
    centered = embedded_map - average
    variance = lax.optimization_barrier(jnp.mean(centered * centered, axis=0, keepdims=True))
    return centered * lax.rsqrt(variance + 1e-05) * feature_scale_factor[:, None, None]

def window_cells(padded, row_off, col_off, block_height, block_breadth):
    return padded[:, row_off:row_off + block_height, col_off:col_off + block_breadth].reshape(padded.shape[0], block_height * block_breadth)

def apply_stencil_layers(padded, weight, block_height, block_breadth):
    totals = None
    for offset in range(9):
        partial_value = jnp.dot(weight[offset], window_cells(padded, offset // 3, offset % 3, block_height, block_breadth), preferred_element_type=jnp.float32)
        totals = partial_value if totals is None else totals + partial_value
    return totals.reshape(weight.shape[1], block_height, block_breadth)

def transpose_conv(padded, weight, block_height, block_breadth):
    totals = None
    for offset in range(9):
        partial_value = jnp.dot(weight[offset].T, window_cells(padded, 2 - offset // 3, 2 - offset % 3, block_height, block_breadth), preferred_element_type=jnp.float32)
        totals = partial_value if totals is None else totals + partial_value
    return totals.reshape(weight.shape[2], block_height, block_breadth)

def weight_grad(grad_out, padded, block_height, block_breadth):
    flat_grad = grad_out.reshape(grad_out.shape[0], block_height * block_breadth)
    terms = []
    for offset in range(9):
        terms.append(jnp.dot(flat_grad, window_cells(padded, offset // 3, offset % 3, block_height, block_breadth).T, preferred_element_type=jnp.float32))
    return jnp.stack(terms)

def periodic_globe_border(values):
    wide = jnp.concatenate([values[:, :, -1:], values, values[:, :, :1]], axis=2)
    return jnp.pad(wide, ((0, 0), (1, 1), (0, 0)))

def evaluate_ensemble_entry(lone_embedding, lone_perturbation, feature_scale_factor, first_stencil_kernel, second_stencil_kernel):
    embedded_map = lone_embedding.astype(jnp.float32) + lone_perturbation.astype(jnp.float32)
    rescaled_map = normalize(embedded_map, feature_scale_factor).astype(jnp.bfloat16)
    preceding_nonlinearity = apply_stencil_layers(periodic_globe_border(rescaled_map), first_stencil_kernel, MERIDIAN_LINES, PARALLEL_POINTS)
    intermediate_map = jax.nn.gelu(preceding_nonlinearity).astype(jnp.bfloat16)
    entry_prediction = embedded_map + apply_stencil_layers(periodic_globe_border(intermediate_map), second_stencil_kernel, MERIDIAN_LINES, PARALLEL_POINTS)
    return (embedded_map, rescaled_map, preceding_nonlinearity, intermediate_map, entry_prediction)

def reference(embeddings, entry_perturbation, target, feature_scale_factor, first_stencil_kernel, second_stencil_kernel):
    prediction_ensemble = lax.map(lambda entry_arguments: evaluate_ensemble_entry(entry_arguments[0], entry_arguments[1], feature_scale_factor, first_stencil_kernel, second_stencil_kernel)[4], (embeddings, entry_perturbation))
    measured_truth_values = target.astype(jnp.float32)

    def entry_sensitivity(entry_prediction):
        couple_difference_total = lax.optimization_barrier(jnp.sum(differentiable_derivative(entry_prediction[None] - prediction_ensemble), axis=0))
        return differentiable_derivative(entry_prediction - measured_truth_values) - couple_difference_total / (ENSEMBLE_SIZE - 1)
    prediction_sensitivities = lax.map(entry_sensitivity, prediction_ensemble)

    def reverse_mode_update(running, entry_arguments):
        lone_embedding, lone_perturbation, prediction_sensitivity = entry_arguments
        embedded_map, rescaled_map, preceding_nonlinearity, intermediate_map, entry_prediction = evaluate_ensemble_entry(lone_embedding, lone_perturbation, feature_scale_factor, first_stencil_kernel, second_stencil_kernel)
        truncated_sensitivity = prediction_sensitivity.astype(jnp.bfloat16)
        grad_hidden = transpose_conv(periodic_globe_border(truncated_sensitivity), second_stencil_kernel, MERIDIAN_LINES, PARALLEL_POINTS)
        unused, gelu_pull = jax.vjp(jax.nn.gelu, preceding_nonlinearity)
        grad_pre = gelu_pull(grad_hidden)[0].astype(jnp.bfloat16)
        rescaled_sensitivity = transpose_conv(periodic_globe_border(grad_pre), first_stencil_kernel, MERIDIAN_LINES, PARALLEL_POINTS)
        unused_two, rescale_reverse_mode = jax.vjp(lambda values: normalize(values, feature_scale_factor), embedded_map)
        embedding_sensitivity = (prediction_sensitivity + rescale_reverse_mode(rescaled_sensitivity)[0]).astype(jnp.bfloat16)
        grad_out = weight_grad(truncated_sensitivity, periodic_globe_border(intermediate_map), MERIDIAN_LINES, PARALLEL_POINTS)
        grad_in = weight_grad(grad_pre, periodic_globe_border(rescaled_map), MERIDIAN_LINES, PARALLEL_POINTS)
        return ((running[0] + grad_in, running[1] + grad_out), embedding_sensitivity)
    starting_totals = (jnp.zeros((9, HID, C), jnp.float32), jnp.zeros((9, C, HID), jnp.float32))
    accrued_totals, embedding_sensitivities = lax.scan(reverse_mode_update, starting_totals, (embeddings, entry_perturbation, prediction_sensitivities))
    grad_scale = 1.0 / jnp.sqrt(jnp.float32(ENSEMBLE_SIZE * MERIDIAN_LINES * PARALLEL_POINTS))
    return (embedding_sensitivities, accrued_totals[0] * grad_scale, accrued_totals[1] * grad_scale)
```

```python
import jax
import jax.numpy as jnp
from jax import lax
from jax.sharding import PartitionSpec as P

soft_eps = 0.01


def extended(block, sides, width, periodic):
    for axis, dim in sides:
        count = lax.axis_size(axis)
        forward = [(i, i + 1) for i in range(count - 1)]
        if periodic:
            forward.append((count - 1, 0))
        backward = [(target, source) for source, target in forward]
        low = lax.ppermute(
            lax.slice_in_dim(block, block.shape[dim] - width, None, axis=dim), axis, forward
        )
        high = lax.ppermute(lax.slice_in_dim(block, 0, width, axis=dim), axis, backward)
        block = jnp.concatenate([low, block, high], axis=dim)
    return block


def differentiable_derivative(values):
    return values / jnp.sqrt(values * values + soft_eps)


def normalize(embedded_map, feature_scale_factor):
    average = jnp.mean(embedded_map, axis=0, keepdims=True)
    centered = embedded_map - average
    variance = jnp.mean(centered * centered, axis=0, keepdims=True)
    return centered * lax.rsqrt(variance + 1e-05) * feature_scale_factor[:, None, None]


def window_cells(padded, row_off, col_off, block_height, block_breadth):
    return padded[:, row_off : row_off + block_height, col_off : col_off + block_breadth].reshape(
        padded.shape[0], block_height * block_breadth
    )


def apply_stencil_layers(padded, weight, block_height, block_breadth):
    totals = None
    for offset in range(9):
        partial_value = jnp.dot(
            weight[offset],
            window_cells(padded, offset // 3, offset % 3, block_height, block_breadth),
            preferred_element_type=jnp.float32,
        )
        totals = partial_value if totals is None else totals + partial_value
    return totals.reshape(weight.shape[1], block_height, block_breadth)


def transpose_conv(padded, weight, block_height, block_breadth):
    totals = None
    for offset in range(9):
        partial_value = jnp.dot(
            weight[offset].T,
            window_cells(padded, 2 - offset // 3, 2 - offset % 3, block_height, block_breadth),
            preferred_element_type=jnp.float32,
        )
        totals = partial_value if totals is None else totals + partial_value
    return totals.reshape(weight.shape[2], block_height, block_breadth)


def weight_grad(grad_out, padded, block_height, block_breadth):
    flat_grad = grad_out.reshape(grad_out.shape[0], block_height * block_breadth)
    terms = []
    for offset in range(9):
        terms.append(
            jnp.dot(
                flat_grad,
                window_cells(padded, offset // 3, offset % 3, block_height, block_breadth).T,
                preferred_element_type=jnp.float32,
            )
        )
    return jnp.stack(terms)


def summed_everywhere(grad_in, grad_out):
    tail = grad_out.shape[2] - 128
    rows_in = jnp.swapaxes(grad_in, 1, 2).reshape(-1, grad_in.shape[1])
    rows_out = grad_out.reshape(-1, grad_out.shape[2])
    count = rows_in.shape[0]
    packed = jnp.concatenate(
        [
            rows_in[:, :128],
            rows_out[:, :128],
            jnp.concatenate([rows_in[:, 128:], rows_out[:, 128:]], axis=1),
        ]
    )
    places = lax.axis_size("lat") * lax.axis_size("lon")
    members = lax.axis_size("member")
    height = -(-packed.shape[0] // (places * 16)) * 16
    packed = jnp.pad(packed, ((0, places * height - packed.shape[0]), (0, 0)))
    sent = packed.reshape(places, height, 128).astype(jnp.bfloat16)

    def swap(values, axes):
        return lax.all_to_all(values, axes, split_axis=0, concat_axis=0, tiled=True)

    def total(values):
        return jnp.sum(values.astype(jnp.float32), axis=0).astype(jnp.bfloat16)

    def everywhere(values, copies):
        return jnp.broadcast_to(values[None], (copies,) + values.shape)

    own = total(swap(sent, ("lat", "lon")))
    own = total(swap(everywhere(own, members), ("member",)))
    whole = swap(everywhere(own, places), ("lat", "lon")).reshape(-1, 128).astype(jnp.float32)
    shared = whole[2 * count : 3 * count]
    full_in = jnp.concatenate([whole[:count], shared[:, :tail]], axis=1)
    full_out = jnp.concatenate([whole[count : 2 * count], shared[:, tail:]], axis=1)
    return (
        jnp.swapaxes(full_in.reshape(9, -1, full_in.shape[1]), 1, 2),
        full_out.reshape(grad_out.shape),
    )


def with_rims(values, rim_width):
    lon_wide = extended(values, (("lon", 2),), rim_width, True)
    return extended(lon_wide, (("lat", 1),), rim_width, False)


def on_device(
    embeddings,
    entry_perturbation,
    target,
    feature_scale_factor,
    first_stencil_kernel,
    second_stencil_kernel,
):
    embedded_map = embeddings[0].astype(jnp.float32) + entry_perturbation[0].astype(jnp.float32)
    feature_depth, block_height, block_breadth = embedded_map.shape
    rescaled_map = normalize(embedded_map, feature_scale_factor).astype(jnp.bfloat16)
    normed_pad = with_rims(rescaled_map, 1)
    preceding_nonlinearity = apply_stencil_layers(
        normed_pad, first_stencil_kernel, block_height, block_breadth
    )
    padded_hidden = with_rims(jax.nn.gelu(preceding_nonlinearity).astype(jnp.bfloat16), 1)
    entry_prediction = embedded_map + apply_stencil_layers(
        padded_hidden, second_stencil_kernel, block_height, block_breadth
    )
    members = lax.axis_size("member")
    location_total = block_height * block_breadth
    location_vector = entry_prediction.reshape(feature_depth, location_total)
    measured_truth_values = target.astype(jnp.float32).reshape(feature_depth, location_total)
    cell_share = location_total // members
    spread = lax.all_to_all(
        location_vector[:, None, :], "member", split_axis=2, concat_axis=1, tiled=True
    )
    own_truth = lax.dynamic_slice_in_dim(
        measured_truth_values, lax.axis_index("member") * cell_share, cell_share, 1
    )

    def add_member(other, running):
        column = lax.dynamic_slice_in_dim(spread, other, 1, 1)
        return running + differentiable_derivative(spread - column)

    couple_difference_total = lax.fori_loop(0, members, add_member, jnp.zeros_like(spread))
    local_grad = differentiable_derivative(
        spread - own_truth[:, None, :]
    ) - couple_difference_total / (members - 1)
    location_sensitivity = lax.all_to_all(
        local_grad, "member", split_axis=1, concat_axis=2, tiled=True
    )
    prediction_sensitivity = location_sensitivity.reshape(
        feature_depth, block_height, block_breadth
    )
    truncated_sensitivity = prediction_sensitivity.astype(jnp.bfloat16)
    grad_hidden = transpose_conv(
        with_rims(truncated_sensitivity, 1), second_stencil_kernel, block_height, block_breadth
    )
    unused, gelu_pull = jax.vjp(jax.nn.gelu, preceding_nonlinearity)
    grad_pre = gelu_pull(grad_hidden)[0].astype(jnp.bfloat16)
    rescaled_sensitivity = transpose_conv(
        with_rims(grad_pre, 1), first_stencil_kernel, block_height, block_breadth
    )
    unused_two, rescale_reverse_mode = jax.vjp(
        lambda values: normalize(values, feature_scale_factor), embedded_map
    )
    embedding_sensitivities = (
        prediction_sensitivity + rescale_reverse_mode(rescaled_sensitivity)[0]
    ).astype(jnp.bfloat16)[None]
    grad_out = weight_grad(truncated_sensitivity, padded_hidden, block_height, block_breadth)
    grad_in = weight_grad(grad_pre, normed_pad, block_height, block_breadth)
    grad_in, grad_out = summed_everywhere(grad_in, grad_out)
    total_cells = (
        members * block_height * lax.axis_size("lat") * block_breadth * lax.axis_size("lon")
    )
    grad_scale = 1.0 / jnp.sqrt(jnp.float32(total_cells))
    return (embedding_sensitivities, grad_in * grad_scale, grad_out * grad_scale)


def solution(mesh):
    placed = (
        P("member", None, "lat", "lon"),
        P("member", None, "lat", "lon"),
        P(None, "lat", "lon"),
        P(),
        P(),
        P(),
    )
    return jax.shard_map(
        on_device,
        mesh=mesh,
        in_specs=placed,
        out_specs=(P("member", None, "lat", "lon"), P(), P()),
        check_vma=False,
    )
```

```python
import functools
import math

import jax
import jax.numpy as jnp
from jax import lax
from jax.experimental import pallas as pl
from jax.experimental.pallas import tpu as pltpu
from jax.sharding import PartitionSpec as P

soft_eps = 0.01
norm_eps = 1e-05
C = 83
CP = 88
CI = 96
HID = 192
ROWS = 8
COLS = 128
RIM = 4
PITCH = COLS + 2 * RIM
TALL = ROWS + 2 * RIM
FLAT = TALL * PITCH
TILES = FLAT // 128
SPREAD = (2, 15)
HIDDEN = (3, 14)
OWN = (4, 13)
MEMBERS = 16
PLACES = 16
CHUNK = 72
PIECE = 144
f32 = jnp.float32
bf16 = jnp.bfloat16
GELU_A = math.sqrt(2.0 / math.pi)
GELU_B = 0.044715
VMEM_LIMIT = 60 * 1024 * 1024


def call(kernel, outs, scratch, *operands, smem=0):
    specs = [pl.BlockSpec(memory_space=pltpu.SMEM)] * smem
    specs += [pl.BlockSpec(memory_space=pltpu.VMEM)] * (len(operands) - smem)
    return pl.pallas_call(
        kernel,
        out_shape=[jax.ShapeDtypeStruct(shape, kind) for shape, kind in outs],
        in_specs=specs,
        out_specs=[pl.BlockSpec(memory_space=pltpu.VMEM)] * len(outs),
        scratch_shapes=[pltpu.VMEM(shape, kind) for shape, kind in scratch],
        compiler_params=pltpu.CompilerParams(vmem_limit_bytes=VMEM_LIMIT),
    )(*operands)


def step_of(offset):
    return (offset // 3 - 1) * PITCH + offset % 3 - 1


def tile(index):
    return pl.ds(128 * index, 128)


def lanes_of(height):
    return lax.broadcasted_iota(jnp.int32, (height, 128), 1)


def rows_kernel(emb_ref, pert_ref, target_ref, own_ref, up_ref, down_ref, latent, truth):
    latent[...] = emb_ref[...].astype(f32) + pert_ref[...].astype(f32)
    truth[...] = target_ref[...].astype(f32)
    rest = jnp.zeros((CP - C, 128), f32)
    for r in range(ROWS):
        for base, source, sent in ((0, latent, RIM), (ROWS, truth, RIM // 2)):
            row = jnp.concatenate([source[pl.ds(r, C, stride=ROWS), :], rest], axis=0)
            own_ref[base + r] = row
            place = 0 if base == 0 else RIM
            if r < sent:
                up_ref[place + r] = row
            if r >= ROWS - sent:
                down_ref[place + r - (ROWS - sent)] = row


def latent_row(own_ref, top_ref, bottom_ref, row):
    if row < RIM:
        return top_ref[row]
    if row < RIM + ROWS:
        return own_ref[row - RIM]
    return bottom_ref[row - RIM - ROWS]


def truth_row(own_ref, top_ref, bottom_ref, row):
    half = RIM // 2
    if row < half:
        return top_ref[RIM + row]
    if row < half + ROWS:
        return own_ref[ROWS + row - half]
    return bottom_ref[RIM + row - half - ROWS]


def columns_kernel(own_ref, top_ref, bottom_ref, left_ref, right_ref):
    lane = lanes_of(CP)
    left = jnp.zeros((CP, 128), f32)
    right = jnp.zeros((CP, 128), f32)
    plan = [(latent_row, row, RIM * row, RIM) for row in range(TALL)]
    plan += [
        (truth_row, row, RIM * TALL + RIM // 2 * row, RIM // 2) for row in range(ROWS + RIM)
    ]
    for source, row, start, width in plan:
        values = source(own_ref, top_ref, bottom_ref, row)
        here = (lane >= start) & (lane < start + width)
        left = jnp.where(here, pltpu.roll(values, start % 128, 1), left)
        right = jnp.where(here, pltpu.roll(values, (start + width) % 128, 1), right)
    left_ref[...] = left
    right_ref[...] = right


def flat_tiles(pieces, first, last):
    lane = lanes_of(CP)
    rolled = {}
    for index in range(first, last):
        result = jnp.zeros((CP, 128), f32)
        for number, (values, lane_from, flat_to, width) in enumerate(pieces):
            low, high = max(flat_to - 128 * index, 0), min(flat_to + width - 128 * index, 128)
            if low >= high:
                continue
            if number not in rolled:
                shift = (flat_to - lane_from) % 128
                rolled[number] = pltpu.roll(values(), shift, 1) if shift else values()
            result = jnp.where((lane >= low) & (lane < high), rolled[number], result)
        yield index, result


def forward_kernel(
    own_ref, top_ref, bottom_ref, left_ref, right_ref, gain_ref, valid_ref, mine_ref, w1_ref, w2_ref,
    forecast_ref, truth_ref, pre_ref, hidden_ref, window_ref, latent_ref,
    latent, normed, window, hidden, partial,
):
    pieces, truths = [], []
    for row in range(TALL):
        pieces.append((functools.partial(latent_row, own_ref, top_ref, bottom_ref, row), 0, PITCH * row + RIM, COLS))
        pieces.append((lambda: left_ref[...], RIM * row, PITCH * row, RIM))
        pieces.append((lambda: right_ref[...], RIM * row, PITCH * row + RIM + COLS, RIM))
    half = RIM // 2
    for row in range(ROWS + RIM):
        flat, lane = PITCH * (row + half) + RIM, RIM * TALL + half * row
        truths.append((functools.partial(truth_row, own_ref, top_ref, bottom_ref, row), 0, flat, COLS))
        truths.append((lambda: left_ref[...], lane, flat - half, half))
        truths.append((lambda: right_ref[...], lane, flat + COLS, half))
    real = lax.broadcasted_iota(jnp.int32, (CP, 128), 0) < C
    gain = gain_ref[...]
    normed[CP:CI, :] = jnp.zeros((CI - CP, FLAT), f32)
    for index, values in flat_tiles(pieces, 0, TILES):
        latent[:, tile(index)] = values
        average = jnp.sum(values, axis=0, keepdims=True) * (1.0 / C)
        centered = jnp.where(real, values - average, 0.0)
        variance = jnp.sum(centered * centered, axis=0, keepdims=True) * (1.0 / C)
        scaled = centered * lax.rsqrt(variance + norm_eps) * gain
        normed[0:CP, tile(index)] = scaled * valid_ref[:, tile(index)]
    for index, values in flat_tiles(truths, *SPREAD):
        truth_ref[pl.ds(CP * (index - SPREAD[0]), CP), :] = values
    truth_ref[pl.ds(CP * (SPREAD[1] - SPREAD[0]), 8), :] = jnp.zeros((8, 128), f32)
    latent_ref[...] = latent[:, 128 * OWN[0] : 128 * OWN[1]]

    for group in range(CI // 16):
        values = normed[16 * group : 16 * group + 16, :]
        for offset in range(9):
            shift = -step_of(offset) % FLAT
            moved = pltpu.roll(values, shift, 1) if shift else values
            window[CI * offset + 16 * group : CI * offset + 16 * group + 16, :] = moved.astype(bf16)
    window_ref[...] = window[:, 128 * OWN[0] : 128 * OWN[1]]

    for first, last in ((0, 3), (3, 7), (7, 11), (11, 14), (14, 17)):
        span = slice(128 * first, 128 * last)
        pre = jnp.dot(w1_ref[...], window[:, span], preferred_element_type=f32)
        if first >= HIDDEN[0] and last <= HIDDEN[1]:
            pre_ref[:, 128 * (first - HIDDEN[0]) : 128 * (last - HIDDEN[0])] = pre
        curve = jnp.tanh(GELU_A * (pre + GELU_B * (pre * pre * pre)))
        hidden[:, span] = (0.5 * pre * (1.0 + curve) * valid_ref[:, span]).astype(bf16)
        partial[:, span] = jnp.dot(w2_ref[...], hidden[:, span], preferred_element_type=f32)
    hidden_ref[...] = (hidden[:, 128 * OWN[0] : 128 * OWN[1]].astype(f32) * mine_ref[...]).astype(bf16)

    for group in range(CP // 8):
        total = None
        for offset in range(9):
            start = CP * offset + 8 * group
            shift = -step_of(offset) % FLAT
            values = partial[start : start + 8, :]
            moved = pltpu.roll(values, shift, 1) if shift else values
            total = moved if total is None else total + moved
        for index in range(*SPREAD):
            start = CP * (index - SPREAD[0]) + 8 * group
            forecast_ref[start : start + 8, :] = (
                total[:, 128 * index : 128 * index + 128] + latent[8 * group : 8 * group + 8, tile(index)]
            )
    forecast_ref[pl.ds(CP * (SPREAD[1] - SPREAD[0]), 8), :] = jnp.zeros((8, 128), f32)


def soft_slope(values):
    return values * lax.rsqrt(values * values + soft_eps)


def score_kernel(member_ref, forecast_ref, truth_ref, grad_ref, grads):
    base = member_ref[0] * CHUNK

    def body(step, carry):
        span = pl.ds(pl.multiple_of(8 * step, 8), 8)
        truth = truth_ref[pl.ds(pl.multiple_of(base + 8 * step, 8), 8), :]
        values = [forecast_ref[m, span, :] for m in range(MEMBERS)]
        totals = [jnp.zeros((8, 128), f32)] * MEMBERS
        for first in range(MEMBERS):
            for second in range(first):
                slope = soft_slope(values[first] - values[second])
                totals[first] = totals[first] + slope
                totals[second] = totals[second] - slope
        for m in range(MEMBERS):
            grads[m, span, :] = soft_slope(values[m] - truth) - totals[m] * (1.0 / (MEMBERS - 1))
        return carry

    lax.fori_loop(0, CHUNK // 8, body, 0)
    grad_ref[...] = grads[...].astype(bf16)


def backward_kernel(
    grad_ref, pre_ref, hidden_ref, window_ref, latent_ref, gain_ref, valid_ref, mine_ref, w2_ref, w1_ref,
    states_ref, weights_ref,
    chunks, grad, window, grad_pre, partial, shifted, result, packed,
):
    for m in range(MEMBERS):
        chunks[CHUNK * m : CHUNK * m + CHUNK, :] = grad_ref[m].astype(f32)
    edge = 128 * SPREAD[0]
    grad[:, 0:edge] = jnp.zeros((CI, edge), f32)
    grad[:, 128 * SPREAD[1] :] = jnp.zeros((CI, FLAT - 128 * SPREAD[1]), f32)
    grad[CP:CI, :] = jnp.zeros((CI - CP, FLAT), f32)
    for index in range(*SPREAD):
        values = chunks[CP * (index - SPREAD[0]) : CP * (index - SPREAD[0]) + CP, :]
        grad[0:CP, tile(index)] = values * valid_ref[:, tile(index)]
    low, high = 128 * HIDDEN[0], 128 * HIDDEN[1]
    for group in range(CI // 16):
        values = grad[16 * group : 16 * group + 16, :]
        for offset in range(9):
            shift = step_of(offset) % FLAT
            moved = pltpu.roll(values, shift, 1) if shift else values
            window[CI * offset + 16 * group : CI * offset + 16 * group + 16, :] = moved[:, low:high].astype(bf16)
    inner = slice(128 * (OWN[0] - HIDDEN[0]), 128 * (OWN[1] - HIDDEN[0]))
    across = (((1,), (1,)), ((), ()))
    grad_out = lax.dot_general(window[:, inner], hidden_ref[...], across, preferred_element_type=f32)
    for k in range(9):
        values = grad_out[CI * k : CI * k + C, :]
        packed[C * (9 + k) : C * (10 + k), :] = values[:, 0:128]
        packed[C * (18 + k) : C * (19 + k), 64:128] = values[:, 128:192]
    for first, last in ((0, 4), (4, 8), (8, 11)):
        span = slice(128 * first, 128 * last)
        grad_hidden = jnp.dot(w2_ref[...], window[:, span], preferred_element_type=f32)
        pre = pre_ref[:, span]
        square = pre * pre
        curve = jnp.tanh(GELU_A * (pre + GELU_B * (square * pre)))
        slope = 0.5 * (1.0 + curve) + 0.5 * pre * (1.0 - curve * curve) * (GELU_A * (1.0 + 3.0 * GELU_B * square))
        live = valid_ref[:, low + 128 * first : low + 128 * last]
        grad_pre[:, span] = (grad_hidden * slope * live).astype(bf16)
        partial[:, span] = jnp.dot(w1_ref[...], grad_pre[:, span], preferred_element_type=f32)
    own_pre = (grad_pre[:, inner].astype(f32) * mine_ref[...]).astype(bf16)
    grad_in = lax.dot_general(window_ref[...], own_pre, across, preferred_element_type=f32)
    for k in range(9):
        values = grad_in[CI * k : CI * k + C, :]
        packed[C * k : C * (k + 1), :] = values[:, 0:128]
        packed[C * (18 + k) : C * (19 + k), 0:64] = values[:, 128:192]
    packed[27 * C :, :] = jnp.zeros((PLACES * PIECE - 27 * C, 128), f32)
    for place in range(PLACES):
        weights_ref[place] = packed[PIECE * place : PIECE * place + PIECE, :].astype(bf16)

    span = high - low
    for group in range(CP // 8):
        total = None
        for offset in range(9):
            start = CP * offset + 8 * group
            shift = step_of(offset) % span
            values = partial[start : start + 8, :]
            moved = pltpu.roll(values, shift, 1) if shift else values
            total = moved if total is None else total + moved
        shifted[8 * group : 8 * group + 8, :] = total[:, inner]
    real = lax.broadcasted_iota(jnp.int32, (CP, 128), 0) < C
    gain = gain_ref[...]
    for index in range(OWN[1] - OWN[0]):
        values = latent_ref[:, tile(index)]
        average = jnp.sum(values, axis=0, keepdims=True) * (1.0 / C)
        centered = jnp.where(real, values - average, 0.0)
        variance = jnp.sum(centered * centered, axis=0, keepdims=True) * (1.0 / C)
        scale = lax.rsqrt(variance + norm_eps)
        unit = centered * scale
        pull = shifted[:, tile(index)] * gain
        mean_pull = jnp.sum(pull, axis=0, keepdims=True) * (1.0 / C)
        mean_both = jnp.sum(pull * unit, axis=0, keepdims=True) * (1.0 / C)
        shifted[:, tile(index)] = (
            grad[0:CP, tile(index + OWN[0])] + scale * (pull - mean_pull - unit * mean_both)
        )
    lane = lanes_of(CP)
    for row in range(ROWS):
        start = PITCH * (row + RIM) + RIM - 128 * OWN[0]
        index, off = divmod(start, 128)
        values = shifted[:, tile(index)]
        if off:
            near = pltpu.roll(values, 128 - off, 1)
            far = pltpu.roll(shifted[:, tile(index + 1)], 128 - off, 1)
            values = jnp.where(lane < 128 - off, near, far)
        result[pl.ds(row, C, stride=ROWS), :] = values[0:C]
    states_ref[...] = result[...].astype(bf16)


def total_kernel(parts_ref, copies_ref):
    total = parts_ref[0].astype(f32)
    for index in range(1, parts_ref.shape[0]):
        total = total + parts_ref[index].astype(f32)
    total = total.astype(bf16)
    for index in range(copies_ref.shape[0]):
        copies_ref[index] = total


def weights_kernel(parts_ref, grad_in_ref, grad_out_ref, packed):
    scale = 1.0 / math.sqrt(MEMBERS * 32 * 512)
    for place in range(PLACES):
        packed[PIECE * place : PIECE * place + PIECE, :] = parts_ref[place].astype(f32) * scale
    for k in range(9):
        first = packed[C * k : C * (k + 1), :]
        second = packed[C * (9 + k) : C * (10 + k), :]
        shared = packed[C * (18 + k) : C * (19 + k), :]
        grad_out_ref[k, :, 0:128] = second
        grad_out_ref[k, :, 128:192] = shared[:, 64:128]
        grad_in_ref[k, 0:128, :] = first.T
        grad_in_ref[k, 128:192, :] = shared[:, 0:64].T


def neighbours(axis, periodic):
    count = lax.axis_size(axis)
    forward = [(i, i + 1) for i in range(count - 1)]
    if periodic:
        forward.append((count - 1, 0))
    return forward, [(target, source) for source, target in forward]


def swap(values, axes):
    return lax.all_to_all(values, axes, split_axis=0, concat_axis=0, tiled=True)


def on_device(
    embeddings,
    entry_perturbation,
    target,
    feature_scale_factor,
    first_stencil_kernel,
    second_stencil_kernel,
):
    def rows(values):
        return values.reshape(C * ROWS, COLS)

    def padded(weight, dim, size):
        pads = [(0, 0)] * 3
        pads[dim] = (0, size - weight.shape[dim])
        return jnp.pad(weight, pads)

    own, up, down = call(
        rows_kernel,
        [((2 * ROWS, CP, 128), f32), ((RIM + RIM // 2, CP, 128), f32), ((RIM + RIM // 2, CP, 128), f32)],
        [((C * ROWS, COLS), f32)] * 2,
        rows(embeddings), rows(entry_perturbation), rows(target),
    )
    forward, backward = neighbours("lat", False)
    top = lax.ppermute(down, "lat", forward)
    bottom = lax.ppermute(up, "lat", backward)
    to_left, to_right = call(
        columns_kernel, [((CP, 128), f32)] * 2, [], own, top, bottom
    )
    forward, backward = neighbours("lon", True)
    left = lax.ppermute(to_right, "lon", forward)
    right = lax.ppermute(to_left, "lon", backward)

    gain = jnp.broadcast_to(jnp.pad(feature_scale_factor, (0, CP - C))[:, None], (CP, 128))
    place = jnp.arange(FLAT, dtype=jnp.int32)
    row, column = place // PITCH - RIM, place % PITCH - RIM
    line = row + ROWS * lax.axis_index("lat")
    valid = ((line >= 0) & (line < ROWS * lax.axis_size("lat"))).astype(f32)[None]
    mine = ((row >= 0) & (row < ROWS) & (column >= 0) & (column < COLS)).astype(f32)[None]
    mine = mine[:, 128 * OWN[0] : 128 * OWN[1]]
    w1_stack = padded(first_stencil_kernel, 2, CI).transpose(1, 0, 2).reshape(HID, 9 * CI)
    w2_stack = padded(second_stencil_kernel, 1, CP).reshape(9 * CP, HID)
    w2_turned = padded(second_stencil_kernel, 1, CI).transpose(2, 0, 1).reshape(HID, 9 * CI)
    w1_turned = padded(first_stencil_kernel.transpose(0, 2, 1), 1, CP).reshape(9 * CP, HID)

    own_lanes = 128 * (OWN[1] - OWN[0])
    hidden_lanes = 128 * (HIDDEN[1] - HIDDEN[0])
    forecast, truth, pre, hidden, window, latent = call(
        forward_kernel,
        [
            ((MEMBERS * CHUNK, 128), f32),
            ((MEMBERS * CHUNK, 128), f32),
            ((HID, hidden_lanes), f32),
            ((HID, own_lanes), bf16),
            ((9 * CI, own_lanes), bf16),
            ((CP, own_lanes), f32),
        ],
        [
            ((CP, FLAT), f32),
            ((CI, FLAT), f32),
            ((9 * CI, FLAT), bf16),
            ((HID, FLAT), bf16),
            ((9 * CP, FLAT), f32),
        ],
        own, top, bottom, left, right, gain, valid, mine, w1_stack, w2_stack,
    )
    spread = swap(forecast.reshape(MEMBERS, CHUNK, 128), "member")
    member = lax.axis_index("member").astype(jnp.int32)[None]
    (grads,) = call(
        score_kernel,
        [((MEMBERS, CHUNK, 128), bf16)],
        [((MEMBERS, CHUNK, 128), f32)],
        member, spread, truth, smem=1,
    )
    grads = swap(grads, "member")
    states, weights = call(
        backward_kernel,
        [((C * ROWS, COLS), bf16), ((PLACES, PIECE, 128), bf16)],
        [
            ((MEMBERS * CHUNK, 128), f32),
            ((CI, FLAT), f32),
            ((9 * CI, hidden_lanes), bf16),
            ((HID, hidden_lanes), bf16),
            ((9 * CP, hidden_lanes), f32),
            ((CP, own_lanes), f32),
            ((C * ROWS, COLS), f32),
            ((PLACES * PIECE, 128), f32),
        ],
        grads, pre, hidden, window, latent, gain, valid, mine, w2_turned, w1_turned,
    )
    piece = (PIECE, 128)
    (copies,) = call(total_kernel, [((MEMBERS,) + piece, bf16)], [], swap(weights, ("lat", "lon")))
    (copies,) = call(total_kernel, [((PLACES,) + piece, bf16)], [], swap(copies, "member"))
    grad_in, grad_out = call(
        weights_kernel,
        [((9, HID, C), f32), ((9, C, HID), f32)],
        [((PLACES * PIECE, 128), f32)],
        swap(copies, ("lat", "lon")),
    )
    return (states.reshape(embeddings.shape), grad_in, grad_out)


def solution(mesh):
    placed = (
        P("member", None, "lat", "lon"),
        P("member", None, "lat", "lon"),
        P(None, "lat", "lon"),
        P(),
        P(),
        P(),
    )
    return jax.shard_map(
        on_device,
        mesh=mesh,
        in_specs=placed,
        out_specs=(P("member", None, "lat", "lon"), P(), P()),
        check_vma=False,
    )
```

```python
import functools
import math

import jax
import jax.numpy as jnp
from jax import lax
from jax.experimental import pallas as pl
from jax.experimental.pallas import tpu as pltpu
from jax.sharding import PartitionSpec as P

soft_eps = 0.01
norm_eps = 1e-05
C = 83
CP = 88
CI = 96
HID = 192
ROWS = 8
COLS = 128
RIM = 4
PITCH = COLS + 2 * RIM
TALL = ROWS + 2 * RIM
FLAT = TALL * PITCH
TILES = FLAT // 128
SPREAD = (2, 15)
HIDDEN = (3, 14)
OWN = (4, 13)
MEMBERS = 16
GROUPS = 64
CHUNK = 72
PIECE = 40
f32 = jnp.float32
bf16 = jnp.bfloat16
GELU_A = math.sqrt(2.0 / math.pi)
GELU_B = 0.044715


def call(kernel, limit, outs, scratch, *operands, smem=0):
    specs = [pl.BlockSpec(memory_space=pltpu.SMEM)] * smem
    specs += [pl.BlockSpec(memory_space=pltpu.VMEM)] * (len(operands) - smem)
    return pl.pallas_call(
        kernel,
        out_shape=[jax.ShapeDtypeStruct(shape, kind) for shape, kind in outs],
        in_specs=specs,
        out_specs=[pl.BlockSpec(memory_space=pltpu.VMEM)] * len(outs),
        scratch_shapes=[pltpu.VMEM(shape, kind) for shape, kind in scratch],
        compiler_params=pltpu.CompilerParams(vmem_limit_bytes=limit << 20),
    )(*operands)


def step_of(offset):
    return (offset // 3 - 1) * PITCH + offset % 3 - 1


def tile(index):
    return pl.ds(128 * index, 128)


def lanes_of(height):
    return lax.broadcasted_iota(jnp.int32, (height, 128), 1)


def rows_kernel(emb_ref, pert_ref, target_ref, own_ref, up_ref, down_ref, latent, truth):
    latent[...] = emb_ref[...].astype(f32) + pert_ref[...].astype(f32)
    truth[...] = target_ref[...].astype(f32)
    rest = jnp.zeros((CP - C, 128), f32)
    for r in range(ROWS):
        for base, source, sent in ((0, latent, RIM), (ROWS, truth, RIM // 2)):
            row = jnp.concatenate([source[pl.ds(r, C, stride=ROWS), :], rest], axis=0)
            own_ref[base + r] = row
            place = 0 if base == 0 else RIM
            if r < sent:
                up_ref[place + r] = row
            if r >= ROWS - sent:
                down_ref[place + r - (ROWS - sent)] = row


def latent_row(own_ref, top_ref, bottom_ref, row):
    if row < RIM:
        return top_ref[row]
    if row < RIM + ROWS:
        return own_ref[row - RIM]
    return bottom_ref[row - RIM - ROWS]


def truth_row(own_ref, top_ref, bottom_ref, row):
    half = RIM // 2
    if row < half:
        return top_ref[RIM + row]
    if row < half + ROWS:
        return own_ref[ROWS + row - half]
    return bottom_ref[RIM + row - half - ROWS]


def columns_kernel(own_ref, top_ref, bottom_ref, left_ref, right_ref):
    lane = lanes_of(CP)
    left = jnp.zeros((CP, 128), f32)
    right = jnp.zeros((CP, 128), f32)
    plan = [(latent_row, row, RIM * row, RIM) for row in range(TALL)]
    plan += [
        (truth_row, row, RIM * TALL + RIM // 2 * row, RIM // 2) for row in range(ROWS + RIM)
    ]
    for source, row, start, width in plan:
        values = source(own_ref, top_ref, bottom_ref, row)
        here = (lane >= start) & (lane < start + width)
        left = jnp.where(here, pltpu.roll(values, start % 128, 1), left)
        right = jnp.where(here, pltpu.roll(values, (start + width) % 128, 1), right)
    left_ref[...] = left
    right_ref[...] = right


def flat_tiles(pieces, first, last):
    lane = lanes_of(CP)
    rolled = {}
    for index in range(first, last):
        result = jnp.zeros((CP, 128), f32)
        for number, (values, lane_from, flat_to, width) in enumerate(pieces):
            low, high = max(flat_to - 128 * index, 0), min(flat_to + width - 128 * index, 128)
            if low >= high:
                continue
            if number not in rolled:
                shift = (flat_to - lane_from) % 128
                rolled[number] = pltpu.roll(values(), shift, 1) if shift else values()
            result = jnp.where((lane >= low) & (lane < high), rolled[number], result)
        yield index, result


def forward_kernel(
    member_ref, own_ref, top_ref, bottom_ref, left_ref, right_ref, gain_ref, valid_ref, mine_ref, w1_ref, w2_ref,
    forecast_ref, truth_ref, pre_ref, hidden_ref, window_ref, latent_ref,
    latent, normed, window, hidden, partial, truth,
):
    pieces, truths = [], []
    for row in range(TALL):
        pieces.append((functools.partial(latent_row, own_ref, top_ref, bottom_ref, row), 0, PITCH * row + RIM, COLS))
        pieces.append((lambda: left_ref[...], RIM * row, PITCH * row, RIM))
        pieces.append((lambda: right_ref[...], RIM * row, PITCH * row + RIM + COLS, RIM))
    half = RIM // 2
    for row in range(ROWS + RIM):
        flat, lane = PITCH * (row + half) + RIM, RIM * TALL + half * row
        truths.append((functools.partial(truth_row, own_ref, top_ref, bottom_ref, row), 0, flat, COLS))
        truths.append((lambda: left_ref[...], lane, flat - half, half))
        truths.append((lambda: right_ref[...], lane, flat + COLS, half))
    real = lax.broadcasted_iota(jnp.int32, (CP, 128), 0) < C
    gain = gain_ref[...]
    normed[CP:CI, :] = jnp.zeros((CI - CP, FLAT), f32)
    for index, values in flat_tiles(pieces, 0, TILES):
        latent[:, tile(index)] = values
        average = jnp.sum(values, axis=0, keepdims=True) * (1.0 / C)
        centered = jnp.where(real, values - average, 0.0)
        variance = jnp.sum(centered * centered, axis=0, keepdims=True) * (1.0 / C)
        scaled = centered * lax.rsqrt(variance + norm_eps) * gain
        normed[0:CP, tile(index)] = scaled * valid_ref[:, tile(index)]
    for index, values in flat_tiles(truths, *SPREAD):
        truth[pl.ds(CP * (index - SPREAD[0]), CP), :] = values
    truth[pl.ds(CP * (SPREAD[1] - SPREAD[0]), 8), :] = jnp.zeros((8, 128), f32)
    truth_ref[...] = truth[pl.ds(pl.multiple_of(member_ref[0] * CHUNK, 8), CHUNK), :]
    latent_ref[...] = latent[:, 128 * OWN[0] : 128 * OWN[1]]

    for group in range(CI // 16):
        values = normed[16 * group : 16 * group + 16, :]
        for offset in range(9):
            shift = -step_of(offset) % FLAT
            moved = pltpu.roll(values, shift, 1) if shift else values
            window[CI * offset + 16 * group : CI * offset + 16 * group + 16, :] = moved.astype(bf16)
    window_ref[...] = window[:, 128 * OWN[0] : 128 * OWN[1]]

    for first, last in ((0, 3), (3, 7), (7, 11), (11, 14), (14, 17)):
        span = slice(128 * first, 128 * last)
        pre = jnp.dot(w1_ref[...], window[:, span], preferred_element_type=f32)
        if first >= HIDDEN[0] and last <= HIDDEN[1]:
            pre_ref[:, 128 * (first - HIDDEN[0]) : 128 * (last - HIDDEN[0])] = pre
        curve = jnp.tanh(GELU_A * (pre + GELU_B * (pre * pre * pre)))
        hidden[:, span] = (0.5 * pre * (1.0 + curve) * valid_ref[:, span]).astype(bf16)
        partial[:, span] = jnp.dot(w2_ref[...], hidden[:, span], preferred_element_type=f32)
    hidden_ref[...] = (hidden[:, 128 * OWN[0] : 128 * OWN[1]].astype(f32) * mine_ref[...]).astype(bf16)

    for group in range(CP // 8):
        total = None
        for offset in range(9):
            start = CP * offset + 8 * group
            shift = -step_of(offset) % FLAT
            values = partial[start : start + 8, :]
            moved = pltpu.roll(values, shift, 1) if shift else values
            total = moved if total is None else total + moved
        for index in range(*SPREAD):
            start = CP * (index - SPREAD[0]) + 8 * group
            forecast_ref[start : start + 8, :] = (
                total[:, 128 * index : 128 * index + 128] + latent[8 * group : 8 * group + 8, tile(index)]
            )
    forecast_ref[pl.ds(CP * (SPREAD[1] - SPREAD[0]), 8), :] = jnp.zeros((8, 128), f32)


def soft_slope(values):
    return values * lax.rsqrt(values * values + soft_eps)


def score_kernel(forecast_ref, truth_ref, grad_ref, grads):
    def body(step, carry):
        span = pl.ds(pl.multiple_of(8 * step, 8), 8)
        truth = truth_ref[span, :]
        values = [forecast_ref[m, span, :] for m in range(MEMBERS)]
        totals = [jnp.zeros((8, 128), f32)] * MEMBERS
        for first in range(MEMBERS):
            for second in range(first):
                slope = soft_slope(values[first] - values[second])
                totals[first] = totals[first] + slope
                totals[second] = totals[second] - slope
        for m in range(MEMBERS):
            grads[m, span, :] = soft_slope(values[m] - truth) - totals[m] * (1.0 / (MEMBERS - 1))
        return carry

    lax.fori_loop(0, CHUNK // 8, body, 0)
    grad_ref[...] = grads[...].astype(bf16)


def backward_kernel(
    grad_ref, pre_ref, hidden_ref, window_ref, latent_ref, gain_ref, valid_ref, mine_ref, w2_ref, w1_ref,
    states_ref, weights_ref,
    chunks, grad, window, grad_pre, partial, shifted, result, packed,
):
    for m in range(MEMBERS):
        chunks[CHUNK * m : CHUNK * m + CHUNK, :] = grad_ref[m].astype(f32)
    edge = 128 * SPREAD[0]
    grad[:, 0:edge] = jnp.zeros((CI, edge), f32)
    grad[:, 128 * SPREAD[1] :] = jnp.zeros((CI, FLAT - 128 * SPREAD[1]), f32)
    grad[CP:CI, :] = jnp.zeros((CI - CP, FLAT), f32)
    for index in range(*SPREAD):
        values = chunks[CP * (index - SPREAD[0]) : CP * (index - SPREAD[0]) + CP, :]
        grad[0:CP, tile(index)] = values * valid_ref[:, tile(index)]
    low, high = 128 * HIDDEN[0], 128 * HIDDEN[1]
    for group in range(CI // 16):
        values = grad[16 * group : 16 * group + 16, :]
        for offset in range(9):
            shift = step_of(offset) % FLAT
            moved = pltpu.roll(values, shift, 1) if shift else values
            window[CI * offset + 16 * group : CI * offset + 16 * group + 16, :] = moved[:, low:high].astype(bf16)
    inner = slice(128 * (OWN[0] - HIDDEN[0]), 128 * (OWN[1] - HIDDEN[0]))
    across = (((1,), (1,)), ((), ()))
    grad_out = lax.dot_general(window[:, inner], hidden_ref[...], across, preferred_element_type=f32)
    for k in range(9):
        values = grad_out[CI * k : CI * k + C, :]
        packed[C * (9 + k) : C * (10 + k), :] = values[:, 0:128]
        packed[C * (18 + k) : C * (19 + k), 64:128] = values[:, 128:192]
    for first, last in ((0, 4), (4, 8), (8, 11)):
        span = slice(128 * first, 128 * last)
        grad_hidden = jnp.dot(w2_ref[...], window[:, span], preferred_element_type=f32)
        pre = pre_ref[:, span]
        square = pre * pre
        curve = jnp.tanh(GELU_A * (pre + GELU_B * (square * pre)))
        slope = 0.5 * (1.0 + curve) + 0.5 * pre * (1.0 - curve * curve) * (GELU_A * (1.0 + 3.0 * GELU_B * square))
        live = valid_ref[:, low + 128 * first : low + 128 * last]
        grad_pre[:, span] = (grad_hidden * slope * live).astype(bf16)
        partial[:, span] = jnp.dot(w1_ref[...], grad_pre[:, span], preferred_element_type=f32)
    own_pre = (grad_pre[:, inner].astype(f32) * mine_ref[...]).astype(bf16)
    grad_in = lax.dot_general(window_ref[...], own_pre, across, preferred_element_type=f32)
    for k in range(9):
        values = grad_in[CI * k : CI * k + C, :]
        packed[C * k : C * (k + 1), :] = values[:, 0:128]
        packed[C * (18 + k) : C * (19 + k), 0:64] = values[:, 128:192]
    packed[27 * C :, :] = jnp.zeros((GROUPS * PIECE - 27 * C, 128), f32)
    for place in range(GROUPS):
        weights_ref[place] = packed[PIECE * place : PIECE * place + PIECE, :].astype(bf16)

    span = high - low
    for group in range(CP // 8):
        total = None
        for offset in range(9):
            start = CP * offset + 8 * group
            shift = step_of(offset) % span
            values = partial[start : start + 8, :]
            moved = pltpu.roll(values, shift, 1) if shift else values
            total = moved if total is None else total + moved
        shifted[8 * group : 8 * group + 8, :] = total[:, inner]
    real = lax.broadcasted_iota(jnp.int32, (CP, 128), 0) < C
    gain = gain_ref[...]
    for index in range(OWN[1] - OWN[0]):
        values = latent_ref[:, tile(index)]
        average = jnp.sum(values, axis=0, keepdims=True) * (1.0 / C)
        centered = jnp.where(real, values - average, 0.0)
        variance = jnp.sum(centered * centered, axis=0, keepdims=True) * (1.0 / C)
        scale = lax.rsqrt(variance + norm_eps)
        unit = centered * scale
        pull = shifted[:, tile(index)] * gain
        mean_pull = jnp.sum(pull, axis=0, keepdims=True) * (1.0 / C)
        mean_both = jnp.sum(pull * unit, axis=0, keepdims=True) * (1.0 / C)
        shifted[:, tile(index)] = (
            grad[0:CP, tile(index + OWN[0])] + scale * (pull - mean_pull - unit * mean_both)
        )
    lane = lanes_of(CP)
    for row in range(ROWS):
        start = PITCH * (row + RIM) + RIM - 128 * OWN[0]
        index, off = divmod(start, 128)
        values = shifted[:, tile(index)]
        if off:
            near = pltpu.roll(values, 128 - off, 1)
            far = pltpu.roll(shifted[:, tile(index + 1)], 128 - off, 1)
            values = jnp.where(lane < 128 - off, near, far)
        result[pl.ds(row, C, stride=ROWS), :] = values[0:C]
    states_ref[...] = result[...].astype(bf16)


def total_kernel(parts_ref, copies_ref):
    total = parts_ref[0].astype(f32)
    for index in range(1, parts_ref.shape[0]):
        total = total + parts_ref[index].astype(f32)
    total = total.astype(bf16)
    for index in range(copies_ref.shape[0]):
        copies_ref[index] = total


def weights_kernel(parts_ref, grad_in_ref, grad_out_ref, packed):
    scale = 1.0 / math.sqrt(MEMBERS * 32 * 512)
    for place in range(GROUPS):
        packed[PIECE * place : PIECE * place + PIECE, :] = parts_ref[place].astype(f32) * scale
    for k in range(9):
        first = packed[C * k : C * (k + 1), :]
        second = packed[C * (9 + k) : C * (10 + k), :]
        shared = packed[C * (18 + k) : C * (19 + k), :]
        grad_out_ref[k, :, 0:128] = second
        grad_out_ref[k, :, 128:192] = shared[:, 64:128]
        grad_in_ref[k, :, 0:128] = first
        grad_in_ref[k, :, 128:192] = shared[:, 0:64]


def neighbours(axis, periodic):
    count = lax.axis_size(axis)
    forward = [(i, i + 1) for i in range(count - 1)]
    if periodic:
        forward.append((count - 1, 0))
    return forward, [(target, source) for source, target in forward]


def swap(values, axes):
    return lax.all_to_all(values, axes, split_axis=0, concat_axis=0, tiled=True)


def on_device(
    embeddings,
    entry_perturbation,
    target,
    feature_scale_factor,
    first_stencil_kernel,
    second_stencil_kernel,
):
    def rows(values):
        return values.reshape(C * ROWS, COLS)

    def padded(weight, dim, size):
        pads = [(0, 0)] * 3
        pads[dim] = (0, size - weight.shape[dim])
        return jnp.pad(weight, pads)

    own, up, down = call(
        rows_kernel,
        6,
        [((2 * ROWS, CP, 128), f32), ((RIM + RIM // 2, CP, 128), f32), ((RIM + RIM // 2, CP, 128), f32)],
        [((C * ROWS, COLS), f32)] * 2,
        rows(embeddings), rows(entry_perturbation), rows(target),
    )
    forward, backward = neighbours("lat", False)
    top = lax.ppermute(down, "lat", forward)
    bottom = lax.ppermute(up, "lat", backward)
    to_left, to_right = call(
        columns_kernel, 6, [((CP, 128), f32)] * 2, [], own, top, bottom
    )
    forward, backward = neighbours("lon", True)
    left = lax.ppermute(to_right, "lon", forward)
    right = lax.ppermute(to_left, "lon", backward)

    gain = jnp.broadcast_to(jnp.pad(feature_scale_factor, (0, CP - C))[:, None], (CP, 128))
    place = jnp.arange(FLAT, dtype=jnp.int32)
    row, column = place // PITCH - RIM, place % PITCH - RIM
    line = row + ROWS * lax.axis_index("lat")
    valid = ((line >= 0) & (line < ROWS * lax.axis_size("lat"))).astype(f32)[None]
    mine = ((row >= 0) & (row < ROWS) & (column >= 0) & (column < COLS)).astype(f32)[None]
    mine = mine[:, 128 * OWN[0] : 128 * OWN[1]]
    w1_stack = padded(first_stencil_kernel, 2, CI).transpose(1, 0, 2).reshape(HID, 9 * CI)
    w2_stack = padded(second_stencil_kernel, 1, CP).reshape(9 * CP, HID)
    w2_turned = padded(second_stencil_kernel, 1, CI).transpose(2, 0, 1).reshape(HID, 9 * CI)
    w1_turned = padded(first_stencil_kernel.transpose(0, 2, 1), 1, CP).reshape(9 * CP, HID)

    member = lax.axis_index("member").astype(jnp.int32)[None]
    own_lanes = 128 * (OWN[1] - OWN[0])
    hidden_lanes = 128 * (HIDDEN[1] - HIDDEN[0])
    forecast, truth, pre, hidden, window, latent = call(
        forward_kernel,
        26,
        [
            ((MEMBERS * CHUNK, 128), f32),
            ((CHUNK, 128), f32),
            ((HID, hidden_lanes), f32),
            ((HID, own_lanes), bf16),
            ((9 * CI, own_lanes), bf16),
            ((CP, own_lanes), f32),
        ],
        [
            ((CP, FLAT), f32),
            ((CI, FLAT), f32),
            ((9 * CI, FLAT), bf16),
            ((HID, FLAT), bf16),
            ((9 * CP, FLAT), f32),
            ((MEMBERS * CHUNK, 128), f32),
        ],
        member, own, top, bottom, left, right, gain, valid, mine, w1_stack, w2_stack, smem=1,
    )
    spread = swap(forecast.reshape(MEMBERS, CHUNK, 128), "member")
    (grads,) = call(
        score_kernel,
        6,
        [((MEMBERS, CHUNK, 128), bf16)],
        [((MEMBERS, CHUNK, 128), f32)],
        spread, truth,
    )
    grads = swap(grads, "member")
    states, weights = call(
        backward_kernel,
        24,
        [((C * ROWS, COLS), bf16), ((GROUPS, PIECE, 128), bf16)],
        [
            ((MEMBERS * CHUNK, 128), f32),
            ((CI, FLAT), f32),
            ((9 * CI, hidden_lanes), bf16),
            ((HID, hidden_lanes), bf16),
            ((9 * CP, hidden_lanes), f32),
            ((CP, own_lanes), f32),
            ((C * ROWS, COLS), f32),
            ((GROUPS * PIECE, 128), f32),
        ],
        grads, pre, hidden, window, latent, gain, valid, mine, w2_turned, w1_turned,
    )
    across, along = ("member", "lat"), "lon"
    piece = (PIECE, 128)
    (copies,) = call(total_kernel, 6, [((4,) + piece, bf16)], [], swap(weights, across))
    (copies,) = call(total_kernel, 6, [((GROUPS,) + piece, bf16)], [], swap(copies, along))
    grad_in, grad_out = call(
        weights_kernel,
        8,
        [((9, C, HID), f32), ((9, C, HID), f32)],
        [((GROUPS * PIECE, 128), f32)],
        swap(copies, across),
    )
    grad_in = grad_in.transpose(0, 2, 1)
    return (states.reshape(embeddings.shape), grad_in, grad_out)


def solution(mesh):
    placed = (
        P("member", None, "lat", "lon"),
        P("member", None, "lat", "lon"),
        P(None, "lat", "lon"),
        P(),
        P(),
        P(),
    )
    return jax.shard_map(
        on_device,
        mesh=mesh,
        in_specs=placed,
        out_specs=(P("member", None, "lat", "lon"), P(), P()),
        check_vma=False,
    )
```

```python
import functools
import math

import jax
import jax.numpy as jnp
from jax import lax
from jax.experimental import pallas as pl
from jax.experimental.pallas import tpu as pltpu
from jax.sharding import PartitionSpec as P

soft_eps = 0.01
norm_eps = 1e-05
C = 83
CP = 88
CI = 96
HID = 192
ROWS = 8
COLS = 128
RIM = 4
PITCH = COLS + 2 * RIM
TALL = ROWS + 2 * RIM
FLAT = TALL * PITCH
TILES = FLAT // 128
SPREAD = (2, 15)
HIDDEN = (3, 14)
OWN = (4, 13)
MEMBERS = 16
GROUPS = 32
RING = 8
CHUNK = 72
PIECE = 72
HALF = RIM // 2
f32 = jnp.float32
bf16 = jnp.bfloat16
GELU_A = math.sqrt(2.0 / math.pi)
GELU_B = 0.044715


def call(kernel, limit, outs, scratch, *operands, smem=0, far=(), copies=0):
    near = pl.BlockSpec(memory_space=pltpu.VMEM)
    away = pl.BlockSpec(memory_space=pltpu.HBM)
    specs = [pl.BlockSpec(memory_space=pltpu.SMEM)] * smem
    specs += [away if i in far else near for i in range(smem, len(operands))]
    kinds = [kind[0] if isinstance(kind, tuple) else kind for _, kind in outs]
    kept = [pltpu.VMEM(shape, kind) for shape, kind in scratch]
    return pl.pallas_call(
        kernel,
        out_shape=[jax.ShapeDtypeStruct(shape, kind) for (shape, _), kind in zip(outs, kinds)],
        in_specs=specs,
        out_specs=[away if isinstance(kind, tuple) else near for _, kind in outs],
        scratch_shapes=kept + ([pltpu.SemaphoreType.DMA((copies,))] if copies else []),
        compiler_params=pltpu.CompilerParams(vmem_limit_bytes=limit << 20),
    )(*operands)


def started(*pairs, semaphores):
    moves = [
        pltpu.make_async_copy(source, target, semaphores.at[i]) for i, (source, target) in enumerate(pairs)
    ]
    for move in moves:
        move.start()
    return moves


def gain_column(gain_ref):
    row = lax.broadcasted_iota(jnp.int32, (CP, C), 0)
    lane = lax.broadcasted_iota(jnp.int32, (CP, C), 1)
    spread = jnp.where(row == lane, jnp.broadcast_to(gain_ref[...], (CP, C)), 0.0)
    return jnp.sum(spread, axis=1, keepdims=True)


def centred(values):
    real = lax.broadcasted_iota(jnp.int32, (CP, 128), 0) < C
    average = jnp.sum(values, axis=0, keepdims=True) * (1.0 / C)
    centered = jnp.where(real, values - average, 0.0)
    variance = jnp.sum(centered * centered, axis=0, keepdims=True) * (1.0 / C)
    return centered, lax.rsqrt(variance + norm_eps)


def step_of(offset):
    return (offset // 3 - 1) * PITCH + offset % 3 - 1


def tile(index):
    return pl.ds(128 * index, 128)


def lanes_of(height):
    return lax.broadcasted_iota(jnp.int32, (height, 128), 1)


def rows_kernel(
    emb_ref, pert_ref, target_ref, gain_ref, own_ref, up_ref, down_ref, emb, pert, target, first, second, truth, semaphores,
):
    moves = started((emb_ref, emb), (pert_ref, pert), (target_ref, target), semaphores=semaphores)
    for move, source, wide in zip(moves, (emb, pert, target), (first, second, truth)):
        move.wait()
        wide[...] = source[...].astype(f32).reshape(C * ROWS, COLS)
    rest = jnp.zeros((CP - C, 128), f32)
    gain = gain_column(gain_ref)

    def row_of(source, r):
        return jnp.concatenate([source[pl.ds(r, C, stride=ROWS), :], rest], axis=0)

    for r in range(ROWS):
        parts = row_of(first, r), row_of(second, r)
        goal = row_of(truth, r)
        latent = parts[0] + parts[1]
        own_ref[r] = latent
        own_ref[ROWS + r] = goal
        sent, place = (up_ref, r) if r < RIM else (down_ref, ROWS - 1 - r)
        if place < HALF:
            near = r if r < RIM else r - (ROWS - HALF)
            sent[near] = parts[0].astype(bf16)
            sent[HALF + near] = parts[1].astype(bf16)
            sent[3 * HALF + near] = goal.astype(bf16)
        else:
            centered, scale = centred(latent)
            outer = r - HALF if r < RIM else r - RIM
            sent[2 * HALF + outer] = (centered * scale * gain).astype(bf16)


def latent_row(own_ref, top_ref, bottom_ref, row):
    def near(rim_ref, r):
        return rim_ref[r].astype(f32) + rim_ref[HALF + r].astype(f32)

    if row < HALF:
        return top_ref[2 * HALF + row].astype(f32)
    if row < RIM:
        return near(top_ref, row - HALF)
    if row < RIM + ROWS:
        return own_ref[row - RIM]
    if row < RIM + ROWS + HALF:
        return near(bottom_ref, row - RIM - ROWS)
    return bottom_ref[2 * HALF + row - RIM - ROWS - HALF].astype(f32)


def truth_row(own_ref, top_ref, bottom_ref, row):
    if row < HALF:
        return top_ref[3 * HALF + row].astype(f32)
    if row < HALF + ROWS:
        return own_ref[ROWS + row - HALF]
    return bottom_ref[3 * HALF + row - HALF - ROWS].astype(f32)


def columns_kernel(own_ref, top_ref, bottom_ref, left_ref, right_ref):
    lane = lanes_of(CP)
    left = jnp.zeros((CP, 128), f32)
    right = jnp.zeros((CP, 128), f32)
    plan = [(latent_row, row, RIM * row, RIM) for row in range(TALL)]
    plan += [
        (truth_row, row, RIM * TALL + RIM // 2 * row, RIM // 2) for row in range(ROWS + RIM)
    ]
    for source, row, start, width in plan:
        values = source(own_ref, top_ref, bottom_ref, row)
        here = (lane >= start) & (lane < start + width)
        left = jnp.where(here, pltpu.roll(values, start % 128, 1), left)
        right = jnp.where(here, pltpu.roll(values, (start + width) % 128, 1), right)
    left_ref[...] = left
    right_ref[...] = right


def flat_tiles(pieces, first, last):
    lane = lanes_of(CP)
    rolled = {}
    for index in range(first, last):
        result = jnp.zeros((CP, 128), f32)
        for number, (values, lane_from, flat_to, width) in enumerate(pieces):
            low, high = max(flat_to - 128 * index, 0), min(flat_to + width - 128 * index, 128)
            if low >= high:
                continue
            if number not in rolled:
                shift = (flat_to - lane_from) % 128
                rolled[number] = pltpu.roll(values(), shift, 1) if shift else values()
            result = jnp.where((lane >= low) & (lane < high), rolled[number], result)
        yield index, result


def forward_kernel(
    member_ref, own_ref, top_ref, bottom_ref, left_ref, right_ref, gain_ref, valid_ref, mine_ref, w1_ref, w2_ref,
    forecast_ref, truth_ref, pre_ref, hidden_ref, window_ref, latent_ref,
    latent, normed, window, hidden, partial, truth, pre_kept, hidden_kept, semaphores,
):
    pieces, truths = [], []
    for row in range(TALL):
        pieces.append((functools.partial(latent_row, own_ref, top_ref, bottom_ref, row), 0, PITCH * row + RIM, COLS))
        pieces.append((lambda: left_ref[...], RIM * row, PITCH * row, RIM))
        pieces.append((lambda: right_ref[...], RIM * row, PITCH * row + RIM + COLS, RIM))
    half = HALF
    for row in range(ROWS + RIM):
        flat, lane = PITCH * (row + half) + RIM, RIM * TALL + half * row
        truths.append((functools.partial(truth_row, own_ref, top_ref, bottom_ref, row), 0, flat, COLS))
        truths.append((lambda: left_ref[...], lane, flat - half, half))
        truths.append((lambda: right_ref[...], lane, flat + COLS, half))
    gain = gain_column(gain_ref)
    lane = lanes_of(CP)
    inner_low, inner_high = PITCH * HALF, PITCH * (TALL - HALF)
    normed[CP:CI, :] = jnp.zeros((CI - CP, FLAT), f32)
    for index, values in flat_tiles(pieces, 0, TILES):
        latent[:, tile(index)] = values
        start = 128 * index
        if start < inner_high and start + 128 > inner_low:
            centered, scale = centred(values)
            scaled = centered * scale * gain
            if start < inner_low or start + 128 > inner_high:
                inside = (lane >= inner_low - start) & (lane < inner_high - start)
                scaled = jnp.where(inside, scaled, values)
            values = scaled
        normed[0:CP, tile(index)] = values * valid_ref[:, tile(index)]
    own = pl.ds(128 * OWN[0], 128 * (OWN[1] - OWN[0]))
    moves = started((latent.at[:, own], latent_ref), semaphores=semaphores)
    for index, values in flat_tiles(truths, *SPREAD):
        truth[pl.ds(CP * (index - SPREAD[0]), CP), :] = values
    truth[pl.ds(CP * (SPREAD[1] - SPREAD[0]), 8), :] = jnp.zeros((8, 128), f32)
    truth_ref[...] = truth[pl.ds(pl.multiple_of(member_ref[0] * CHUNK, 8), CHUNK), :]

    for group in range(CI // 16):
        values = normed[16 * group : 16 * group + 16, :]
        for offset in range(9):
            shift = -step_of(offset) % FLAT
            moved = pltpu.roll(values, shift, 1) if shift else values
            window[CI * offset + 16 * group : CI * offset + 16 * group + 16, :] = moved.astype(bf16)
    moves += started((window.at[:, own], window_ref), semaphores=semaphores.at[1:2])

    for first, last in ((0, 3), (3, 7), (7, 11), (11, 14), (14, 17)):
        span = slice(128 * first, 128 * last)
        pre = jnp.dot(w1_ref[...], window[:, span], preferred_element_type=f32)
        if first >= HIDDEN[0] and last <= HIDDEN[1]:
            pre_kept[:, 128 * (first - HIDDEN[0]) : 128 * (last - HIDDEN[0])] = pre
        curve = jnp.tanh(GELU_A * (pre + GELU_B * (pre * pre * pre)))
        hidden[:, span] = (0.5 * pre * (1.0 + curve) * valid_ref[:, span]).astype(bf16)
        partial[:, span] = jnp.dot(w2_ref[...], hidden[:, span], preferred_element_type=f32)
    hidden_kept[...] = (hidden[:, 128 * OWN[0] : 128 * OWN[1]].astype(f32) * mine_ref[...]).astype(bf16)
    moves += started((pre_kept, pre_ref), (hidden_kept, hidden_ref), semaphores=semaphores.at[2:4])

    for group in range(CP // 8):
        total = None
        for offset in range(9):
            start = CP * offset + 8 * group
            shift = -step_of(offset) % FLAT
            values = partial[start : start + 8, :]
            moved = pltpu.roll(values, shift, 1) if shift else values
            total = moved if total is None else total + moved
        for index in range(*SPREAD):
            start = CP * (index - SPREAD[0]) + 8 * group
            forecast_ref[start : start + 8, :] = (
                total[:, 128 * index : 128 * index + 128] + latent[8 * group : 8 * group + 8, tile(index)]
            )
    forecast_ref[pl.ds(CP * (SPREAD[1] - SPREAD[0]), 8), :] = jnp.zeros((8, 128), f32)
    for move in moves:
        move.wait()


def soft_slope(values):
    return values * lax.rsqrt(values * values + soft_eps)


def score_kernel(forecast_ref, truth_ref, grad_ref, grads):
    def body(step, carry):
        span = pl.ds(pl.multiple_of(8 * step, 8), 8)
        truth = truth_ref[span, :]
        values = [forecast_ref[m, span, :] for m in range(MEMBERS)]
        totals = [jnp.zeros((8, 128), f32)] * MEMBERS
        for first in range(MEMBERS):
            for second in range(first):
                slope = soft_slope(values[first] - values[second])
                totals[first] = totals[first] + slope
                totals[second] = totals[second] - slope
        for m in range(MEMBERS):
            grads[m, span, :] = soft_slope(values[m] - truth) - totals[m] * (1.0 / (MEMBERS - 1))
        return carry

    lax.fori_loop(0, CHUNK // 8, body, 0)
    grad_ref[...] = grads[...].astype(bf16)


def backward_kernel(
    grad_ref, pre_far, hidden_far, window_far, valid_ref, mine_ref, w2_ref,
    grad_pre_ref, own_grad_ref, weights_ref,
    pre_ref, hidden_ref, window_ref, chunks, grad, window, grad_pre, packed, semaphores,
):
    moves = started((hidden_far, hidden_ref), (pre_far, pre_ref), (window_far, window_ref), semaphores=semaphores)
    for m in range(MEMBERS):
        chunks[CHUNK * m : CHUNK * m + CHUNK, :] = grad_ref[m].astype(f32)
    edge = 128 * SPREAD[0]
    grad[:, 0:edge] = jnp.zeros((CI, edge), f32)
    grad[:, 128 * SPREAD[1] :] = jnp.zeros((CI, FLAT - 128 * SPREAD[1]), f32)
    grad[CP:CI, :] = jnp.zeros((CI - CP, FLAT), f32)
    for index in range(*SPREAD):
        values = chunks[CP * (index - SPREAD[0]) : CP * (index - SPREAD[0]) + CP, :]
        grad[0:CP, tile(index)] = values * valid_ref[:, tile(index)]
    low, high = 128 * HIDDEN[0], 128 * HIDDEN[1]
    for group in range(CI // 16):
        values = grad[16 * group : 16 * group + 16, :]
        for offset in range(9):
            shift = step_of(offset) % FLAT
            moved = pltpu.roll(values, shift, 1) if shift else values
            window[CI * offset + 16 * group : CI * offset + 16 * group + 16, :] = moved[:, low:high].astype(bf16)
    own = pl.ds(128 * OWN[0], 128 * (OWN[1] - OWN[0]))
    later = started((grad.at[0:CP, own], own_grad_ref), semaphores=semaphores.at[3:4])
    inner = slice(128 * (OWN[0] - HIDDEN[0]), 128 * (OWN[1] - HIDDEN[0]))
    moves[0].wait()
    across = (((1,), (1,)), ((), ()))
    grad_out = lax.dot_general(window[:, inner], hidden_ref[...], across, preferred_element_type=f32)
    for k in range(9):
        values = grad_out[CI * k : CI * k + C, :]
        packed[C * (9 + k) : C * (10 + k), :] = values[:, 0:128]
        packed[C * (18 + k) : C * (19 + k), 64:128] = values[:, 128:192]
    moves[1].wait()
    for first, last in ((0, 4), (4, 8), (8, 11)):
        span = slice(128 * first, 128 * last)
        grad_hidden = jnp.dot(w2_ref[...], window[:, span], preferred_element_type=f32)
        pre = pre_ref[:, span]
        square = pre * pre
        curve = jnp.tanh(GELU_A * (pre + GELU_B * (square * pre)))
        slope = 0.5 * (1.0 + curve) + 0.5 * pre * (1.0 - curve * curve) * (GELU_A * (1.0 + 3.0 * GELU_B * square))
        live = valid_ref[:, low + 128 * first : low + 128 * last]
        grad_pre[:, span] = (grad_hidden * slope * live).astype(bf16)
    later += started((grad_pre, grad_pre_ref), semaphores=semaphores.at[4:5])
    own_pre = (grad_pre[:, inner].astype(f32) * mine_ref[...]).astype(bf16)
    moves[2].wait()
    grad_in = lax.dot_general(window_ref[...], own_pre, across, preferred_element_type=f32)
    for k in range(9):
        values = grad_in[CI * k : CI * k + C, :]
        packed[C * k : C * (k + 1), :] = values[:, 0:128]
        packed[C * (18 + k) : C * (19 + k), 0:64] = values[:, 128:192]
    packed[27 * C :, :] = jnp.zeros((GROUPS * PIECE - 27 * C, 128), f32)
    for place in range(GROUPS):
        weights_ref[place] = packed[PIECE * place : PIECE * place + PIECE, :].astype(bf16)
    for move in later:
        move.wait()


def states_kernel(
    grad_pre_far, grad_far, latent_far, gain_ref, w1_ref,
    states_ref,
    grad_pre, grad, latent, partial, shifted, result, semaphores,
):
    moves = started((grad_pre_far, grad_pre), (latent_far, latent), (grad_far, grad), semaphores=semaphores)
    span = 128 * (HIDDEN[1] - HIDDEN[0])
    inner = slice(128 * (OWN[0] - HIDDEN[0]), 128 * (OWN[1] - HIDDEN[0]))
    moves[0].wait()
    for first in range(0, span, 512):
        some = slice(first, min(first + 512, span))
        partial[:, some] = jnp.dot(w1_ref[...], grad_pre[:, some], preferred_element_type=f32)
    for group in range(CP // 8):
        total = None
        for offset in range(9):
            start = CP * offset + 8 * group
            shift = step_of(offset) % span
            values = partial[start : start + 8, :]
            moved = pltpu.roll(values, shift, 1) if shift else values
            total = moved if total is None else total + moved
        shifted[8 * group : 8 * group + 8, :] = total[:, inner]
    gain = gain_column(gain_ref)
    for move in moves[1:]:
        move.wait()
    for index in range(OWN[1] - OWN[0]):
        centered, scale = centred(latent[:, tile(index)])
        unit = centered * scale
        pull = shifted[:, tile(index)] * gain
        mean_pull = jnp.sum(pull, axis=0, keepdims=True) * (1.0 / C)
        mean_both = jnp.sum(pull * unit, axis=0, keepdims=True) * (1.0 / C)
        shifted[:, tile(index)] = grad[:, tile(index)] + scale * (pull - mean_pull - unit * mean_both)
    lane = lanes_of(CP)
    for row in range(ROWS):
        start = PITCH * (row + RIM) + RIM - 128 * OWN[0]
        index, off = divmod(start, 128)
        values = shifted[:, tile(index)]
        if off:
            near = pltpu.roll(values, 128 - off, 1)
            far = pltpu.roll(shifted[:, tile(index + 1)], 128 - off, 1)
            values = jnp.where(lane < 128 - off, near, far)
        result[pl.ds(row, C, stride=ROWS), :] = values[0:C]
    states_ref[...] = result[...].astype(bf16)


def total_kernel(parts_ref, copies_ref):
    total = parts_ref[0].astype(f32)
    for index in range(1, parts_ref.shape[0]):
        total = total + parts_ref[index].astype(f32)
    total = total.astype(bf16)
    for index in range(copies_ref.shape[0]):
        copies_ref[index] = total


def weights_kernel(parts_ref, grad_in_ref, grad_out_ref, packed):
    scale = 1.0 / math.sqrt(MEMBERS * 32 * 512)
    for place in range(GROUPS):
        packed[PIECE * place : PIECE * place + PIECE, :] = parts_ref[place].astype(f32) * scale
    for k in range(9):
        first = packed[C * k : C * (k + 1), :]
        second = packed[C * (9 + k) : C * (10 + k), :]
        shared = packed[C * (18 + k) : C * (19 + k), :]
        grad_out_ref[k, :, 0:128] = second
        grad_out_ref[k, :, 128:192] = shared[:, 64:128]
        grad_in_ref[k, :, 0:128] = first
        grad_in_ref[k, :, 128:192] = shared[:, 0:64]


def neighbours(axis, periodic):
    count = lax.axis_size(axis)
    forward = [(i, i + 1) for i in range(count - 1)]
    if periodic:
        forward.append((count - 1, 0))
    return forward, [(target, source) for source, target in forward]


def swap(values, axes):
    return lax.all_to_all(values, axes, split_axis=0, concat_axis=0, tiled=True)


def on_device(
    embeddings,
    entry_perturbation,
    target,
    feature_scale_factor,
    first_stencil_kernel,
    second_stencil_kernel,
):
    def padded(weight, dim, size):
        pads = [(0, 0)] * 3
        pads[dim] = (0, size - weight.shape[dim])
        return jnp.pad(weight, pads)

    member_axes, plane = ("half", "ring"), ("half", "lat", "lon")
    gain = feature_scale_factor[None]
    block = (C, ROWS, COLS)
    rim = ((4 * HALF, CP, 128), bf16)
    own, up, down = call(
        rows_kernel,
        6,
        [((2 * ROWS, CP, 128), f32), rim, rim],
        [(block, bf16)] * 3 + [((C * ROWS, COLS), f32)] * 3,
        embeddings.reshape(block), entry_perturbation.reshape(block), target, gain,
        far=(0, 1, 2), copies=3,
    )
    forward, backward = neighbours("lat", False)
    top = lax.ppermute(down, "lat", forward)
    bottom = lax.ppermute(up, "lat", backward)
    to_left, to_right = call(
        columns_kernel, 6, [((CP, 128), f32)] * 2, [], own, top, bottom
    )
    forward, backward = neighbours("lon", True)
    left = lax.ppermute(to_right, "lon", forward)
    right = lax.ppermute(to_left, "lon", backward)

    place = jnp.arange(FLAT, dtype=jnp.int32)
    row, column = place // PITCH - RIM, place % PITCH - RIM
    line = row + ROWS * lax.axis_index("lat")
    valid = ((line >= 0) & (line < ROWS * lax.axis_size("lat"))).astype(f32)[None]
    mine = ((row >= 0) & (row < ROWS) & (column >= 0) & (column < COLS)).astype(f32)[None]
    mine = mine[:, 128 * OWN[0] : 128 * OWN[1]]
    w1_stack = padded(first_stencil_kernel, 2, CI).transpose(1, 0, 2).reshape(HID, 9 * CI)
    w2_stack = padded(second_stencil_kernel, 1, CP).reshape(9 * CP, HID)
    w2_turned = padded(second_stencil_kernel, 1, CI).transpose(2, 0, 1).reshape(HID, 9 * CI)
    w1_turned = padded(first_stencil_kernel.transpose(0, 2, 1), 1, CP).reshape(9 * CP, HID)

    member = lax.axis_index(member_axes).astype(jnp.int32)[None]
    own_lanes = 128 * (OWN[1] - OWN[0])
    hidden_lanes = 128 * (HIDDEN[1] - HIDDEN[0])
    forecast, truth, pre, hidden, window, latent = call(
        forward_kernel,
        26,
        [
            ((MEMBERS * CHUNK, 128), f32),
            ((CHUNK, 128), f32),
            ((HID, hidden_lanes), (f32,)),
            ((HID, own_lanes), (bf16,)),
            ((9 * CI, own_lanes), (bf16,)),
            ((CP, own_lanes), (f32,)),
        ],
        [
            ((CP, FLAT), f32),
            ((CI, FLAT), f32),
            ((9 * CI, FLAT), bf16),
            ((HID, FLAT), bf16),
            ((9 * CP, FLAT), f32),
            ((MEMBERS * CHUNK, 128), f32),
            ((HID, hidden_lanes), f32),
            ((HID, own_lanes), bf16),
        ],
        member, own, top, bottom, left, right, gain, valid, mine, w1_stack, w2_stack,
        smem=1, copies=4,
    )
    spread = swap(forecast.reshape(MEMBERS, CHUNK, 128), member_axes)
    (grads,) = call(
        score_kernel,
        6,
        [((MEMBERS, CHUNK, 128), bf16)],
        [((MEMBERS, CHUNK, 128), f32)],
        spread, truth,
    )
    grads = swap(grads, member_axes)
    grad_pre, own_grad, weights = call(
        backward_kernel,
        22,
        [
            ((HID, hidden_lanes), (bf16,)),
            ((CP, own_lanes), (f32,)),
            ((GROUPS, PIECE, 128), bf16),
        ],
        [
            ((HID, hidden_lanes), f32),
            ((HID, own_lanes), bf16),
            ((9 * CI, own_lanes), bf16),
            ((MEMBERS * CHUNK, 128), f32),
            ((CI, FLAT), f32),
            ((9 * CI, hidden_lanes), bf16),
            ((HID, hidden_lanes), bf16),
            ((GROUPS * PIECE, 128), f32),
        ],
        grads, pre, hidden, window, valid, mine, w2_turned,
        far=(1, 2, 3), copies=5,
    )
    parts = swap(weights, plane)
    (states,) = call(
        states_kernel,
        14,
        [((C * ROWS, COLS), bf16)],
        [
            ((HID, hidden_lanes), bf16),
            ((CP, own_lanes), f32),
            ((CP, own_lanes), f32),
            ((9 * CP, hidden_lanes), f32),
            ((CP, own_lanes), f32),
            ((C * ROWS, COLS), f32),
        ],
        grad_pre, own_grad, latent, gain, w1_turned,
        far=(0, 1, 2), copies=3,
    )
    piece = (PIECE, 128)
    (copies,) = call(total_kernel, 6, [((RING,) + piece, bf16)], [], parts)
    (copies,) = call(total_kernel, 6, [((GROUPS,) + piece, bf16)], [], swap(copies, "ring"))
    grad_in, grad_out = call(
        weights_kernel,
        8,
        [((9, C, HID), f32), ((9, C, HID), f32)],
        [((GROUPS * PIECE, 128), f32)],
        swap(copies, plane),
    )
    grad_in = grad_in.transpose(0, 2, 1)
    return (states.reshape(embeddings.shape), grad_in, grad_out)


def solution(mesh):
    places = mesh.devices.reshape(MEMBERS // RING, RING, *mesh.devices.shape[1:])
    fine = jax.sharding.Mesh(places, ("half", "ring", "lat", "lon"))
    whole = P(("half", "ring"), None, "lat", "lon")
    return jax.shard_map(
        on_device,
        mesh=fine,
        in_specs=(whole, whole, P(None, "lat", "lon"), P(), P(), P()),
        out_specs=(whole, P(), P()),
        check_vma=False,
    )
```

```python
import functools
import math

import jax
import jax.numpy as jnp
from jax import lax
from jax.experimental import pallas as pl
from jax.experimental.pallas import tpu as pltpu
from jax.sharding import PartitionSpec as P

soft_eps = 0.01
norm_eps = 1e-05
C = 83
CP = 88
CI = 96
HID = 192
ROWS = 8
COLS = 128
RIM = 4
PITCH = COLS + 2 * RIM
TALL = ROWS + 2 * RIM
FLAT = TALL * PITCH
TILES = FLAT // 128
SPREAD = (2, 15)
HIDDEN = (3, 14)
OWN = (4, 13)
MEMBERS = 16
GROUPS = 32
RING = 8
CHUNK = 72
PIECE = 72
HALF = RIM // 2
f32 = jnp.float32
bf16 = jnp.bfloat16
GELU_A = math.sqrt(2.0 / math.pi)
GELU_B = 0.044715


def call(kernel, limit, outs, scratch, *operands, smem=0, far=(), close=(), home=(), copies=0):
    near = pl.BlockSpec(memory_space=pltpu.VMEM)
    away = pl.BlockSpec(memory_space=pltpu.HBM)
    specs = [pl.BlockSpec(memory_space=pltpu.SMEM)] * smem
    specs += [away if i in far else near for i in range(smem, len(operands))]
    kinds = [kind[0] if isinstance(kind, tuple) else kind for _, kind in outs]
    placed = {i: pltpu.VMEM for i in close} | {i: pltpu.HBM for i in (*far, *home)}
    operands = [
        pltpu.with_memory_space_constraint(operand, placed[i]) if i in placed else operand
        for i, operand in enumerate(operands)
    ]
    kept = [pltpu.VMEM(shape, kind) for shape, kind in scratch]
    return pl.pallas_call(
        kernel,
        out_shape=[
            (pltpu.HBM if isinstance(given, tuple) else jax.ShapeDtypeStruct)(shape, kind)
            for (shape, given), kind in zip(outs, kinds)
        ],
        in_specs=specs,
        out_specs=[away if isinstance(kind, tuple) else near for _, kind in outs],
        scratch_shapes=kept + ([pltpu.SemaphoreType.DMA((copies,))] if copies else []),
        compiler_params=pltpu.CompilerParams(vmem_limit_bytes=limit << 20),
    )(*operands)


def started(*pairs, semaphores):
    moves = [
        pltpu.make_async_copy(source, target, semaphores.at[i]) for i, (source, target) in enumerate(pairs)
    ]
    for move in moves:
        move.start()
    return moves


def gain_column(gain_ref):
    row = lax.broadcasted_iota(jnp.int32, (CP, C), 0)
    lane = lax.broadcasted_iota(jnp.int32, (CP, C), 1)
    spread = jnp.where(row == lane, jnp.broadcast_to(gain_ref[...], (CP, C)), 0.0)
    return jnp.sum(spread, axis=1, keepdims=True)


def centred(values):
    real = lax.broadcasted_iota(jnp.int32, (CP, 128), 0) < C
    average = jnp.sum(values, axis=0, keepdims=True) * (1.0 / C)
    centered = jnp.where(real, values - average, 0.0)
    variance = jnp.sum(centered * centered, axis=0, keepdims=True) * (1.0 / C)
    return centered, lax.rsqrt(variance + norm_eps)


def step_of(offset):
    return (offset // 3 - 1) * PITCH + offset % 3 - 1


def tile(index):
    return pl.ds(128 * index, 128)


def lanes_of(height):
    return lax.broadcasted_iota(jnp.int32, (height, 128), 1)


def rows_kernel(
    emb_ref, pert_ref, target_ref, gain_ref, own_ref, up_ref, down_ref, emb, pert, target, first, second, truth, semaphores,
):
    moves = started((emb_ref, emb), (pert_ref, pert), (target_ref, target), semaphores=semaphores)
    for move, source, wide in zip(moves, (emb, pert, target), (first, second, truth)):
        move.wait()
        wide[...] = source[...].astype(f32).reshape(C * ROWS, COLS)
    rest = jnp.zeros((CP - C, 128), f32)
    gain = gain_column(gain_ref)

    def row_of(source, r):
        return jnp.concatenate([source[pl.ds(r, C, stride=ROWS), :], rest], axis=0)

    for r in range(ROWS):
        parts = row_of(first, r), row_of(second, r)
        goal = row_of(truth, r)
        latent = parts[0] + parts[1]
        own_ref[r] = latent
        own_ref[ROWS + r] = goal
        sent, place = (up_ref, r) if r < RIM else (down_ref, ROWS - 1 - r)
        if place < HALF:
            near = r if r < RIM else r - (ROWS - HALF)
            sent[near] = parts[0].astype(bf16)
            sent[HALF + near] = parts[1].astype(bf16)
            sent[3 * HALF + near] = goal.astype(bf16)
        else:
            centered, scale = centred(latent)
            outer = r - HALF if r < RIM else r - RIM
            sent[2 * HALF + outer] = (centered * scale * gain).astype(bf16)


def latent_row(own_ref, top_ref, bottom_ref, row):
    def near(rim_ref, r):
        return rim_ref[r].astype(f32) + rim_ref[HALF + r].astype(f32)

    if row < HALF:
        return top_ref[2 * HALF + row].astype(f32)
    if row < RIM:
        return near(top_ref, row - HALF)
    if row < RIM + ROWS:
        return own_ref[row - RIM]
    if row < RIM + ROWS + HALF:
        return near(bottom_ref, row - RIM - ROWS)
    return bottom_ref[2 * HALF + row - RIM - ROWS - HALF].astype(f32)


def truth_row(own_ref, top_ref, bottom_ref, row):
    if row < HALF:
        return top_ref[3 * HALF + row].astype(f32)
    if row < HALF + ROWS:
        return own_ref[ROWS + row - HALF]
    return bottom_ref[3 * HALF + row - HALF - ROWS].astype(f32)


def columns_kernel(own_ref, top_ref, bottom_ref, left_ref, right_ref):
    lane = lanes_of(CP)
    left = jnp.zeros((CP, 128), f32)
    right = jnp.zeros((CP, 128), f32)
    plan = [(latent_row, row, RIM * row, RIM) for row in range(TALL)]
    plan += [
        (truth_row, row, RIM * TALL + RIM // 2 * row, RIM // 2) for row in range(ROWS + RIM)
    ]
    for source, row, start, width in plan:
        values = source(own_ref, top_ref, bottom_ref, row)
        here = (lane >= start) & (lane < start + width)
        left = jnp.where(here, pltpu.roll(values, start % 128, 1), left)
        right = jnp.where(here, pltpu.roll(values, (start + width) % 128, 1), right)
    left_ref[...] = left
    right_ref[...] = right


def flat_tiles(pieces, first, last):
    lane = lanes_of(CP)
    rolled = {}
    for index in range(first, last):
        result = jnp.zeros((CP, 128), f32)
        for number, (values, lane_from, flat_to, width) in enumerate(pieces):
            low, high = max(flat_to - 128 * index, 0), min(flat_to + width - 128 * index, 128)
            if low >= high:
                continue
            if number not in rolled:
                shift = (flat_to - lane_from) % 128
                rolled[number] = pltpu.roll(values(), shift, 1) if shift else values()
            result = jnp.where((lane >= low) & (lane < high), rolled[number], result)
        yield index, result


def forward_kernel(
    member_ref, own_ref, top_ref, bottom_ref, left_ref, right_ref, gain_ref, valid_ref, mine_ref, w1_ref, w2_ref,
    forecast_ref, truth_ref, pre_ref, hidden_ref, window_ref, latent_ref,
    latent, normed, window, hidden, partial, truth, pre_kept, hidden_kept, semaphores,
):
    pieces, truths = [], []
    for row in range(TALL):
        pieces.append((functools.partial(latent_row, own_ref, top_ref, bottom_ref, row), 0, PITCH * row + RIM, COLS))
        pieces.append((lambda: left_ref[...], RIM * row, PITCH * row, RIM))
        pieces.append((lambda: right_ref[...], RIM * row, PITCH * row + RIM + COLS, RIM))
    half = HALF
    for row in range(ROWS + RIM):
        flat, lane = PITCH * (row + half) + RIM, RIM * TALL + half * row
        truths.append((functools.partial(truth_row, own_ref, top_ref, bottom_ref, row), 0, flat, COLS))
        truths.append((lambda: left_ref[...], lane, flat - half, half))
        truths.append((lambda: right_ref[...], lane, flat + COLS, half))
    gain = gain_column(gain_ref)
    lane = lanes_of(CP)
    inner_low, inner_high = PITCH * HALF, PITCH * (TALL - HALF)
    normed[CP:CI, :] = jnp.zeros((CI - CP, FLAT), f32)
    for index, values in flat_tiles(pieces, 0, TILES):
        latent[:, tile(index)] = values
        start = 128 * index
        if start < inner_high and start + 128 > inner_low:
            centered, scale = centred(values)
            scaled = centered * scale * gain
            if start < inner_low or start + 128 > inner_high:
                inside = (lane >= inner_low - start) & (lane < inner_high - start)
                scaled = jnp.where(inside, scaled, values)
            values = scaled
        normed[0:CP, tile(index)] = values * valid_ref[:, tile(index)]
    own = pl.ds(128 * OWN[0], 128 * (OWN[1] - OWN[0]))
    moves = started((latent.at[:, own], latent_ref), semaphores=semaphores)
    for index, values in flat_tiles(truths, *SPREAD):
        truth[pl.ds(CP * (index - SPREAD[0]), CP), :] = values
    truth[pl.ds(CP * (SPREAD[1] - SPREAD[0]), 8), :] = jnp.zeros((8, 128), f32)
    truth_ref[...] = truth[pl.ds(pl.multiple_of(member_ref[0] * CHUNK, 8), CHUNK), :]

    for group in range(CI // 16):
        values = normed[16 * group : 16 * group + 16, :]
        for offset in range(9):
            shift = -step_of(offset) % FLAT
            moved = pltpu.roll(values, shift, 1) if shift else values
            window[CI * offset + 16 * group : CI * offset + 16 * group + 16, :] = moved.astype(bf16)
    moves += started((window.at[:, own], window_ref), semaphores=semaphores.at[1:2])

    for number, (first, last) in enumerate(((0, 3), (3, 7), (7, 11), (11, 14), (14, 17))):
        span = slice(128 * first, 128 * last)
        pre = jnp.dot(w1_ref[...], window[:, span], preferred_element_type=f32)
        if first >= HIDDEN[0] and last <= HIDDEN[1]:
            kept = pl.ds(128 * (first - HIDDEN[0]), 128 * (last - first))
            pre_kept[:, kept] = pre
            moves += started((pre_kept.at[:, kept], pre_ref.at[:, kept]), semaphores=semaphores.at[number + 2 : number + 3])
        curve = jnp.tanh(GELU_A * (pre + GELU_B * (pre * pre * pre)))
        hidden[:, span] = (0.5 * pre * (1.0 + curve) * valid_ref[:, span]).astype(bf16)
        partial[:, span] = jnp.dot(w2_ref[...], hidden[:, span], preferred_element_type=f32)
    hidden_kept[...] = (hidden[:, 128 * OWN[0] : 128 * OWN[1]].astype(f32) * mine_ref[...]).astype(bf16)
    moves += started((hidden_kept, hidden_ref), semaphores=semaphores.at[2:3])

    for group in range(CP // 8):
        total = None
        for offset in range(9):
            start = CP * offset + 8 * group
            shift = -step_of(offset) % FLAT
            values = partial[start : start + 8, :]
            moved = pltpu.roll(values, shift, 1) if shift else values
            total = moved if total is None else total + moved
        for index in range(*SPREAD):
            start = CP * (index - SPREAD[0]) + 8 * group
            forecast_ref[start : start + 8, :] = (
                total[:, 128 * index : 128 * index + 128] + latent[8 * group : 8 * group + 8, tile(index)]
            )
    forecast_ref[pl.ds(CP * (SPREAD[1] - SPREAD[0]), 8), :] = jnp.zeros((8, 128), f32)
    for move in moves:
        move.wait()


def soft_slope(values):
    return values * lax.rsqrt(values * values + soft_eps)


def score_kernel(forecast_ref, truth_ref, grad_ref, grads):
    def body(step, carry):
        span = pl.ds(pl.multiple_of(8 * step, 8), 8)
        truth = truth_ref[span, :]
        values = [forecast_ref[m, span, :] for m in range(MEMBERS)]
        totals = [jnp.zeros((8, 128), f32)] * MEMBERS
        for first in range(MEMBERS):
            for second in range(first):
                slope = soft_slope(values[first] - values[second])
                totals[first] = totals[first] + slope
                totals[second] = totals[second] - slope
        for m in range(MEMBERS):
            grads[m, span, :] = soft_slope(values[m] - truth) - totals[m] * (1.0 / (MEMBERS - 1))
        return carry

    lax.fori_loop(0, CHUNK // 8, body, 0)
    grad_ref[...] = grads[...].astype(bf16)


def backward_kernel(
    grad_ref, pre_far, hidden_far, window_far, valid_ref, mine_ref, w2_ref,
    grad_pre_ref, own_grad_ref, weights_ref,
    pre_ref, hidden_ref, window_ref, chunks, grad, window, grad_pre, packed, semaphores,
):
    moves = started((hidden_far, hidden_ref), (pre_far, pre_ref), (window_far, window_ref), semaphores=semaphores)
    for m in range(MEMBERS):
        chunks[CHUNK * m : CHUNK * m + CHUNK, :] = grad_ref[m].astype(f32)
    edge = 128 * SPREAD[0]
    grad[:, 0:edge] = jnp.zeros((CI, edge), f32)
    grad[:, 128 * SPREAD[1] :] = jnp.zeros((CI, FLAT - 128 * SPREAD[1]), f32)
    grad[CP:CI, :] = jnp.zeros((CI - CP, FLAT), f32)
    for index in range(*SPREAD):
        values = chunks[CP * (index - SPREAD[0]) : CP * (index - SPREAD[0]) + CP, :]
        grad[0:CP, tile(index)] = values * valid_ref[:, tile(index)]
    low, high = 128 * HIDDEN[0], 128 * HIDDEN[1]
    for group in range(CI // 16):
        values = grad[16 * group : 16 * group + 16, :]
        for offset in range(9):
            shift = step_of(offset) % FLAT
            moved = pltpu.roll(values, shift, 1) if shift else values
            window[CI * offset + 16 * group : CI * offset + 16 * group + 16, :] = moved[:, low:high].astype(bf16)
    own = pl.ds(128 * OWN[0], 128 * (OWN[1] - OWN[0]))
    later = started((grad.at[0:CP, own], own_grad_ref), semaphores=semaphores.at[3:4])
    inner = slice(128 * (OWN[0] - HIDDEN[0]), 128 * (OWN[1] - HIDDEN[0]))
    moves[0].wait()
    across = (((1,), (1,)), ((), ()))
    grad_out = lax.dot_general(window[:, inner], hidden_ref[...], across, preferred_element_type=f32)
    for k in range(9):
        values = grad_out[CI * k : CI * k + C, :]
        packed[C * (9 + k) : C * (10 + k), :] = values[:, 0:128]
        packed[C * (18 + k) : C * (19 + k), 64:128] = values[:, 128:192]
    moves[1].wait()
    for first, last in ((0, 4), (4, 8), (8, 11)):
        span = slice(128 * first, 128 * last)
        grad_hidden = jnp.dot(w2_ref[...], window[:, span], preferred_element_type=f32)
        pre = pre_ref[:, span]
        square = pre * pre
        curve = jnp.tanh(GELU_A * (pre + GELU_B * (square * pre)))
        slope = 0.5 * (1.0 + curve) + 0.5 * pre * (1.0 - curve * curve) * (GELU_A * (1.0 + 3.0 * GELU_B * square))
        live = valid_ref[:, low + 128 * first : low + 128 * last]
        grad_pre[:, span] = (grad_hidden * slope * live).astype(bf16)
    later += started((grad_pre, grad_pre_ref), semaphores=semaphores.at[4:5])
    own_pre = (grad_pre[:, inner].astype(f32) * mine_ref[...]).astype(bf16)
    moves[2].wait()
    grad_in = lax.dot_general(window_ref[...], own_pre, across, preferred_element_type=f32)
    for k in range(9):
        values = grad_in[CI * k : CI * k + C, :]
        packed[C * k : C * (k + 1), :] = values[:, 0:128]
        packed[C * (18 + k) : C * (19 + k), 0:64] = values[:, 128:192]
    packed[27 * C :, :] = jnp.zeros((GROUPS * PIECE - 27 * C, 128), f32)
    for place in range(GROUPS):
        weights_ref[place] = packed[PIECE * place : PIECE * place + PIECE, :].astype(bf16)
    for move in later:
        move.wait()


def states_kernel(
    grad_pre_far, grad_far, latent_far, gain_ref, w1_ref,
    states_ref,
    grad_pre, grad, latent, partial, shifted, result, semaphores,
):
    moves = started((grad_pre_far, grad_pre), (latent_far, latent), (grad_far, grad), semaphores=semaphores)
    span = 128 * (HIDDEN[1] - HIDDEN[0])
    inner = slice(128 * (OWN[0] - HIDDEN[0]), 128 * (OWN[1] - HIDDEN[0]))
    moves[0].wait()
    for first in range(0, span, 512):
        some = slice(first, min(first + 512, span))
        partial[:, some] = jnp.dot(w1_ref[...], grad_pre[:, some], preferred_element_type=f32)
    for group in range(CP // 8):
        total = None
        for offset in range(9):
            start = CP * offset + 8 * group
            shift = step_of(offset) % span
            values = partial[start : start + 8, :]
            moved = pltpu.roll(values, shift, 1) if shift else values
            total = moved if total is None else total + moved
        shifted[8 * group : 8 * group + 8, :] = total[:, inner]
    gain = gain_column(gain_ref)
    for move in moves[1:]:
        move.wait()
    for index in range(OWN[1] - OWN[0]):
        centered, scale = centred(latent[:, tile(index)])
        unit = centered * scale
        pull = shifted[:, tile(index)] * gain
        mean_pull = jnp.sum(pull, axis=0, keepdims=True) * (1.0 / C)
        mean_both = jnp.sum(pull * unit, axis=0, keepdims=True) * (1.0 / C)
        shifted[:, tile(index)] = grad[:, tile(index)] + scale * (pull - mean_pull - unit * mean_both)
    lane = lanes_of(CP)
    for row in range(ROWS):
        start = PITCH * (row + RIM) + RIM - 128 * OWN[0]
        index, off = divmod(start, 128)
        values = shifted[:, tile(index)]
        if off:
            near = pltpu.roll(values, 128 - off, 1)
            far = pltpu.roll(shifted[:, tile(index + 1)], 128 - off, 1)
            values = jnp.where(lane < 128 - off, near, far)
        result[pl.ds(row, C, stride=ROWS), :] = values[0:C]
    states_ref[...] = result[...].astype(bf16)


def total_kernel(parts_ref, copies_ref):
    total = parts_ref[0].astype(f32)
    for index in range(1, parts_ref.shape[0]):
        total = total + parts_ref[index].astype(f32)
    total = total.astype(bf16)
    for index in range(copies_ref.shape[0]):
        copies_ref[index] = total


def weights_kernel(parts_ref, grad_in_ref, grad_out_ref, packed):
    scale = 1.0 / math.sqrt(MEMBERS * 32 * 512)
    for place in range(GROUPS):
        packed[PIECE * place : PIECE * place + PIECE, :] = parts_ref[place].astype(f32) * scale
    for k in range(9):
        first = packed[C * k : C * (k + 1), :]
        second = packed[C * (9 + k) : C * (10 + k), :]
        shared = packed[C * (18 + k) : C * (19 + k), :]
        grad_out_ref[k, :, 0:128] = second
        grad_out_ref[k, :, 128:192] = shared[:, 64:128]
        grad_in_ref[k, :, 0:128] = first
        grad_in_ref[k, :, 128:192] = shared[:, 0:64]


def neighbours(axis, periodic):
    count = lax.axis_size(axis)
    forward = [(i, i + 1) for i in range(count - 1)]
    if periodic:
        forward.append((count - 1, 0))
    return forward, [(target, source) for source, target in forward]


def swap(values, axes):
    return lax.all_to_all(values, axes, split_axis=0, concat_axis=0, tiled=True)


def on_device(
    embeddings,
    entry_perturbation,
    target,
    feature_scale_factor,
    first_stencil_kernel,
    second_stencil_kernel,
):
    def padded(weight, dim, size):
        pads = [(0, 0)] * 3
        pads[dim] = (0, size - weight.shape[dim])
        return jnp.pad(weight, pads)

    member_axes, plane = ("half", "ring"), ("half", "lat", "lon")
    gain = feature_scale_factor[None]
    block = (C, ROWS, COLS)
    rim = ((4 * HALF, CP, 128), bf16)
    own, up, down = call(
        rows_kernel,
        6,
        [((2 * ROWS, CP, 128), f32), rim, rim],
        [(block, bf16)] * 3 + [((C * ROWS, COLS), f32)] * 3,
        embeddings.reshape(block), entry_perturbation.reshape(block), target, gain,
        far=(0, 1, 2), home=(3,), copies=3,
    )
    forward, backward = neighbours("lat", False)
    top = lax.ppermute(down, "lat", forward)
    bottom = lax.ppermute(up, "lat", backward)
    to_left, to_right = call(
        columns_kernel, 6, [((CP, 128), f32)] * 2, [], own, top, bottom, close=(0, 1, 2)
    )
    forward, backward = neighbours("lon", True)
    left = lax.ppermute(to_right, "lon", forward)
    right = lax.ppermute(to_left, "lon", backward)

    place = jnp.arange(FLAT, dtype=jnp.int32)
    row, column = place // PITCH - RIM, place % PITCH - RIM
    line = row + ROWS * lax.axis_index("lat")
    valid = ((line >= 0) & (line < ROWS * lax.axis_size("lat"))).astype(f32)[None]
    mine = ((row >= 0) & (row < ROWS) & (column >= 0) & (column < COLS)).astype(f32)[None]
    mine = mine[:, 128 * OWN[0] : 128 * OWN[1]]
    w1_stack = padded(first_stencil_kernel, 2, CI).transpose(1, 0, 2).reshape(HID, 9 * CI)
    w2_stack = padded(second_stencil_kernel, 1, CP).reshape(9 * CP, HID)
    w2_turned = padded(second_stencil_kernel, 1, CI).transpose(2, 0, 1).reshape(HID, 9 * CI)
    w1_turned = padded(first_stencil_kernel.transpose(0, 2, 1), 1, CP).reshape(9 * CP, HID)

    member = lax.axis_index(member_axes).astype(jnp.int32)[None]
    own_lanes = 128 * (OWN[1] - OWN[0])
    hidden_lanes = 128 * (HIDDEN[1] - HIDDEN[0])
    forecast, truth, pre, hidden, window, latent = call(
        forward_kernel,
        26,
        [
            ((MEMBERS * CHUNK, 128), f32),
            ((CHUNK, 128), f32),
            ((HID, hidden_lanes), (f32,)),
            ((HID, own_lanes), (bf16,)),
            ((9 * CI, own_lanes), (bf16,)),
            ((CP, own_lanes), (f32,)),
        ],
        [
            ((CP, FLAT), f32),
            ((CI, FLAT), f32),
            ((9 * CI, FLAT), bf16),
            ((HID, FLAT), bf16),
            ((9 * CP, FLAT), f32),
            ((MEMBERS * CHUNK, 128), f32),
            ((HID, hidden_lanes), f32),
            ((HID, own_lanes), bf16),
        ],
        member, own, top, bottom, left, right, gain, valid, mine, w1_stack, w2_stack,
        smem=1, close=(1, 2, 3, 4, 5), copies=6,
    )
    spread = swap(forecast.reshape(MEMBERS, CHUNK, 128), member_axes)
    (grads,) = call(
        score_kernel,
        6,
        [((MEMBERS, CHUNK, 128), bf16)],
        [((MEMBERS, CHUNK, 128), f32)],
        spread, truth,
    )
    grads = swap(grads, member_axes)
    grad_pre, own_grad, weights = call(
        backward_kernel,
        22,
        [
            ((HID, hidden_lanes), (bf16,)),
            ((CP, own_lanes), (f32,)),
            ((GROUPS, PIECE, 128), bf16),
        ],
        [
            ((HID, hidden_lanes), f32),
            ((HID, own_lanes), bf16),
            ((9 * CI, own_lanes), bf16),
            ((MEMBERS * CHUNK, 128), f32),
            ((CI, FLAT), f32),
            ((9 * CI, hidden_lanes), bf16),
            ((HID, hidden_lanes), bf16),
            ((GROUPS * PIECE, 128), f32),
        ],
        grads, pre, hidden, window, valid, mine, w2_turned,
        far=(1, 2, 3), copies=5,
    )
    parts = swap(weights, plane)
    (states,) = call(
        states_kernel,
        14,
        [((C * ROWS, COLS), bf16)],
        [
            ((HID, hidden_lanes), bf16),
            ((CP, own_lanes), f32),
            ((CP, own_lanes), f32),
            ((9 * CP, hidden_lanes), f32),
            ((CP, own_lanes), f32),
            ((C * ROWS, COLS), f32),
        ],
        grad_pre, own_grad, latent, gain, w1_turned,
        far=(0, 1, 2), copies=3,
    )
    piece = (PIECE, 128)
    (copies,) = call(total_kernel, 6, [((RING,) + piece, bf16)], [], parts)
    (copies,) = call(total_kernel, 6, [((GROUPS,) + piece, bf16)], [], swap(copies, "ring"))
    grad_in, grad_out = call(
        weights_kernel,
        8,
        [((9, C, HID), f32), ((9, C, HID), f32)],
        [((GROUPS * PIECE, 128), f32)],
        swap(copies, plane),
    )
    grad_in = grad_in.transpose(0, 2, 1)
    return (states.reshape(embeddings.shape), grad_in, grad_out)


def solution(mesh):
    places = mesh.devices.reshape(MEMBERS // RING, RING, *mesh.devices.shape[1:])
    fine = jax.sharding.Mesh(places, ("half", "ring", "lat", "lon"))
    whole = P(("half", "ring"), None, "lat", "lon")
    return jax.shard_map(
        on_device,
        mesh=fine,
        in_specs=(whole, whole, P(None, "lat", "lon"), P(), P(), P()),
        out_specs=(whole, P(), P()),
        check_vma=False,
    )
```

```python
import functools
import math

import jax
import jax.numpy as jnp
from jax import lax
from jax.experimental import pallas as pl
from jax.experimental.pallas import tpu as pltpu
from jax.sharding import PartitionSpec as P

soft_eps = 0.01
norm_eps = 1e-05
C = 83
CP = 88
CI = 96
HID = 192
ROWS = 8
COLS = 128
NEAR = 1
FAR = 2
RIM = NEAR + FAR
PITCH = COLS + 2 * RIM
TALL = ROWS + 2 * RIM
TILES = -(-TALL * PITCH // 128)
FLAT = 128 * TILES
SPREAD = (2, 13)
OWN = (3, 12)
OWN_LANES = 128 * (OWN[1] - OWN[0])
MEMBERS = 16
GROUPS = 32
RING = 8
CHUNK = 64
PIECE = 72
f32 = jnp.float32
bf16 = jnp.bfloat16
GELU_A = math.sqrt(2.0 / math.pi)
GELU_B = 0.044715


def call(kernel, limit, outs, scratch, *operands, smem=0, far=(), close=(), home=(), copies=0):
    near = pl.BlockSpec(memory_space=pltpu.VMEM)
    away = pl.BlockSpec(memory_space=pltpu.HBM)
    specs = [pl.BlockSpec(memory_space=pltpu.SMEM)] * smem
    specs += [away if i in far else near for i in range(smem, len(operands))]
    kinds = [kind[0] if isinstance(kind, tuple) else kind for _, kind in outs]
    placed = {i: pltpu.VMEM for i in close} | {i: pltpu.HBM for i in (*far, *home)}
    operands = [
        pltpu.with_memory_space_constraint(operand, placed[i]) if i in placed else operand
        for i, operand in enumerate(operands)
    ]
    kept = [pltpu.VMEM(shape, kind) for shape, kind in scratch]
    return pl.pallas_call(
        kernel,
        out_shape=[
            (pltpu.HBM if isinstance(given, tuple) else jax.ShapeDtypeStruct)(shape, kind)
            for (shape, given), kind in zip(outs, kinds)
        ],
        in_specs=specs,
        out_specs=[away if isinstance(kind, tuple) else near for _, kind in outs],
        scratch_shapes=kept + ([pltpu.SemaphoreType.DMA((copies,))] if copies else []),
        compiler_params=pltpu.CompilerParams(vmem_limit_bytes=limit << 20),
    )(*operands)


def started(*pairs, semaphores):
    moves = [
        pltpu.make_async_copy(source, target, semaphores.at[i]) for i, (source, target) in enumerate(pairs)
    ]
    for move in moves:
        move.start()
    return moves


def gain_column(gain_ref):
    row = lax.broadcasted_iota(jnp.int32, (CP, C), 0)
    lane = lax.broadcasted_iota(jnp.int32, (CP, C), 1)
    spread = jnp.where(row == lane, jnp.broadcast_to(gain_ref[...], (CP, C)), 0.0)
    return jnp.sum(spread, axis=1, keepdims=True)


def centred(values):
    real = lax.broadcasted_iota(jnp.int32, (CP, 128), 0) < C
    average = jnp.sum(values, axis=0, keepdims=True) * (1.0 / C)
    centered = jnp.where(real, values - average, 0.0)
    variance = jnp.sum(centered * centered, axis=0, keepdims=True) * (1.0 / C)
    return centered, lax.rsqrt(variance + norm_eps)


def step_of(offset):
    return (offset // 3 - 1) * PITCH + offset % 3 - 1


def tile(index):
    return pl.ds(128 * index, 128)


def lanes_of(height):
    return lax.broadcasted_iota(jnp.int32, (height, 128), 1)


def rows_kernel(
    emb_ref, pert_ref, target_ref, gain_ref, own_ref, up_ref, down_ref, emb, pert, target, first, second, truth, semaphores,
):
    moves = started((emb_ref, emb), (pert_ref, pert), (target_ref, target), semaphores=semaphores)
    for move, source, wide in zip(moves, (emb, pert, target), (first, second, truth)):
        move.wait()
        wide[...] = source[...].astype(f32).reshape(C * ROWS, COLS)
    rest = jnp.zeros((CP - C, 128), f32)
    gain = gain_column(gain_ref)

    def row_of(source, r):
        return jnp.concatenate([source[pl.ds(r, C, stride=ROWS), :], rest], axis=0)

    for r in range(ROWS):
        parts = row_of(first, r), row_of(second, r)
        goal = row_of(truth, r)
        latent = parts[0] + parts[1]
        own_ref[r] = latent
        own_ref[ROWS + r] = goal
        if RIM <= r < ROWS - RIM:
            continue
        sent, first_row = (up_ref, 0) if r < RIM else (down_ref, ROWS - RIM)
        if r < NEAR or r >= ROWS - NEAR:
            index = r - first_row if r < RIM else r - (ROWS - NEAR)
            sent[index] = parts[0].astype(bf16)
            sent[NEAR + index] = parts[1].astype(bf16)
            sent[2 * NEAR + FAR + index] = goal.astype(bf16)
        else:
            centered, scale = centred(latent)
            index = r - NEAR if r < RIM else r - first_row
            sent[2 * NEAR + index] = (centered * scale * gain).astype(bf16)


def latent_row(own_ref, top_ref, bottom_ref, row):
    def near(rim_ref, r):
        return rim_ref[r].astype(f32) + rim_ref[NEAR + r].astype(f32)

    if row < FAR:
        return top_ref[2 * NEAR + row].astype(f32)
    if row < RIM:
        return near(top_ref, row - FAR)
    if row < RIM + ROWS:
        return own_ref[row - RIM]
    if row < RIM + ROWS + NEAR:
        return near(bottom_ref, row - RIM - ROWS)
    return bottom_ref[2 * NEAR + row - RIM - ROWS - NEAR].astype(f32)


def truth_row(own_ref, top_ref, bottom_ref, row):
    base = 2 * NEAR + FAR
    if row < NEAR:
        return top_ref[base + row].astype(f32)
    if row < NEAR + ROWS:
        return own_ref[ROWS + row - NEAR]
    return bottom_ref[base + row - NEAR - ROWS].astype(f32)


def columns_kernel(own_ref, top_ref, bottom_ref, left_ref, right_ref):
    lane = lanes_of(CP)
    left = jnp.zeros((CP, 128), f32)
    right = jnp.zeros((CP, 128), f32)
    plan = [(latent_row, row, RIM * row, RIM) for row in range(TALL)]
    plan += [
        (truth_row, row, RIM * TALL + NEAR * row, NEAR) for row in range(ROWS + 2 * NEAR)
    ]
    for source, row, start, width in plan:
        values = source(own_ref, top_ref, bottom_ref, row)
        here = (lane >= start) & (lane < start + width)
        left = jnp.where(here, pltpu.roll(values, start % 128, 1), left)
        right = jnp.where(here, pltpu.roll(values, (start + width) % 128, 1), right)
    left_ref[...] = left
    right_ref[...] = right


def flat_tiles(pieces, first, last, height=CP, base=None):
    lane = lanes_of(height)
    rolled = {}
    for index in range(first, last):
        result = jnp.zeros((height, 128), f32) if base is None else base(index)
        for number, (values, lane_from, flat_to, width) in enumerate(pieces):
            low, high = max(flat_to - 128 * index, 0), min(flat_to + width - 128 * index, 128)
            if low >= high:
                continue
            if number not in rolled:
                shift = (flat_to - lane_from) % 128
                rolled[number] = pltpu.roll(values(), shift, 1) if shift else values()
            result = jnp.where((lane >= low) & (lane < high), rolled[number], result)
        yield index, result


def forward_kernel(
    member_ref, own_ref, top_ref, bottom_ref, left_ref, right_ref, gain_ref, valid_ref, mine_ref, w1_ref, w2_ref,
    forecast_ref, truth_ref, pre_ref, hidden_ref, window_ref, latent_ref,
    latent, normed, window, hidden, partial, truth, pre_kept, hidden_kept, semaphores,
):
    pieces, truths = [], []
    for row in range(TALL):
        pieces.append((functools.partial(latent_row, own_ref, top_ref, bottom_ref, row), 0, PITCH * row + RIM, COLS))
        pieces.append((lambda: left_ref[...], RIM * row, PITCH * row, RIM))
        pieces.append((lambda: right_ref[...], RIM * row, PITCH * row + RIM + COLS, RIM))
    for row in range(ROWS + 2 * NEAR):
        flat, lane = PITCH * (row + FAR) + RIM, RIM * TALL + NEAR * row
        truths.append((functools.partial(truth_row, own_ref, top_ref, bottom_ref, row), 0, flat, COLS))
        truths.append((lambda: left_ref[...], lane, flat - NEAR, NEAR))
        truths.append((lambda: right_ref[...], lane, flat + COLS, NEAR))
    gain = gain_column(gain_ref)
    lane = lanes_of(CP)
    inner_low, inner_high = PITCH * FAR, PITCH * (TALL - FAR)
    normed[CP:CI, :] = jnp.zeros((CI - CP, FLAT), f32)
    for index, values in flat_tiles(pieces, 0, TILES):
        latent[:, tile(index)] = values
        start = 128 * index
        if start < inner_high and start + 128 > inner_low:
            centered, scale = centred(values)
            scaled = centered * scale * gain
            if start < inner_low or start + 128 > inner_high:
                inside = (lane >= inner_low - start) & (lane < inner_high - start)
                scaled = jnp.where(inside, scaled, values)
            values = scaled
        normed[0:CP, tile(index)] = values * valid_ref[:, tile(index)]
    own = pl.ds(128 * OWN[0], 128 * (OWN[1] - OWN[0]))
    moves = started((latent.at[:, own], latent_ref), semaphores=semaphores)
    for index, values in flat_tiles(truths, *SPREAD):
        truth[pl.ds(CP * (index - SPREAD[0]), CP), :] = values
    filled = CP * (SPREAD[1] - SPREAD[0])
    truth[filled:, :] = jnp.zeros((MEMBERS * CHUNK - filled, 128), f32)
    truth_ref[...] = truth[pl.ds(pl.multiple_of(member_ref[0] * CHUNK, 8), CHUNK), :]

    for group in range(CI // 16):
        values = normed[16 * group : 16 * group + 16, :]
        for offset in range(9):
            shift = -step_of(offset) % FLAT
            moved = pltpu.roll(values, shift, 1) if shift else values
            window[CI * offset + 16 * group : CI * offset + 16 * group + 16, :] = moved.astype(bf16)
    moves += started((window.at[:, own], window_ref), semaphores=semaphores.at[1:2])

    for number, first in enumerate(range(0, TILES, 4)):
        last = min(first + 4, TILES)
        span = slice(128 * first, 128 * last)
        pre = jnp.dot(w1_ref[...], window[:, span], preferred_element_type=f32)
        low, high = max(first, OWN[0]), min(last, OWN[1])
        if low < high:
            kept = pl.ds(128 * (low - OWN[0]), 128 * (high - low))
            pre_kept[:, kept] = pre[:, 128 * (low - first) : 128 * (high - first)]
            moves += started((pre_kept.at[:, kept], pre_ref.at[:, kept]), semaphores=semaphores.at[number + 3 : number + 4])
        curve = jnp.tanh(GELU_A * (pre + GELU_B * (pre * pre * pre)))
        hidden[:, span] = (0.5 * pre * (1.0 + curve) * valid_ref[:, span]).astype(bf16)
        partial[:, span] = jnp.dot(w2_ref[...], hidden[:, span], preferred_element_type=f32)
    hidden_kept[...] = (hidden[:, 128 * OWN[0] : 128 * OWN[1]].astype(f32) * mine_ref[...]).astype(bf16)
    moves += started((hidden_kept, hidden_ref), semaphores=semaphores.at[2:3])

    for group in range(CP // 8):
        total = None
        for offset in range(9):
            start = CP * offset + 8 * group
            shift = -step_of(offset) % FLAT
            values = partial[start : start + 8, :]
            moved = pltpu.roll(values, shift, 1) if shift else values
            total = moved if total is None else total + moved
        for index in range(*SPREAD):
            start = CP * (index - SPREAD[0]) + 8 * group
            forecast_ref[start : start + 8, :] = (
                total[:, 128 * index : 128 * index + 128] + latent[8 * group : 8 * group + 8, tile(index)]
            )
    forecast_ref[filled:, :] = jnp.zeros((MEMBERS * CHUNK - filled, 128), f32)
    for move in moves:
        move.wait()


def soft_slope(values):
    return values * lax.rsqrt(values * values + soft_eps)


def score_kernel(forecast_ref, truth_ref, grad_ref, grads):
    def body(step, carry):
        span = pl.ds(pl.multiple_of(8 * step, 8), 8)
        truth = truth_ref[span, :]
        values = [forecast_ref[m, span, :] for m in range(MEMBERS)]
        totals = [jnp.zeros((8, 128), f32)] * MEMBERS
        for first in range(MEMBERS):
            for second in range(first):
                slope = soft_slope(values[first] - values[second])
                totals[first] = totals[first] + slope
                totals[second] = totals[second] - slope
        for m in range(MEMBERS):
            grads[m, span, :] = soft_slope(values[m] - truth) - totals[m] * (1.0 / (MEMBERS - 1))
        return carry

    lax.fori_loop(0, CHUNK // 8, body, 0)
    grad_ref[...] = grads[...].astype(bf16)


def flat_row(values, row, first):
    index, off = divmod(PITCH * (row + RIM) + RIM, 128)
    near = pltpu.roll(values(index - first), 128 - off, 1)
    far = pltpu.roll(values(index + 1 - first), 128 - off, 1)
    return jnp.where(lanes_of(near.shape[0]) < 128 - off, near, far)


def backward_kernel(
    grad_ref, pre_far, hidden_far, window_far, valid_ref, mine_ref, w2_ref,
    grad_pre_ref, own_grad_ref, weights_ref, up_ref, down_ref, left_ref, right_ref,
    pre_ref, hidden_ref, window_ref, chunks, grad, window, grad_pre, packed, semaphores,
):
    moves = started((hidden_far, hidden_ref), (pre_far, pre_ref), (window_far, window_ref), semaphores=semaphores)
    for m in range(MEMBERS):
        chunks[CHUNK * m : CHUNK * m + CHUNK, :] = grad_ref[m].astype(f32)
    edge = 128 * SPREAD[0]
    grad[:, 0:edge] = jnp.zeros((CI, edge), f32)
    grad[:, 128 * SPREAD[1] :] = jnp.zeros((CI, FLAT - 128 * SPREAD[1]), f32)
    grad[CP:CI, :] = jnp.zeros((CI - CP, FLAT), f32)
    for index in range(*SPREAD):
        values = chunks[CP * (index - SPREAD[0]) : CP * (index - SPREAD[0]) + CP, :]
        grad[0:CP, tile(index)] = values * valid_ref[:, tile(index)]
    low, high = 128 * OWN[0], 128 * OWN[1]
    for group in range(CI // 16):
        values = grad[16 * group : 16 * group + 16, :]
        for offset in range(9):
            shift = step_of(offset) % FLAT
            moved = pltpu.roll(values, shift, 1) if shift else values
            window[CI * offset + 16 * group : CI * offset + 16 * group + 16, :] = moved[:, low:high].astype(bf16)
    own = pl.ds(low, high - low)
    later = started((grad.at[0:CP, own], own_grad_ref), semaphores=semaphores.at[3:4])
    moves[0].wait()
    across = (((1,), (1,)), ((), ()))
    grad_out = lax.dot_general(window[...], hidden_ref[...], across, preferred_element_type=f32)
    for k in range(9):
        values = grad_out[CI * k : CI * k + C, :]
        packed[C * (9 + k) : C * (10 + k), :] = values[:, 0:128]
        packed[C * (18 + k) : C * (19 + k), 64:128] = values[:, 128:192]
    moves[1].wait()
    for first in range(0, high - low, 512):
        span = slice(first, min(first + 512, high - low))
        grad_hidden = jnp.dot(w2_ref[...], window[:, span], preferred_element_type=f32)
        pre = pre_ref[:, span]
        square = pre * pre
        curve = jnp.tanh(GELU_A * (pre + GELU_B * (square * pre)))
        slope = 0.5 * (1.0 + curve) + 0.5 * pre * (1.0 - curve * curve) * (GELU_A * (1.0 + 3.0 * GELU_B * square))
        grad_pre[:, span] = (grad_hidden * slope * mine_ref[:, span]).astype(bf16)
    later += started((grad_pre, grad_pre_ref), semaphores=semaphores.at[4:5])
    moves[2].wait()
    grad_in = lax.dot_general(window_ref[...], grad_pre[...], across, preferred_element_type=f32)
    for k in range(9):
        values = grad_in[CI * k : CI * k + C, :]
        packed[C * k : C * (k + 1), :] = values[:, 0:128]
        packed[C * (18 + k) : C * (19 + k), 0:64] = values[:, 128:192]
    packed[27 * C :, :] = jnp.zeros((GROUPS * PIECE - 27 * C, 128), f32)
    for place in range(GROUPS):
        weights_ref[place] = packed[PIECE * place : PIECE * place + PIECE, :].astype(bf16)
    lane = lanes_of(HID)
    left, right = jnp.zeros((HID, 128), f32), jnp.zeros((HID, 128), f32)
    for row in range(ROWS):
        values = flat_row(lambda index: grad_pre[:, tile(index)].astype(f32), row, OWN[0])
        if row == 0:
            up_ref[...] = values.astype(bf16)
        if row == ROWS - 1:
            down_ref[...] = values.astype(bf16)
        left = jnp.where(lane == row + 1, pltpu.roll(values, row + 1, 1), left)
        right = jnp.where(lane == row + 1, pltpu.roll(values, row + 2, 1), right)
    left_ref[...] = left.astype(bf16)
    right_ref[...] = right.astype(bf16)
    for move in later:
        move.wait()


def corners_kernel(top_ref, bottom_ref, left_ref, right_ref, to_left_ref, to_right_ref):
    lane = lanes_of(HID)
    top, bottom = top_ref[...].astype(f32), bottom_ref[...].astype(f32)
    for step, columns_ref, sent_ref in ((0, left_ref, to_left_ref), (1, right_ref, to_right_ref)):
        values = columns_ref[...].astype(f32)
        values = jnp.where(lane == 0, pltpu.roll(top, step, 1) if step else top, values)
        values = jnp.where(lane == ROWS + 1, pltpu.roll(bottom, ROWS + 1 + step, 1), values)
        sent_ref[...] = values.astype(bf16)


def states_kernel(
    grad_pre_far, grad_far, latent_far, gain_ref, w1_ref, top_ref, bottom_ref, left_ref, right_ref,
    states_ref,
    own_pre, grad, latent, grad_pre, partial, shifted, result, semaphores,
):
    moves = started((grad_pre_far, own_pre), (latent_far, latent), (grad_far, grad), semaphores=semaphores)
    span = 128 * (SPREAD[1] - SPREAD[0])
    inner = slice(128 * (OWN[0] - SPREAD[0]), 128 * (OWN[1] - SPREAD[0]))
    moves[0].wait()

    def base(index):
        if OWN[0] <= index < OWN[1]:
            return own_pre[:, tile(index - OWN[0])].astype(f32)
        return jnp.zeros((HID, 128), f32)

    pieces = [
        (lambda: top_ref[...].astype(f32), 0, PITCH * (RIM - 1) + RIM, COLS),
        (lambda: bottom_ref[...].astype(f32), 0, PITCH * (RIM + ROWS) + RIM, COLS),
    ]
    for row in range(ROWS + 2):
        flat = PITCH * (row + RIM - 1) + RIM
        pieces.append((lambda: left_ref[...].astype(f32), row, flat - 1, 1))
        pieces.append((lambda: right_ref[...].astype(f32), row, flat + COLS, 1))
    for index, values in flat_tiles(pieces, *SPREAD, HID, base):
        grad_pre[:, tile(index - SPREAD[0])] = values.astype(bf16)
    for first in range(0, span, 512):
        some = slice(first, min(first + 512, span))
        partial[:, some] = jnp.dot(w1_ref[...], grad_pre[:, some], preferred_element_type=f32)
    for group in range(CP // 8):
        total = None
        for offset in range(9):
            start = CP * offset + 8 * group
            shift = step_of(offset) % span
            values = partial[start : start + 8, :]
            moved = pltpu.roll(values, shift, 1) if shift else values
            total = moved if total is None else total + moved
        shifted[8 * group : 8 * group + 8, :] = total[:, inner]
    gain = gain_column(gain_ref)
    for move in moves[1:]:
        move.wait()
    for index in range(OWN[1] - OWN[0]):
        centered, scale = centred(latent[:, tile(index)])
        unit = centered * scale
        pull = shifted[:, tile(index)] * gain
        mean_pull = jnp.sum(pull, axis=0, keepdims=True) * (1.0 / C)
        mean_both = jnp.sum(pull * unit, axis=0, keepdims=True) * (1.0 / C)
        shifted[:, tile(index)] = grad[:, tile(index)] + scale * (pull - mean_pull - unit * mean_both)
    for row in range(ROWS):
        values = flat_row(lambda index: shifted[:, tile(index)], row, OWN[0])
        result[pl.ds(row, C, stride=ROWS), :] = values[0:C]
    states_ref[...] = result[...].astype(bf16)


def total_kernel(parts_ref, copies_ref):
    total = parts_ref[0].astype(f32)
    for index in range(1, parts_ref.shape[0]):
        total = total + parts_ref[index].astype(f32)
    total = total.astype(bf16)
    for index in range(copies_ref.shape[0]):
        copies_ref[index] = total


def weights_kernel(parts_ref, grad_in_ref, grad_out_ref, packed):
    scale = 1.0 / math.sqrt(MEMBERS * 32 * 512)
    for place in range(GROUPS):
        packed[PIECE * place : PIECE * place + PIECE, :] = parts_ref[place].astype(f32) * scale
    for k in range(9):
        first = packed[C * k : C * (k + 1), :]
        second = packed[C * (9 + k) : C * (10 + k), :]
        shared = packed[C * (18 + k) : C * (19 + k), :]
        grad_out_ref[k, :, 0:128] = second
        grad_out_ref[k, :, 128:192] = shared[:, 64:128]
        grad_in_ref[k, :, 0:128] = first
        grad_in_ref[k, :, 128:192] = shared[:, 0:64]


def neighbours(axis, periodic):
    count = lax.axis_size(axis)
    forward = [(i, i + 1) for i in range(count - 1)]
    if periodic:
        forward.append((count - 1, 0))
    return forward, [(target, source) for source, target in forward]


def swap(values, axes):
    return lax.all_to_all(values, axes, split_axis=0, concat_axis=0, tiled=True)


def on_device(
    embeddings,
    entry_perturbation,
    target,
    feature_scale_factor,
    first_stencil_kernel,
    second_stencil_kernel,
):
    def padded(weight, dim, size):
        pads = [(0, 0)] * 3
        pads[dim] = (0, size - weight.shape[dim])
        return jnp.pad(weight, pads)

    member_axes, plane = ("half", "ring"), ("half", "lat", "lon")
    gain = feature_scale_factor[None]
    block = (C, ROWS, COLS)
    rim = ((3 * NEAR + FAR, CP, 128), bf16)
    own, up, down = call(
        rows_kernel,
        6,
        [((2 * ROWS, CP, 128), f32), rim, rim],
        [(block, bf16)] * 3 + [((C * ROWS, COLS), f32)] * 3,
        embeddings.reshape(block), entry_perturbation.reshape(block), target, gain,
        far=(0, 1, 2), home=(3,), copies=3,
    )
    forward, backward = neighbours("lat", False)
    top = lax.ppermute(down, "lat", forward)
    bottom = lax.ppermute(up, "lat", backward)
    to_left, to_right = call(
        columns_kernel, 6, [((CP, 128), f32)] * 2, [], own, top, bottom, close=(0, 1, 2)
    )
    forward, backward = neighbours("lon", True)
    left = lax.ppermute(to_right, "lon", forward)
    right = lax.ppermute(to_left, "lon", backward)

    place = jnp.arange(FLAT, dtype=jnp.int32)
    row, column = place // PITCH - RIM, place % PITCH - RIM
    line = row + ROWS * lax.axis_index("lat")
    valid = ((line >= 0) & (line < ROWS * lax.axis_size("lat"))).astype(f32)[None]
    mine = ((row >= 0) & (row < ROWS) & (column >= 0) & (column < COLS)).astype(f32)[None]
    mine = mine[:, 128 * OWN[0] : 128 * OWN[1]]
    w1_stack = padded(first_stencil_kernel, 2, CI).transpose(1, 0, 2).reshape(HID, 9 * CI)
    w2_stack = padded(second_stencil_kernel, 1, CP).reshape(9 * CP, HID)
    w2_turned = padded(second_stencil_kernel, 1, CI).transpose(2, 0, 1).reshape(HID, 9 * CI)
    w1_turned = padded(first_stencil_kernel.transpose(0, 2, 1), 1, CP).reshape(9 * CP, HID)

    member = lax.axis_index(member_axes).astype(jnp.int32)[None]
    own_lanes = OWN_LANES
    spread_lanes = 128 * (SPREAD[1] - SPREAD[0])
    forecast, truth, pre, hidden, window, latent = call(
        forward_kernel,
        26,
        [
            ((MEMBERS * CHUNK, 128), f32),
            ((CHUNK, 128), f32),
            ((HID, own_lanes), (f32,)),
            ((HID, own_lanes), (bf16,)),
            ((9 * CI, own_lanes), (bf16,)),
            ((CP, own_lanes), (f32,)),
        ],
        [
            ((CP, FLAT), f32),
            ((CI, FLAT), f32),
            ((9 * CI, FLAT), bf16),
            ((HID, FLAT), bf16),
            ((9 * CP, FLAT), f32),
            ((MEMBERS * CHUNK, 128), f32),
            ((HID, own_lanes), f32),
            ((HID, own_lanes), bf16),
        ],
        member, own, top, bottom, left, right, gain, valid, mine, w1_stack, w2_stack,
        smem=1, close=(1, 2, 3, 4, 5), copies=7,
    )
    spread = swap(forecast.reshape(MEMBERS, CHUNK, 128), member_axes)
    (grads,) = call(
        score_kernel,
        6,
        [((MEMBERS, CHUNK, 128), bf16)],
        [((MEMBERS, CHUNK, 128), f32)],
        spread, truth,
    )
    grads = swap(grads, member_axes)
    strip = ((HID, 128), bf16)
    grad_pre, own_grad, weights, up, down, to_left, to_right = call(
        backward_kernel,
        22,
        [
            ((HID, own_lanes), (bf16,)),
            ((CP, own_lanes), (f32,)),
            ((GROUPS, PIECE, 128), bf16),
            strip, strip, strip, strip,
        ],
        [
            ((HID, own_lanes), f32),
            ((HID, own_lanes), bf16),
            ((9 * CI, own_lanes), bf16),
            ((MEMBERS * CHUNK, 128), f32),
            ((CI, FLAT), f32),
            ((9 * CI, own_lanes), bf16),
            ((HID, own_lanes), bf16),
            ((GROUPS * PIECE, 128), f32),
        ],
        grads, pre, hidden, window, valid, mine, w2_turned,
        far=(1, 2, 3), copies=5,
    )
    parts = swap(weights, plane)
    forward, backward = neighbours("lat", False)
    top = lax.ppermute(down, "lat", forward)
    bottom = lax.ppermute(up, "lat", backward)
    to_left, to_right = call(
        corners_kernel, 4, [strip, strip], [], top, bottom, to_left, to_right
    )
    forward, backward = neighbours("lon", True)
    left = lax.ppermute(to_right, "lon", forward)
    right = lax.ppermute(to_left, "lon", backward)
    (states,) = call(
        states_kernel,
        16,
        [((C * ROWS, COLS), bf16)],
        [
            ((HID, own_lanes), bf16),
            ((CP, own_lanes), f32),
            ((CP, own_lanes), f32),
            ((HID, spread_lanes), bf16),
            ((9 * CP, spread_lanes), f32),
            ((CP, own_lanes), f32),
            ((C * ROWS, COLS), f32),
        ],
        grad_pre, own_grad, latent, gain, w1_turned, top, bottom, left, right,
        far=(0, 1, 2), copies=3,
    )
    piece = (PIECE, 128)
    (copies,) = call(total_kernel, 6, [((RING,) + piece, bf16)], [], parts)
    (copies,) = call(total_kernel, 6, [((GROUPS,) + piece, bf16)], [], swap(copies, "ring"))
    grad_in, grad_out = call(
        weights_kernel,
        8,
        [((9, C, HID), f32), ((9, C, HID), f32)],
        [((GROUPS * PIECE, 128), f32)],
        swap(copies, plane),
    )
    grad_in = grad_in.transpose(0, 2, 1)
    return (states.reshape(embeddings.shape), grad_in, grad_out)


def solution(mesh):
    places = mesh.devices.reshape(MEMBERS // RING, RING, *mesh.devices.shape[1:])
    fine = jax.sharding.Mesh(places, ("half", "ring", "lat", "lon"))
    whole = P(("half", "ring"), None, "lat", "lon")
    return jax.shard_map(
        on_device,
        mesh=fine,
        in_specs=(whole, whole, P(None, "lat", "lon"), P(), P(), P()),
        out_specs=(whole, P(), P()),
        check_vma=False,
    )
```

```python
import functools
import math

import jax
import jax.numpy as jnp
from jax import lax
from jax.experimental import pallas as pl
from jax.experimental.pallas import tpu as pltpu
from jax.sharding import PartitionSpec as P

soft_eps = 0.01
norm_eps = 1e-05
C = 83
CP = 88
CI = 96
HID = 192
ROWS = 8
COLS = 128
NEAR = 1
FAR = 2
RIM = NEAR + FAR
PITCH = COLS + 2 * RIM
TALL = ROWS + 2 * RIM
TILES = -(-TALL * PITCH // 128)
FLAT = 128 * TILES
SPREAD = (2, 13)
OWN = (3, 12)
OWN_LANES = 128 * (OWN[1] - OWN[0])
MEMBERS = 16
GROUPS = 32
RING = 8
CHUNK = 64
PIECE = 72
f32 = jnp.float32
bf16 = jnp.bfloat16
GELU_A = math.sqrt(2.0 / math.pi)
GELU_B = 0.044715


def call(kernel, limit, outs, scratch, *operands, smem=0, far=(), close=(), home=(), copies=0):
    near = pl.BlockSpec(memory_space=pltpu.VMEM)
    away = pl.BlockSpec(memory_space=pltpu.HBM)
    specs = [pl.BlockSpec(memory_space=pltpu.SMEM)] * smem
    specs += [away if i in far else near for i in range(smem, len(operands))]
    kinds = [kind[0] if isinstance(kind, tuple) else kind for _, kind in outs]
    placed = {i: pltpu.VMEM for i in close} | {i: pltpu.HBM for i in (*far, *home)}
    operands = [
        pltpu.with_memory_space_constraint(operand, placed[i]) if i in placed else operand
        for i, operand in enumerate(operands)
    ]
    kept = [pltpu.VMEM(shape, kind) for shape, kind in scratch]
    return pl.pallas_call(
        kernel,
        out_shape=[
            (pltpu.HBM if isinstance(given, tuple) else jax.ShapeDtypeStruct)(shape, kind)
            for (shape, given), kind in zip(outs, kinds)
        ],
        in_specs=specs,
        out_specs=[away if isinstance(kind, tuple) else near for _, kind in outs],
        scratch_shapes=kept + ([pltpu.SemaphoreType.DMA((copies,))] if copies else []),
        compiler_params=pltpu.CompilerParams(vmem_limit_bytes=limit << 20),
    )(*operands)


def started(*pairs, semaphores):
    moves = [
        pltpu.make_async_copy(source, target, semaphores.at[i]) for i, (source, target) in enumerate(pairs)
    ]
    for move in moves:
        move.start()
    return moves


def gain_column(gain_ref):
    row = lax.broadcasted_iota(jnp.int32, (CP, C), 0)
    lane = lax.broadcasted_iota(jnp.int32, (CP, C), 1)
    spread = jnp.where(row == lane, jnp.broadcast_to(gain_ref[...], (CP, C)), 0.0)
    return jnp.sum(spread, axis=1, keepdims=True)


def centred(values):
    real = lax.broadcasted_iota(jnp.int32, (CP, 128), 0) < C
    average = jnp.sum(values, axis=0, keepdims=True) * (1.0 / C)
    centered = jnp.where(real, values - average, 0.0)
    variance = jnp.sum(centered * centered, axis=0, keepdims=True) * (1.0 / C)
    return centered, lax.rsqrt(variance + norm_eps)


def step_of(offset):
    return (offset // 3 - 1) * PITCH + offset % 3 - 1


def tile(index):
    return pl.ds(128 * index, 128)


def lanes_of(height):
    return lax.broadcasted_iota(jnp.int32, (height, 128), 1)


def rows_kernel(
    emb_ref, pert_ref, target_ref, gain_ref, own_ref, up_ref, down_ref, emb, pert, target, first, second, truth, semaphores,
):
    moves = started((emb_ref, emb), (pert_ref, pert), (target_ref, target), semaphores=semaphores)
    for move, source, wide in zip(moves, (emb, pert, target), (first, second, truth)):
        move.wait()
        wide[...] = source[...].astype(f32).reshape(C * ROWS, COLS)
    rest = jnp.zeros((CP - C, 128), f32)
    gain = gain_column(gain_ref)

    def row_of(source, r):
        return jnp.concatenate([source[pl.ds(r, C, stride=ROWS), :], rest], axis=0)

    for r in range(ROWS):
        parts = row_of(first, r), row_of(second, r)
        goal = row_of(truth, r)
        latent = parts[0] + parts[1]
        own_ref[r] = latent
        own_ref[ROWS + r] = goal
        if RIM <= r < ROWS - RIM:
            continue
        sent, first_row = (up_ref, 0) if r < RIM else (down_ref, ROWS - RIM)
        if r < NEAR or r >= ROWS - NEAR:
            index = r - first_row if r < RIM else r - (ROWS - NEAR)
            sent[index] = parts[0].astype(bf16)
            sent[NEAR + index] = parts[1].astype(bf16)
            sent[2 * NEAR + FAR + index] = goal.astype(bf16)
        else:
            centered, scale = centred(latent)
            index = r - NEAR if r < RIM else r - first_row
            sent[2 * NEAR + index] = (centered * scale * gain).astype(bf16)


def latent_row(own_ref, top_ref, bottom_ref, row):
    def near(rim_ref, r):
        return rim_ref[r].astype(f32) + rim_ref[NEAR + r].astype(f32)

    if row < FAR:
        return top_ref[2 * NEAR + row].astype(f32)
    if row < RIM:
        return near(top_ref, row - FAR)
    if row < RIM + ROWS:
        return own_ref[row - RIM]
    if row < RIM + ROWS + NEAR:
        return near(bottom_ref, row - RIM - ROWS)
    return bottom_ref[2 * NEAR + row - RIM - ROWS - NEAR].astype(f32)


def truth_row(own_ref, top_ref, bottom_ref, row):
    base = 2 * NEAR + FAR
    if row < NEAR:
        return top_ref[base + row].astype(f32)
    if row < NEAR + ROWS:
        return own_ref[ROWS + row - NEAR]
    return bottom_ref[base + row - NEAR - ROWS].astype(f32)


def columns_kernel(own_ref, top_ref, bottom_ref, left_ref, right_ref):
    lane = lanes_of(CP)
    left = jnp.zeros((CP, 128), f32)
    right = jnp.zeros((CP, 128), f32)
    plan = [(latent_row, row, RIM * row, RIM) for row in range(TALL)]
    plan += [
        (truth_row, row, RIM * TALL + NEAR * row, NEAR) for row in range(ROWS + 2 * NEAR)
    ]
    for source, row, start, width in plan:
        values = source(own_ref, top_ref, bottom_ref, row)
        here = (lane >= start) & (lane < start + width)
        left = jnp.where(here, pltpu.roll(values, start % 128, 1), left)
        right = jnp.where(here, pltpu.roll(values, (start + width) % 128, 1), right)
    left_ref[...] = left
    right_ref[...] = right


def flat_tiles(pieces, first, last, height=CP, base=None):
    lane = lanes_of(height)
    rolled = {}
    for index in range(first, last):
        result = jnp.zeros((height, 128), f32) if base is None else base(index)
        for number, (values, lane_from, flat_to, width) in enumerate(pieces):
            low, high = max(flat_to - 128 * index, 0), min(flat_to + width - 128 * index, 128)
            if low >= high:
                continue
            if number not in rolled:
                shift = (flat_to - lane_from) % 128
                rolled[number] = pltpu.roll(values(), shift, 1) if shift else values()
            result = jnp.where((lane >= low) & (lane < high), rolled[number], result)
        yield index, result


def forward_kernel(
    member_ref, own_ref, top_ref, bottom_ref, left_ref, right_ref, gain_ref, valid_ref, mine_ref, w1_ref, w2_ref,
    forecast_ref, truth_ref, pre_ref, hidden_ref, window_ref, latent_ref,
    latent, normed, window, hidden, partial, truth, pre_kept, hidden_kept, semaphores,
):
    pieces, truths = [], []
    for row in range(TALL):
        pieces.append((functools.partial(latent_row, own_ref, top_ref, bottom_ref, row), 0, PITCH * row + RIM, COLS))
        pieces.append((lambda: left_ref[...], RIM * row, PITCH * row, RIM))
        pieces.append((lambda: right_ref[...], RIM * row, PITCH * row + RIM + COLS, RIM))
    for row in range(ROWS + 2 * NEAR):
        flat, lane = PITCH * (row + FAR) + RIM, RIM * TALL + NEAR * row
        truths.append((functools.partial(truth_row, own_ref, top_ref, bottom_ref, row), 0, flat, COLS))
        truths.append((lambda: left_ref[...], lane, flat - NEAR, NEAR))
        truths.append((lambda: right_ref[...], lane, flat + COLS, NEAR))
    gain = gain_column(gain_ref)
    lane = lanes_of(CP)
    inner_low, inner_high = PITCH * FAR, PITCH * (TALL - FAR)
    normed[CP:CI, :] = jnp.zeros((CI - CP, FLAT), f32)
    for index, values in flat_tiles(pieces, 0, TILES):
        latent[:, tile(index)] = values
        start = 128 * index
        if start < inner_high and start + 128 > inner_low:
            centered, scale = centred(values)
            scaled = centered * scale * gain
            if start < inner_low or start + 128 > inner_high:
                inside = (lane >= inner_low - start) & (lane < inner_high - start)
                scaled = jnp.where(inside, scaled, values)
            values = scaled
        normed[0:CP, tile(index)] = values * valid_ref[:, tile(index)]
    own = pl.ds(128 * OWN[0], 128 * (OWN[1] - OWN[0]))
    moves = started((latent.at[:, own], latent_ref), semaphores=semaphores)
    for index, values in flat_tiles(truths, *SPREAD):
        truth[pl.ds(CP * (index - SPREAD[0]), CP), :] = values
    filled = CP * (SPREAD[1] - SPREAD[0])
    truth[filled:, :] = jnp.zeros((MEMBERS * CHUNK - filled, 128), f32)
    truth_ref[...] = truth[pl.ds(pl.multiple_of(member_ref[0] * CHUNK, 8), CHUNK), :]

    for group in range(CI // 16):
        values = normed[16 * group : 16 * group + 16, :]
        for offset in range(9):
            shift = -step_of(offset) % FLAT
            moved = pltpu.roll(values, shift, 1) if shift else values
            window[CI * offset + 16 * group : CI * offset + 16 * group + 16, :] = moved.astype(bf16)
    moves += started((window.at[:, own], window_ref), semaphores=semaphores.at[1:2])

    for number, first in enumerate(range(0, TILES, 4)):
        last = min(first + 4, TILES)
        span = slice(128 * first, 128 * last)
        pre = jnp.dot(w1_ref[...], window[:, span], preferred_element_type=f32)
        low, high = max(first, OWN[0]), min(last, OWN[1])
        if low < high:
            kept = pl.ds(128 * (low - OWN[0]), 128 * (high - low))
            pre_kept[:, kept] = pre[:, 128 * (low - first) : 128 * (high - first)]
            moves += started((pre_kept.at[:, kept], pre_ref.at[:, kept]), semaphores=semaphores.at[number + 3 : number + 4])
        curve = jnp.tanh(GELU_A * (pre + GELU_B * (pre * pre * pre)))
        hidden[:, span] = (0.5 * pre * (1.0 + curve) * valid_ref[:, span]).astype(bf16)
        partial[:, span] = jnp.dot(w2_ref[...], hidden[:, span], preferred_element_type=f32)
    hidden_kept[...] = (hidden[:, 128 * OWN[0] : 128 * OWN[1]].astype(f32) * mine_ref[...]).astype(bf16)
    moves += started((hidden_kept, hidden_ref), semaphores=semaphores.at[2:3])

    for group in range(CP // 8):
        total = None
        for offset in range(9):
            start = CP * offset + 8 * group
            shift = -step_of(offset) % FLAT
            values = partial[start : start + 8, :]
            moved = pltpu.roll(values, shift, 1) if shift else values
            total = moved if total is None else total + moved
        for index in range(*SPREAD):
            start = CP * (index - SPREAD[0]) + 8 * group
            forecast_ref[start : start + 8, :] = (
                total[:, 128 * index : 128 * index + 128] + latent[8 * group : 8 * group + 8, tile(index)]
            )
    forecast_ref[filled:, :] = jnp.zeros((MEMBERS * CHUNK - filled, 128), f32)
    for move in moves:
        move.wait()


def soft_slope(values):
    return values * lax.rsqrt(values * values + soft_eps)


def score_kernel(forecast_ref, truth_ref, grad_ref, grads):
    def body(step, carry):
        span = pl.ds(pl.multiple_of(8 * step, 8), 8)
        truth = truth_ref[span, :]
        values = [forecast_ref[m, span, :] for m in range(MEMBERS)]
        totals = [jnp.zeros((8, 128), f32)] * MEMBERS
        for first in range(MEMBERS):
            for second in range(first):
                slope = soft_slope(values[first] - values[second])
                totals[first] = totals[first] + slope
                totals[second] = totals[second] - slope
        for m in range(MEMBERS):
            grads[m, span, :] = soft_slope(values[m] - truth) - totals[m] * (1.0 / (MEMBERS - 1))
        return carry

    lax.fori_loop(0, CHUNK // 8, body, 0)
    grad_ref[...] = grads[...].astype(bf16)


def flat_row(values, row, first):
    index, off = divmod(PITCH * (row + RIM) + RIM, 128)
    near = pltpu.roll(values(index - first), 128 - off, 1)
    far = pltpu.roll(values(index + 1 - first), 128 - off, 1)
    return jnp.where(lanes_of(near.shape[0]) < 128 - off, near, far)


def backward_kernel(
    grad_ref, pre_far, hidden_far, window_far, valid_ref, mine_ref, w2_ref,
    grad_pre_ref, own_grad_ref, weights_ref, up_ref, down_ref, left_ref, right_ref,
    pre_ref, hidden_ref, window_ref, chunks, grad, window, grad_pre, packed, semaphores,
):
    moves = started((hidden_far, hidden_ref), (pre_far, pre_ref), (window_far, window_ref), semaphores=semaphores)
    for m in range(MEMBERS):
        chunks[CHUNK * m : CHUNK * m + CHUNK, :] = grad_ref[m].astype(f32)
    edge = 128 * SPREAD[0]
    grad[:, 0:edge] = jnp.zeros((CI, edge), f32)
    grad[:, 128 * SPREAD[1] :] = jnp.zeros((CI, FLAT - 128 * SPREAD[1]), f32)
    grad[CP:CI, :] = jnp.zeros((CI - CP, FLAT), f32)
    for index in range(*SPREAD):
        values = chunks[CP * (index - SPREAD[0]) : CP * (index - SPREAD[0]) + CP, :]
        grad[0:CP, tile(index)] = values * valid_ref[:, tile(index)]
    low, high = 128 * OWN[0], 128 * OWN[1]
    for group in range(CI // 16):
        values = grad[16 * group : 16 * group + 16, :]
        for offset in range(9):
            shift = step_of(offset) % FLAT
            moved = pltpu.roll(values, shift, 1) if shift else values
            window[CI * offset + 16 * group : CI * offset + 16 * group + 16, :] = moved[:, low:high].astype(bf16)
    own = pl.ds(low, high - low)
    later = started((grad.at[0:CP, own], own_grad_ref), semaphores=semaphores.at[3:4])
    moves[0].wait()
    across = (((1,), (1,)), ((), ()))
    grad_out = lax.dot_general(window[...], hidden_ref[...], across, preferred_element_type=f32)
    for k in range(9):
        values = grad_out[CI * k : CI * k + C, :]
        packed[C * (9 + k) : C * (10 + k), :] = values[:, 0:128]
        packed[C * (18 + k) : C * (19 + k), 64:128] = values[:, 128:192]
    moves[1].wait()
    for first in range(0, high - low, 512):
        span = slice(first, min(first + 512, high - low))
        grad_hidden = jnp.dot(w2_ref[...], window[:, span], preferred_element_type=f32)
        pre = pre_ref[:, span]
        square = pre * pre
        curve = jnp.tanh(GELU_A * (pre + GELU_B * (square * pre)))
        slope = 0.5 * (1.0 + curve) + 0.5 * pre * (1.0 - curve * curve) * (GELU_A * (1.0 + 3.0 * GELU_B * square))
        grad_pre[:, span] = (grad_hidden * slope * mine_ref[:, span]).astype(bf16)
    later += started((grad_pre, grad_pre_ref), semaphores=semaphores.at[4:5])
    moves[2].wait()
    grad_in = lax.dot_general(window_ref[...], grad_pre[...], across, preferred_element_type=f32)
    for k in range(9):
        values = grad_in[CI * k : CI * k + C, :]
        packed[C * k : C * (k + 1), :] = values[:, 0:128]
        packed[C * (18 + k) : C * (19 + k), 0:64] = values[:, 128:192]
    packed[27 * C :, :] = jnp.zeros((GROUPS * PIECE - 27 * C, 128), f32)
    for place in range(GROUPS):
        weights_ref[place] = packed[PIECE * place : PIECE * place + PIECE, :].astype(bf16)
    lane = lanes_of(HID)
    left, right = jnp.zeros((HID, 128), f32), jnp.zeros((HID, 128), f32)
    for row in range(ROWS):
        values = flat_row(lambda index: grad_pre[:, tile(index)].astype(f32), row, OWN[0])
        if row == 0:
            up_ref[...] = values.astype(bf16)
        if row == ROWS - 1:
            down_ref[...] = values.astype(bf16)
        left = jnp.where(lane == row + 1, pltpu.roll(values, row + 1, 1), left)
        right = jnp.where(lane == row + 1, pltpu.roll(values, row + 2, 1), right)
    left_ref[...] = left.astype(bf16)
    right_ref[...] = right.astype(bf16)
    for move in later:
        move.wait()


def corners_kernel(top_ref, bottom_ref, left_ref, right_ref, to_left_ref, to_right_ref):
    lane = lanes_of(HID)
    top, bottom = top_ref[...].astype(f32), bottom_ref[...].astype(f32)
    for step, columns_ref, sent_ref in ((0, left_ref, to_left_ref), (1, right_ref, to_right_ref)):
        values = columns_ref[...].astype(f32)
        values = jnp.where(lane == 0, pltpu.roll(top, step, 1) if step else top, values)
        values = jnp.where(lane == ROWS + 1, pltpu.roll(bottom, ROWS + 1 + step, 1), values)
        sent_ref[...] = values.astype(bf16)


def states_kernel(
    grad_pre_far, grad_far, latent_far, gain_ref, w1_ref, top_ref, bottom_ref, left_ref, right_ref,
    states_ref,
    own_pre, grad, latent, grad_pre, partial, shifted, result, semaphores,
):
    moves = started((grad_pre_far, own_pre), (latent_far, latent), (grad_far, grad), semaphores=semaphores)
    span = 128 * (SPREAD[1] - SPREAD[0])
    inner = slice(128 * (OWN[0] - SPREAD[0]), 128 * (OWN[1] - SPREAD[0]))
    moves[0].wait()

    def base(index):
        if OWN[0] <= index < OWN[1]:
            return own_pre[:, tile(index - OWN[0])].astype(f32)
        return jnp.zeros((HID, 128), f32)

    pieces = [
        (lambda: top_ref[...].astype(f32), 0, PITCH * (RIM - 1) + RIM, COLS),
        (lambda: bottom_ref[...].astype(f32), 0, PITCH * (RIM + ROWS) + RIM, COLS),
    ]
    for row in range(ROWS + 2):
        flat = PITCH * (row + RIM - 1) + RIM
        pieces.append((lambda: left_ref[...].astype(f32), row, flat - 1, 1))
        pieces.append((lambda: right_ref[...].astype(f32), row, flat + COLS, 1))
    for index, values in flat_tiles(pieces, *SPREAD, HID, base):
        grad_pre[:, tile(index - SPREAD[0])] = values.astype(bf16)
    for first in range(0, span, 512):
        some = slice(first, min(first + 512, span))
        partial[:, some] = jnp.dot(w1_ref[...], grad_pre[:, some], preferred_element_type=f32)
    for group in range(CP // 8):
        total = None
        for offset in range(9):
            start = CP * offset + 8 * group
            shift = step_of(offset) % span
            values = partial[start : start + 8, :]
            moved = pltpu.roll(values, shift, 1) if shift else values
            total = moved if total is None else total + moved
        shifted[8 * group : 8 * group + 8, :] = total[:, inner]
    gain = gain_column(gain_ref)
    for move in moves[1:]:
        move.wait()
    for index in range(OWN[1] - OWN[0]):
        centered, scale = centred(latent[:, tile(index)])
        unit = centered * scale
        pull = shifted[:, tile(index)] * gain
        mean_pull = jnp.sum(pull, axis=0, keepdims=True) * (1.0 / C)
        mean_both = jnp.sum(pull * unit, axis=0, keepdims=True) * (1.0 / C)
        shifted[:, tile(index)] = grad[:, tile(index)] + scale * (pull - mean_pull - unit * mean_both)
    for row in range(ROWS):
        values = flat_row(lambda index: shifted[:, tile(index)], row, OWN[0])
        result[pl.ds(row, C, stride=ROWS), :] = values[0:C]
    states_ref[...] = result[...].astype(bf16)


def total_kernel(parts_ref, copies_ref):
    total = parts_ref[0].astype(f32)
    for index in range(1, parts_ref.shape[0]):
        total = total + parts_ref[index].astype(f32)
    total = total.astype(bf16)
    for index in range(copies_ref.shape[0]):
        copies_ref[index] = total


def weights_kernel(parts_ref, grad_in_ref, grad_out_ref, packed):
    scale = 1.0 / math.sqrt(MEMBERS * 32 * 512)
    for place in range(GROUPS):
        packed[PIECE * place : PIECE * place + PIECE, :] = parts_ref[place].astype(f32) * scale
    for k in range(9):
        first = packed[C * k : C * (k + 1), :]
        second = packed[C * (9 + k) : C * (10 + k), :]
        shared = packed[C * (18 + k) : C * (19 + k), :]
        grad_out_ref[k, :, 0:128] = second
        grad_out_ref[k, :, 128:192] = shared[:, 64:128]
        grad_in_ref[k, :, 0:128] = first
        grad_in_ref[k, :, 128:192] = shared[:, 0:64]


def neighbours(axis, periodic):
    count = lax.axis_size(axis)
    forward = [(i, i + 1) for i in range(count - 1)]
    if periodic:
        forward.append((count - 1, 0))
    return forward, [(target, source) for source, target in forward]


def swap(values, axes):
    return lax.all_to_all(values, axes, split_axis=0, concat_axis=0, tiled=True)


def on_device(
    embeddings,
    entry_perturbation,
    target,
    feature_scale_factor,
    first_stencil_kernel,
    second_stencil_kernel,
):
    def padded(weight, dim, size):
        pads = [(0, 0)] * 3
        pads[dim] = (0, size - weight.shape[dim])
        return jnp.pad(weight, pads)

    member_axes, plane = ("half", "ring"), ("half", "lat", "lon")
    gain = feature_scale_factor[None]
    block = (C, ROWS, COLS)
    rim = ((3 * NEAR + FAR, CP, 128), bf16)
    own, up, down = call(
        rows_kernel,
        6,
        [((2 * ROWS, CP, 128), f32), rim, rim],
        [(block, bf16)] * 3 + [((C * ROWS, COLS), f32)] * 3,
        embeddings.reshape(block), entry_perturbation.reshape(block), target, gain,
        far=(0, 1, 2), home=(3,), copies=3,
    )
    forward, backward = neighbours("lat", False)
    top = lax.ppermute(down, "lat", forward)
    bottom = lax.ppermute(up, "lat", backward)
    to_left, to_right = call(
        columns_kernel, 6, [((CP, 128), f32)] * 2, [], own, top, bottom, close=(0, 1, 2)
    )
    forward, backward = neighbours("lon", True)
    left = lax.ppermute(to_right, "lon", forward)
    right = lax.ppermute(to_left, "lon", backward)

    place = jnp.arange(FLAT, dtype=jnp.int32)
    row, column = place // PITCH - RIM, place % PITCH - RIM
    line = row + ROWS * lax.axis_index("lat")
    valid = ((line >= 0) & (line < ROWS * lax.axis_size("lat"))).astype(f32)[None]
    mine = ((row >= 0) & (row < ROWS) & (column >= 0) & (column < COLS)).astype(f32)[None]
    mine = mine[:, 128 * OWN[0] : 128 * OWN[1]]
    w1_stack = padded(first_stencil_kernel, 2, CI).transpose(1, 0, 2).reshape(HID, 9 * CI)
    w2_stack = padded(second_stencil_kernel, 1, CP).reshape(9 * CP, HID)
    w2_turned = padded(second_stencil_kernel, 1, CI).transpose(2, 0, 1).reshape(HID, 9 * CI)
    w1_turned = padded(first_stencil_kernel.transpose(0, 2, 1), 1, CP).reshape(9 * CP, HID)

    member = lax.axis_index(member_axes).astype(jnp.int32)[None]
    own_lanes = OWN_LANES
    spread_lanes = 128 * (SPREAD[1] - SPREAD[0])
    forecast, truth, pre, hidden, window, latent = call(
        forward_kernel,
        26,
        [
            ((MEMBERS * CHUNK, 128), f32),
            ((CHUNK, 128), f32),
            ((HID, own_lanes), (f32,)),
            ((HID, own_lanes), (bf16,)),
            ((9 * CI, own_lanes), (bf16,)),
            ((CP, own_lanes), (f32,)),
        ],
        [
            ((CP, FLAT), f32),
            ((CI, FLAT), f32),
            ((9 * CI, FLAT), bf16),
            ((HID, FLAT), bf16),
            ((9 * CP, FLAT), f32),
            ((MEMBERS * CHUNK, 128), f32),
            ((HID, own_lanes), f32),
            ((HID, own_lanes), bf16),
        ],
        member, own, top, bottom, left, right, gain, valid, mine, w1_stack, w2_stack,
        smem=1, close=(1, 2, 3, 4, 5), copies=7,
    )
    spread = swap(forecast.reshape(MEMBERS, CHUNK, 128), member_axes)
    (grads,) = call(
        score_kernel,
        6,
        [((MEMBERS, CHUNK, 128), bf16)],
        [((MEMBERS, CHUNK, 128), f32)],
        spread, truth,
    )
    grads = swap(grads, member_axes)
    strip = ((HID, 128), bf16)
    grad_pre, own_grad, weights, up, down, to_left, to_right = call(
        backward_kernel,
        22,
        [
            ((HID, own_lanes), (bf16,)),
            ((CP, own_lanes), (f32,)),
            ((GROUPS, PIECE, 128), bf16),
            strip, strip, strip, strip,
        ],
        [
            ((HID, own_lanes), f32),
            ((HID, own_lanes), bf16),
            ((9 * CI, own_lanes), bf16),
            ((MEMBERS * CHUNK, 128), f32),
            ((CI, FLAT), f32),
            ((9 * CI, own_lanes), bf16),
            ((HID, own_lanes), bf16),
            ((GROUPS * PIECE, 128), f32),
        ],
        grads, pre, hidden, window, valid, mine, w2_turned,
        far=(1, 2, 3), copies=5,
    )
    parts = swap(weights, plane)
    forward, backward = neighbours("lat", False)
    parts, top, bottom = lax.optimization_barrier(
        (parts, lax.ppermute(down, "lat", forward), lax.ppermute(up, "lat", backward))
    )
    to_left, to_right = call(
        corners_kernel, 4, [strip, strip], [], top, bottom, to_left, to_right
    )
    forward, backward = neighbours("lon", True)
    left = lax.ppermute(to_right, "lon", forward)
    right = lax.ppermute(to_left, "lon", backward)
    piece = (PIECE, 128)
    (copies,) = call(total_kernel, 6, [((RING,) + piece, bf16)], [], parts)
    parts, left, right = lax.optimization_barrier((swap(copies, "ring"), left, right))
    (copies,) = call(total_kernel, 6, [((GROUPS,) + piece, bf16)], [], parts)
    (states,) = call(
        states_kernel,
        16,
        [((C * ROWS, COLS), bf16)],
        [
            ((HID, own_lanes), bf16),
            ((CP, own_lanes), f32),
            ((CP, own_lanes), f32),
            ((HID, spread_lanes), bf16),
            ((9 * CP, spread_lanes), f32),
            ((CP, own_lanes), f32),
            ((C * ROWS, COLS), f32),
        ],
        grad_pre, own_grad, latent, gain, w1_turned, top, bottom, left, right,
        far=(0, 1, 2), copies=3,
    )
    grad_in, grad_out = call(
        weights_kernel,
        8,
        [((9, C, HID), f32), ((9, C, HID), f32)],
        [((GROUPS * PIECE, 128), f32)],
        swap(copies, plane),
    )
    grad_in = grad_in.transpose(0, 2, 1)
    return (states.reshape(embeddings.shape), grad_in, grad_out)


def solution(mesh):
    places = mesh.devices.reshape(MEMBERS // RING, RING, *mesh.devices.shape[1:])
    fine = jax.sharding.Mesh(places, ("half", "ring", "lat", "lon"))
    whole = P(("half", "ring"), None, "lat", "lon")
    return jax.shard_map(
        on_device,
        mesh=fine,
        in_specs=(whole, whole, P(None, "lat", "lon"), P(), P(), P()),
        out_specs=(whole, P(), P()),
        check_vma=False,
    )
```

```python
import functools
import math

import jax
import jax.numpy as jnp
from jax import lax
from jax.experimental import pallas as pl
from jax.experimental.pallas import tpu as pltpu
from jax.sharding import PartitionSpec as P

soft_eps = 0.01
norm_eps = 1e-05
C = 83
CP = 88
CI = 96
HID = 192
ROWS = 8
COLS = 128
NEAR = 1
FAR = 2
RIM = NEAR + FAR
SIDE = 4
BESIDE = 2
PITCH = COLS + 2 * SIDE
TALL = ROWS + 2 * RIM
TILES = -(-TALL * PITCH // 128)
FLAT = 128 * TILES
SPREAD = (2, 13)
OWN = (3, 12)
OWN_LANES = 128 * (OWN[1] - OWN[0])
MEMBERS = 16
GROUPS = 32
RING = 8
CHUNK = 64
PIECE = 72
f32 = jnp.float32
bf16 = jnp.bfloat16
GELU_A = math.sqrt(2.0 / math.pi)
GELU_B = 0.044715


def call(kernel, limit, outs, scratch, *operands, smem=0, far=(), close=(), home=(), copies=0):
    near = pl.BlockSpec(memory_space=pltpu.VMEM)
    away = pl.BlockSpec(memory_space=pltpu.HBM)
    specs = [pl.BlockSpec(memory_space=pltpu.SMEM)] * smem
    specs += [away if i in far else near for i in range(smem, len(operands))]
    kinds = [kind[0] if isinstance(kind, tuple) else kind for _, kind in outs]
    placed = {i: pltpu.VMEM for i in close} | {i: pltpu.HBM for i in (*far, *home)}
    operands = [
        pltpu.with_memory_space_constraint(operand, placed[i]) if i in placed else operand
        for i, operand in enumerate(operands)
    ]
    kept = [pltpu.VMEM(shape, kind) for shape, kind in scratch]
    return pl.pallas_call(
        kernel,
        out_shape=[
            (pltpu.HBM if isinstance(given, tuple) else jax.ShapeDtypeStruct)(shape, kind)
            for (shape, given), kind in zip(outs, kinds)
        ],
        in_specs=specs,
        out_specs=[away if isinstance(kind, tuple) else near for _, kind in outs],
        scratch_shapes=kept + ([pltpu.SemaphoreType.DMA((copies,))] if copies else []),
        compiler_params=pltpu.CompilerParams(vmem_limit_bytes=limit << 20),
    )(*operands)


def started(*pairs, semaphores):
    moves = [
        pltpu.make_async_copy(source, target, semaphores.at[i]) for i, (source, target) in enumerate(pairs)
    ]
    for move in moves:
        move.start()
    return moves


def gain_column(gain_ref):
    row = lax.broadcasted_iota(jnp.int32, (CP, C), 0)
    lane = lax.broadcasted_iota(jnp.int32, (CP, C), 1)
    spread = jnp.where(row == lane, jnp.broadcast_to(gain_ref[...], (CP, C)), 0.0)
    return jnp.sum(spread, axis=1, keepdims=True)


def centred(values):
    real = lax.broadcasted_iota(jnp.int32, (CP, 128), 0) < C
    average = jnp.sum(values, axis=0, keepdims=True) * (1.0 / C)
    centered = jnp.where(real, values - average, 0.0)
    variance = jnp.sum(centered * centered, axis=0, keepdims=True) * (1.0 / C)
    return centered, lax.rsqrt(variance + norm_eps)


def step_of(offset):
    return (offset // 3 - 1) * PITCH + offset % 3 - 1


def tile(index):
    return pl.ds(128 * index, 128)


def lanes_of(height):
    return lax.broadcasted_iota(jnp.int32, (height, 128), 1)


def rows_kernel(
    emb_ref, pert_ref, target_ref, gain_ref, own_ref, up_ref, down_ref, emb, pert, target, first, second, truth, semaphores,
):
    moves = started((emb_ref, emb), (pert_ref, pert), (target_ref, target), semaphores=semaphores)
    for move, source, wide in zip(moves, (emb, pert, target), (first, second, truth)):
        move.wait()
        wide[...] = source[...].astype(f32).reshape(C * ROWS, COLS)
    rest = jnp.zeros((CP - C, 128), f32)
    gain = gain_column(gain_ref)

    def row_of(source, r):
        return jnp.concatenate([source[pl.ds(r, C, stride=ROWS), :], rest], axis=0)

    for r in range(ROWS):
        parts = row_of(first, r), row_of(second, r)
        goal = row_of(truth, r)
        latent = parts[0] + parts[1]
        own_ref[r] = latent
        own_ref[ROWS + r] = goal
        if RIM <= r < ROWS - RIM:
            continue
        sent, first_row = (up_ref, 0) if r < RIM else (down_ref, ROWS - RIM)
        if r < NEAR or r >= ROWS - NEAR:
            index = r - first_row if r < RIM else r - (ROWS - NEAR)
            sent[index] = parts[0].astype(bf16)
            sent[NEAR + index] = parts[1].astype(bf16)
            sent[2 * NEAR + FAR + index] = goal.astype(bf16)
        else:
            centered, scale = centred(latent)
            index = r - NEAR if r < RIM else r - first_row
            sent[2 * NEAR + index] = (centered * scale * gain).astype(bf16)


def latent_row(own_ref, top_ref, bottom_ref, row):
    def near(rim_ref, r):
        return rim_ref[r].astype(f32) + rim_ref[NEAR + r].astype(f32)

    if row < FAR:
        return top_ref[2 * NEAR + row].astype(f32)
    if row < RIM:
        return near(top_ref, row - FAR)
    if row < RIM + ROWS:
        return own_ref[row - RIM]
    if row < RIM + ROWS + NEAR:
        return near(bottom_ref, row - RIM - ROWS)
    return bottom_ref[2 * NEAR + row - RIM - ROWS - NEAR].astype(f32)


def truth_row(own_ref, top_ref, bottom_ref, row):
    base = 2 * NEAR + FAR
    if row < NEAR:
        return top_ref[base + row].astype(f32)
    if row < NEAR + ROWS:
        return own_ref[ROWS + row - NEAR]
    return bottom_ref[base + row - NEAR - ROWS].astype(f32)


def columns_kernel(own_ref, top_ref, bottom_ref, left_ref, right_ref):
    lane = lanes_of(CP)
    left = jnp.zeros((CP, 128), f32)
    right = jnp.zeros((CP, 128), f32)
    plan = [(latent_row, row, SIDE * row, SIDE) for row in range(TALL)]
    plan += [
        (truth_row, row, SIDE * TALL + BESIDE * row, BESIDE) for row in range(ROWS + 2 * NEAR)
    ]
    for source, row, start, width in plan:
        values = source(own_ref, top_ref, bottom_ref, row)
        here = (lane >= start) & (lane < start + width)
        left = jnp.where(here, pltpu.roll(values, start % 128, 1), left)
        right = jnp.where(here, pltpu.roll(values, (start + width) % 128, 1), right)
    left_ref[...] = left
    right_ref[...] = right


def flat_tiles(pieces, first, last, height=CP, base=None):
    lane = lanes_of(height)
    rolled = {}
    for index in range(first, last):
        result = jnp.zeros((height, 128), f32) if base is None else base(index)
        for number, (values, lane_from, flat_to, width) in enumerate(pieces):
            low, high = max(flat_to - 128 * index, 0), min(flat_to + width - 128 * index, 128)
            if low >= high:
                continue
            if number not in rolled:
                shift = (flat_to - lane_from) % 128
                rolled[number] = pltpu.roll(values(), shift, 1) if shift else values()
            result = jnp.where((lane >= low) & (lane < high), rolled[number], result)
        yield index, result


def forward_kernel(
    member_ref, own_ref, top_ref, bottom_ref, left_ref, right_ref, gain_ref, valid_ref, mine_ref, w1_ref, w2_ref,
    forecast_ref, truth_ref, pre_ref, hidden_ref, window_ref, latent_ref,
    latent, normed, window, hidden, partial, truth, pre_kept, hidden_kept, semaphores,
):
    pieces, truths = [], []
    for row in range(TALL):
        pieces.append((functools.partial(latent_row, own_ref, top_ref, bottom_ref, row), 0, PITCH * row + SIDE, COLS))
        pieces.append((lambda: left_ref[...], SIDE * row, PITCH * row, SIDE))
        pieces.append((lambda: right_ref[...], SIDE * row, PITCH * row + SIDE + COLS, SIDE))
    for row in range(ROWS + 2 * NEAR):
        flat, lane = PITCH * (row + FAR) + SIDE, SIDE * TALL + BESIDE * row
        truths.append((functools.partial(truth_row, own_ref, top_ref, bottom_ref, row), 0, flat, COLS))
        truths.append((lambda: left_ref[...], lane, flat - BESIDE, BESIDE))
        truths.append((lambda: right_ref[...], lane, flat + COLS, BESIDE))
    gain = gain_column(gain_ref)
    lane = lanes_of(CP)
    inner_low, inner_high = PITCH * FAR, PITCH * (TALL - FAR)
    normed[CP:CI, :] = jnp.zeros((CI - CP, FLAT), f32)
    for index, values in flat_tiles(pieces, 0, TILES):
        latent[:, tile(index)] = values
        start = 128 * index
        if start < inner_high and start + 128 > inner_low:
            centered, scale = centred(values)
            scaled = centered * scale * gain
            if start < inner_low or start + 128 > inner_high:
                inside = (lane >= inner_low - start) & (lane < inner_high - start)
                scaled = jnp.where(inside, scaled, values)
            values = scaled
        normed[0:CP, tile(index)] = values * valid_ref[:, tile(index)]
    own = pl.ds(128 * OWN[0], 128 * (OWN[1] - OWN[0]))
    moves = started((latent.at[:, own], latent_ref), semaphores=semaphores)
    for index, values in flat_tiles(truths, *SPREAD):
        truth[pl.ds(CP * (index - SPREAD[0]), CP), :] = values
    filled = CP * (SPREAD[1] - SPREAD[0])
    truth[filled:, :] = jnp.zeros((MEMBERS * CHUNK - filled, 128), f32)
    truth_ref[...] = truth[pl.ds(pl.multiple_of(member_ref[0] * CHUNK, 8), CHUNK), :]

    for group in range(CI // 16):
        values = normed[16 * group : 16 * group + 16, :]
        for offset in range(9):
            shift = -step_of(offset) % FLAT
            moved = pltpu.roll(values, shift, 1) if shift else values
            window[CI * offset + 16 * group : CI * offset + 16 * group + 16, :] = moved.astype(bf16)
    moves += started((window.at[:, own], window_ref), semaphores=semaphores.at[1:2])

    for number, first in enumerate(range(0, TILES, 4)):
        last = min(first + 4, TILES)
        span = slice(128 * first, 128 * last)
        pre = jnp.dot(w1_ref[...], window[:, span], preferred_element_type=f32)
        low, high = max(first, OWN[0]), min(last, OWN[1])
        if low < high:
            kept = pl.ds(128 * (low - OWN[0]), 128 * (high - low))
            pre_kept[:, kept] = pre[:, 128 * (low - first) : 128 * (high - first)]
            moves += started((pre_kept.at[:, kept], pre_ref.at[:, kept]), semaphores=semaphores.at[number + 3 : number + 4])
        curve = jnp.tanh(GELU_A * (pre + GELU_B * (pre * pre * pre)))
        hidden[:, span] = (0.5 * pre * (1.0 + curve) * valid_ref[:, span]).astype(bf16)
        partial[:, span] = jnp.dot(w2_ref[...], hidden[:, span], preferred_element_type=f32)
    hidden_kept[...] = (hidden[:, 128 * OWN[0] : 128 * OWN[1]].astype(f32) * mine_ref[...]).astype(bf16)
    moves += started((hidden_kept, hidden_ref), semaphores=semaphores.at[2:3])

    for group in range(CP // 8):
        total = None
        for offset in range(9):
            start = CP * offset + 8 * group
            shift = -step_of(offset) % FLAT
            values = partial[start : start + 8, :]
            moved = pltpu.roll(values, shift, 1) if shift else values
            total = moved if total is None else total + moved
        for index in range(*SPREAD):
            start = CP * (index - SPREAD[0]) + 8 * group
            forecast_ref[start : start + 8, :] = (
                total[:, 128 * index : 128 * index + 128] + latent[8 * group : 8 * group + 8, tile(index)]
            )
    forecast_ref[filled:, :] = jnp.zeros((MEMBERS * CHUNK - filled, 128), f32)
    for move in moves:
        move.wait()


def soft_slope(values):
    return values * lax.rsqrt(values * values + soft_eps)


def score_kernel(forecast_ref, truth_ref, grad_ref, grads):
    def body(step, carry):
        span = pl.ds(pl.multiple_of(8 * step, 8), 8)
        truth = truth_ref[span, :]
        values = [forecast_ref[m, span, :] for m in range(MEMBERS)]
        totals = [jnp.zeros((8, 128), f32)] * MEMBERS
        for first in range(MEMBERS):
            for second in range(first):
                slope = soft_slope(values[first] - values[second])
                totals[first] = totals[first] + slope
                totals[second] = totals[second] - slope
        for m in range(MEMBERS):
            grads[m, span, :] = soft_slope(values[m] - truth) - totals[m] * (1.0 / (MEMBERS - 1))
        return carry

    lax.fori_loop(0, CHUNK // 8, body, 0)
    grad_ref[...] = grads[...].astype(bf16)


def flat_lanes(values, start, count):
    index, off = divmod(start - 128 * OWN[0], 128)
    near = pltpu.roll(values(index), 128 - off, 1)
    if index + 1 == count:
        return near
    far = pltpu.roll(values(index + 1), 128 - off, 1)
    return jnp.where(lanes_of(near.shape[0]) < 128 - off, near, far)


def backward_kernel(
    grad_ref, pre_far, hidden_far, window_far, valid_ref, mine_ref, wide_ref, w2_ref,
    grad_pre_ref, own_grad_ref, weights_ref, up_ref, down_ref,
    pre_ref, hidden_ref, window_ref, chunks, grad, window, grad_pre, packed, semaphores,
):
    moves = started((hidden_far, hidden_ref), (pre_far, pre_ref), (window_far, window_ref), semaphores=semaphores)
    for m in range(MEMBERS):
        chunks[CHUNK * m : CHUNK * m + CHUNK, :] = grad_ref[m].astype(f32)
    edge = 128 * SPREAD[0]
    grad[:, 0:edge] = jnp.zeros((CI, edge), f32)
    grad[:, 128 * SPREAD[1] :] = jnp.zeros((CI, FLAT - 128 * SPREAD[1]), f32)
    grad[CP:CI, :] = jnp.zeros((CI - CP, FLAT), f32)
    for index in range(*SPREAD):
        values = chunks[CP * (index - SPREAD[0]) : CP * (index - SPREAD[0]) + CP, :]
        grad[0:CP, tile(index)] = values * valid_ref[:, tile(index)]
    low, high = 128 * OWN[0], 128 * OWN[1]
    for group in range(CI // 16):
        values = grad[16 * group : 16 * group + 16, :]
        for offset in range(9):
            shift = step_of(offset) % FLAT
            moved = pltpu.roll(values, shift, 1) if shift else values
            window[CI * offset + 16 * group : CI * offset + 16 * group + 16, :] = moved[:, low:high].astype(bf16)
    own = pl.ds(low, high - low)
    later = started((grad.at[0:CP, own], own_grad_ref), semaphores=semaphores.at[3:4])
    moves[0].wait()
    across = (((1,), (1,)), ((), ()))
    grad_out = lax.dot_general(window[...], hidden_ref[...], across, preferred_element_type=f32)
    for k in range(9):
        values = grad_out[CI * k : CI * k + C, :]
        packed[C * (9 + k) : C * (10 + k), :] = values[:, 0:128]
        packed[C * (18 + k) : C * (19 + k), 64:128] = values[:, 128:192]
    moves[1].wait()
    for first in range(0, high - low, 512):
        span = slice(first, min(first + 512, high - low))
        grad_hidden = jnp.dot(w2_ref[...], window[:, span], preferred_element_type=f32)
        pre = pre_ref[:, span]
        square = pre * pre
        curve = jnp.tanh(GELU_A * (pre + GELU_B * (square * pre)))
        slope = 0.5 * (1.0 + curve) + 0.5 * pre * (1.0 - curve * curve) * (GELU_A * (1.0 + 3.0 * GELU_B * square))
        grad_pre[:, span] = (grad_hidden * slope * wide_ref[:, span]).astype(bf16)
    later += started((grad_pre, grad_pre_ref), semaphores=semaphores.at[4:5])
    own_pre = (grad_pre[...].astype(f32) * mine_ref[...]).astype(bf16)
    moves[2].wait()
    grad_in = lax.dot_general(window_ref[...], own_pre, across, preferred_element_type=f32)
    for k in range(9):
        values = grad_in[CI * k : CI * k + C, :]
        packed[C * k : C * (k + 1), :] = values[:, 0:128]
        packed[C * (18 + k) : C * (19 + k), 0:64] = values[:, 128:192]
    packed[27 * C :, :] = jnp.zeros((GROUPS * PIECE - 27 * C, 128), f32)
    for place in range(GROUPS):
        weights_ref[place] = packed[PIECE * place : PIECE * place + PIECE, :].astype(bf16)
    for row, sent_ref in ((0, up_ref), (ROWS - 1, down_ref)):
        start = PITCH * (row + RIM) + SIDE - 1
        for half in range(2):
            values = flat_lanes(lambda index: grad_pre[:, tile(index)].astype(f32), start + 128 * half, OWN[1] - OWN[0])
            sent_ref[:, tile(half)] = values.astype(bf16)
    for move in later:
        move.wait()


def states_kernel(
    grad_pre_far, grad_far, latent_far, gain_ref, w1_ref, top_ref, bottom_ref,
    states_ref,
    own_pre, grad, latent, grad_pre, partial, shifted, result, semaphores,
):
    moves = started((grad_pre_far, own_pre), (latent_far, latent), (grad_far, grad), semaphores=semaphores)
    span = 128 * (SPREAD[1] - SPREAD[0])
    inner = slice(128 * (OWN[0] - SPREAD[0]), 128 * (OWN[1] - SPREAD[0]))
    moves[0].wait()

    def base(index):
        if OWN[0] <= index < OWN[1]:
            return own_pre[:, tile(index - OWN[0])].astype(f32)
        return jnp.zeros((HID, 128), f32)

    pieces = []
    for row, strip_ref in ((RIM - 1, top_ref), (RIM + ROWS, bottom_ref)):
        for half, width in ((0, 128), (1, COLS + 2 - 128)):
            values = functools.partial(lambda ref, index: ref[:, tile(index)].astype(f32), strip_ref, half)
            pieces.append((values, 0, PITCH * row + SIDE - 1 + 128 * half, width))
    for index, values in flat_tiles(pieces, *SPREAD, HID, base):
        grad_pre[:, tile(index - SPREAD[0])] = values.astype(bf16)
    for first in range(0, span, 512):
        some = slice(first, min(first + 512, span))
        partial[:, some] = jnp.dot(w1_ref[...], grad_pre[:, some], preferred_element_type=f32)
    for group in range(CP // 8):
        total = None
        for offset in range(9):
            start = CP * offset + 8 * group
            shift = step_of(offset) % span
            values = partial[start : start + 8, :]
            moved = pltpu.roll(values, shift, 1) if shift else values
            total = moved if total is None else total + moved
        shifted[8 * group : 8 * group + 8, :] = total[:, inner]
    gain = gain_column(gain_ref)
    for move in moves[1:]:
        move.wait()
    for index in range(OWN[1] - OWN[0]):
        centered, scale = centred(latent[:, tile(index)])
        unit = centered * scale
        pull = shifted[:, tile(index)] * gain
        mean_pull = jnp.sum(pull, axis=0, keepdims=True) * (1.0 / C)
        mean_both = jnp.sum(pull * unit, axis=0, keepdims=True) * (1.0 / C)
        shifted[:, tile(index)] = grad[:, tile(index)] + scale * (pull - mean_pull - unit * mean_both)
    for row in range(ROWS):
        start = PITCH * (row + RIM) + SIDE
        values = flat_lanes(lambda index: shifted[:, tile(index)], start, OWN[1] - OWN[0])
        result[pl.ds(row, C, stride=ROWS), :] = values[0:C]
    states_ref[...] = result[...].astype(bf16)


def total_kernel(parts_ref, copies_ref):
    total = parts_ref[0].astype(f32)
    for index in range(1, parts_ref.shape[0]):
        total = total + parts_ref[index].astype(f32)
    total = total.astype(bf16)
    for index in range(copies_ref.shape[0]):
        copies_ref[index] = total


def weights_kernel(parts_ref, grad_in_ref, grad_out_ref, packed):
    scale = 1.0 / math.sqrt(MEMBERS * 32 * 512)
    for place in range(GROUPS):
        packed[PIECE * place : PIECE * place + PIECE, :] = parts_ref[place].astype(f32) * scale
    for k in range(9):
        first = packed[C * k : C * (k + 1), :]
        second = packed[C * (9 + k) : C * (10 + k), :]
        shared = packed[C * (18 + k) : C * (19 + k), :]
        grad_out_ref[k, :, 0:128] = second
        grad_out_ref[k, :, 128:192] = shared[:, 64:128]
        grad_in_ref[k, :, 0:128] = first
        grad_in_ref[k, :, 128:192] = shared[:, 0:64]


def neighbours(axis, periodic):
    count = lax.axis_size(axis)
    forward = [(i, i + 1) for i in range(count - 1)]
    if periodic:
        forward.append((count - 1, 0))
    return forward, [(target, source) for source, target in forward]


def swap(values, axes):
    return lax.all_to_all(values, axes, split_axis=0, concat_axis=0, tiled=True)


def on_device(
    embeddings,
    entry_perturbation,
    target,
    feature_scale_factor,
    first_stencil_kernel,
    second_stencil_kernel,
):
    def padded(weight, dim, size):
        pads = [(0, 0)] * 3
        pads[dim] = (0, size - weight.shape[dim])
        return jnp.pad(weight, pads)

    member_axes, plane = ("half", "ring"), ("half", "lat", "lon")
    gain = feature_scale_factor[None]
    block = (C, ROWS, COLS)
    rim = ((3 * NEAR + FAR, CP, 128), bf16)
    own, up, down = call(
        rows_kernel,
        6,
        [((2 * ROWS, CP, 128), f32), rim, rim],
        [(block, bf16)] * 3 + [((C * ROWS, COLS), f32)] * 3,
        embeddings.reshape(block), entry_perturbation.reshape(block), target, gain,
        far=(0, 1, 2), home=(3,), copies=3,
    )
    forward, backward = neighbours("lat", False)
    top = lax.ppermute(down, "lat", forward)
    bottom = lax.ppermute(up, "lat", backward)
    to_left, to_right = call(
        columns_kernel, 6, [((CP, 128), f32)] * 2, [], own, top, bottom, close=(0, 1, 2)
    )
    forward, backward = neighbours("lon", True)
    left = lax.ppermute(to_right, "lon", forward)
    right = lax.ppermute(to_left, "lon", backward)

    place = jnp.arange(FLAT, dtype=jnp.int32)
    row, column = place // PITCH - RIM, place % PITCH - SIDE
    line = row + ROWS * lax.axis_index("lat")
    valid = ((line >= 0) & (line < ROWS * lax.axis_size("lat"))).astype(f32)[None]
    mine = ((row >= 0) & (row < ROWS) & (column >= 0) & (column < COLS)).astype(f32)[None]
    mine = mine[:, 128 * OWN[0] : 128 * OWN[1]]
    wide = ((row >= 0) & (row < ROWS) & (column >= -1) & (column <= COLS)).astype(f32)[None]
    wide = wide[:, 128 * OWN[0] : 128 * OWN[1]]
    w1_stack = padded(first_stencil_kernel, 2, CI).transpose(1, 0, 2).reshape(HID, 9 * CI)
    w2_stack = padded(second_stencil_kernel, 1, CP).reshape(9 * CP, HID)
    w2_turned = padded(second_stencil_kernel, 1, CI).transpose(2, 0, 1).reshape(HID, 9 * CI)
    w1_turned = padded(first_stencil_kernel.transpose(0, 2, 1), 1, CP).reshape(9 * CP, HID)

    member = lax.axis_index(member_axes).astype(jnp.int32)[None]
    own_lanes = OWN_LANES
    spread_lanes = 128 * (SPREAD[1] - SPREAD[0])
    forecast, truth, pre, hidden, window, latent = call(
        forward_kernel,
        26,
        [
            ((MEMBERS * CHUNK, 128), f32),
            ((CHUNK, 128), f32),
            ((HID, own_lanes), (f32,)),
            ((HID, own_lanes), (bf16,)),
            ((9 * CI, own_lanes), (bf16,)),
            ((CP, own_lanes), (f32,)),
        ],
        [
            ((CP, FLAT), f32),
            ((CI, FLAT), f32),
            ((9 * CI, FLAT), bf16),
            ((HID, FLAT), bf16),
            ((9 * CP, FLAT), f32),
            ((MEMBERS * CHUNK, 128), f32),
            ((HID, own_lanes), f32),
            ((HID, own_lanes), bf16),
        ],
        member, own, top, bottom, left, right, gain, valid, mine, w1_stack, w2_stack,
        smem=1, close=(1, 2, 3, 4, 5), copies=7,
    )
    spread = swap(forecast.reshape(MEMBERS, CHUNK, 128), member_axes)
    (grads,) = call(
        score_kernel,
        6,
        [((MEMBERS, CHUNK, 128), bf16)],
        [((MEMBERS, CHUNK, 128), f32)],
        spread, truth,
    )
    grads = swap(grads, member_axes)
    strip = ((HID, 256), bf16)
    grad_pre, own_grad, weights, up, down = call(
        backward_kernel,
        22,
        [
            ((HID, own_lanes), (bf16,)),
            ((CP, own_lanes), (f32,)),
            ((GROUPS, PIECE, 128), bf16),
            strip, strip,
        ],
        [
            ((HID, own_lanes), f32),
            ((HID, own_lanes), bf16),
            ((9 * CI, own_lanes), bf16),
            ((MEMBERS * CHUNK, 128), f32),
            ((CI, FLAT), f32),
            ((9 * CI, own_lanes), bf16),
            ((HID, own_lanes), bf16),
            ((GROUPS * PIECE, 128), f32),
        ],
        grads, pre, hidden, window, valid, mine, wide, w2_turned,
        far=(1, 2, 3), copies=5,
    )
    parts = swap(weights, plane)
    forward, backward = neighbours("lat", False)
    parts, top, bottom = lax.optimization_barrier(
        (parts, lax.ppermute(down, "lat", forward), lax.ppermute(up, "lat", backward))
    )
    piece = (PIECE, 128)
    (copies,) = call(total_kernel, 6, [((RING,) + piece, bf16)], [], parts)
    (copies,) = call(total_kernel, 6, [((GROUPS,) + piece, bf16)], [], swap(copies, "ring"))
    (states,) = call(
        states_kernel,
        16,
        [((C * ROWS, COLS), bf16)],
        [
            ((HID, own_lanes), bf16),
            ((CP, own_lanes), f32),
            ((CP, own_lanes), f32),
            ((HID, spread_lanes), bf16),
            ((9 * CP, spread_lanes), f32),
            ((CP, own_lanes), f32),
            ((C * ROWS, COLS), f32),
        ],
        grad_pre, own_grad, latent, gain, w1_turned, top, bottom,
        far=(0, 1, 2), copies=3,
    )
    grad_in, grad_out = call(
        weights_kernel,
        8,
        [((9, C, HID), f32), ((9, C, HID), f32)],
        [((GROUPS * PIECE, 128), f32)],
        swap(copies, plane),
    )
    grad_in = grad_in.transpose(0, 2, 1)
    return (states.reshape(embeddings.shape), grad_in, grad_out)


def solution(mesh):
    places = mesh.devices.reshape(MEMBERS // RING, RING, *mesh.devices.shape[1:])
    fine = jax.sharding.Mesh(places, ("half", "ring", "lat", "lon"))
    whole = P(("half", "ring"), None, "lat", "lon")
    return jax.shard_map(
        on_device,
        mesh=fine,
        in_specs=(whole, whole, P(None, "lat", "lon"), P(), P(), P()),
        out_specs=(whole, P(), P()),
        check_vma=False,
    )
```

```python
import functools
import math

import jax
import jax.numpy as jnp
from jax import lax
from jax.experimental import pallas as pl
from jax.experimental.pallas import tpu as pltpu
from jax.sharding import PartitionSpec as P

soft_eps = 0.01
norm_eps = 1e-05
C = 83
CP = 88
CI = 96
HID = 192
ROWS = 8
COLS = 128
NEAR = 1
FAR = 2
RIM = NEAR + FAR
SIDE = 4
BESIDE = 2
PITCH = COLS + 2 * SIDE
TALL = ROWS + 2 * RIM
TILES = -(-TALL * PITCH // 128)
FLAT = 128 * TILES
SPREAD = (2, 13)
OWN = (3, 12)
OWN_LANES = 128 * (OWN[1] - OWN[0])
MEMBERS = 16
GROUPS = 32
RING = 8
CHUNK = 64
PIECE = 72
f32 = jnp.float32
bf16 = jnp.bfloat16
GELU_A = math.sqrt(2.0 / math.pi)
GELU_B = 0.044715


def call(kernel, limit, outs, scratch, *operands, smem=0, far=(), close=(), home=(), copies=0):
    near = pl.BlockSpec(memory_space=pltpu.VMEM)
    away = pl.BlockSpec(memory_space=pltpu.HBM)
    specs = [pl.BlockSpec(memory_space=pltpu.SMEM)] * smem
    specs += [away if i in far else near for i in range(smem, len(operands))]
    kinds = [kind[0] if isinstance(kind, tuple) else kind for _, kind in outs]
    placed = {i: pltpu.VMEM for i in close} | {i: pltpu.HBM for i in (*far, *home)}
    operands = [
        pltpu.with_memory_space_constraint(operand, placed[i]) if i in placed else operand
        for i, operand in enumerate(operands)
    ]
    kept = [pltpu.VMEM(shape, kind) for shape, kind in scratch]
    return pl.pallas_call(
        kernel,
        out_shape=[
            (pltpu.HBM if isinstance(given, tuple) else jax.ShapeDtypeStruct)(shape, kind)
            for (shape, given), kind in zip(outs, kinds)
        ],
        in_specs=specs,
        out_specs=[away if isinstance(kind, tuple) else near for _, kind in outs],
        scratch_shapes=kept + ([pltpu.SemaphoreType.DMA((copies,))] if copies else []),
        compiler_params=pltpu.CompilerParams(vmem_limit_bytes=limit << 20),
    )(*operands)


def started(*pairs, semaphores):
    moves = [
        pltpu.make_async_copy(source, target, semaphores.at[i]) for i, (source, target) in enumerate(pairs)
    ]
    for move in moves:
        move.start()
    return moves


def gain_column(gain_ref):
    row = lax.broadcasted_iota(jnp.int32, (CP, C), 0)
    lane = lax.broadcasted_iota(jnp.int32, (CP, C), 1)
    spread = jnp.where(row == lane, jnp.broadcast_to(gain_ref[...], (CP, C)), 0.0)
    return jnp.sum(spread, axis=1, keepdims=True)


def centred(values):
    real = lax.broadcasted_iota(jnp.int32, (CP, 128), 0) < C
    average = jnp.sum(values, axis=0, keepdims=True) * (1.0 / C)
    centered = jnp.where(real, values - average, 0.0)
    variance = jnp.sum(centered * centered, axis=0, keepdims=True) * (1.0 / C)
    return centered, lax.rsqrt(variance + norm_eps)


def step_of(offset):
    return (offset // 3 - 1) * PITCH + offset % 3 - 1


def tile(index):
    return pl.ds(128 * index, 128)


def lanes_of(height):
    return lax.broadcasted_iota(jnp.int32, (height, 128), 1)


def rows_kernel(
    emb_ref, pert_ref, target_ref, gain_ref, own_ref, up_ref, down_ref, left_ref, right_ref, emb, pert, target, first, second, truth, semaphores,
):
    moves = started((emb_ref, emb), (pert_ref, pert), (target_ref, target), semaphores=semaphores)
    for move, source, wide in zip(moves, (emb, pert, target), (first, second, truth)):
        move.wait()
        wide[...] = source[...].astype(f32).reshape(C * ROWS, COLS)
    rest = jnp.zeros((CP - C, 128), f32)
    gain = gain_column(gain_ref)

    def row_of(source, r):
        return jnp.concatenate([source[pl.ds(r, C, stride=ROWS), :], rest], axis=0)

    lane = lanes_of(CP)
    left, right = jnp.zeros((CP, 128), f32), jnp.zeros((CP, 128), f32)
    for r in range(ROWS):
        parts = row_of(first, r), row_of(second, r)
        goal = row_of(truth, r)
        latent = parts[0] + parts[1]
        own_ref[r] = latent
        own_ref[ROWS + r] = goal
        sides = (latent, SIDE * (RIM + r), SIDE), (goal, SIDE * TALL + BESIDE * (NEAR + r), BESIDE)
        for values, start, width in sides:
            here = (lane >= start) & (lane < start + width)
            left = jnp.where(here, pltpu.roll(values, start % 128, 1), left)
            right = jnp.where(here, pltpu.roll(values, (start + width) % 128, 1), right)
        if RIM <= r < ROWS - RIM:
            continue
        sent, first_row = (up_ref, 0) if r < RIM else (down_ref, ROWS - RIM)
        if r < NEAR or r >= ROWS - NEAR:
            index = r - first_row if r < RIM else r - (ROWS - NEAR)
            sent[index] = parts[0].astype(bf16)
            sent[NEAR + index] = parts[1].astype(bf16)
            sent[2 * NEAR + FAR + index] = goal.astype(bf16)
        else:
            centered, scale = centred(latent)
            index = r - NEAR if r < RIM else r - first_row
            sent[2 * NEAR + index] = (centered * scale * gain).astype(bf16)
    left_ref[...] = left
    right_ref[...] = right


def latent_row(own_ref, top_ref, bottom_ref, row):
    def near(rim_ref, r):
        return rim_ref[r].astype(f32) + rim_ref[NEAR + r].astype(f32)

    if row < FAR:
        return top_ref[2 * NEAR + row].astype(f32)
    if row < RIM:
        return near(top_ref, row - FAR)
    if row < RIM + ROWS:
        return own_ref[row - RIM]
    if row < RIM + ROWS + NEAR:
        return near(bottom_ref, row - RIM - ROWS)
    return bottom_ref[2 * NEAR + row - RIM - ROWS - NEAR].astype(f32)


def truth_row(own_ref, top_ref, bottom_ref, row):
    base = 2 * NEAR + FAR
    if row < NEAR:
        return top_ref[base + row].astype(f32)
    if row < NEAR + ROWS:
        return own_ref[ROWS + row - NEAR]
    return bottom_ref[base + row - NEAR - ROWS].astype(f32)


def columns_kernel(left_ref, right_ref, both_ref):
    both_ref[0] = left_ref[...]
    both_ref[1] = right_ref[...]


def flat_tiles(pieces, first, last, height=CP, base=None):
    lane = lanes_of(height)
    rolled = {}
    for index in range(first, last):
        result = jnp.zeros((height, 128), f32) if base is None else base(index)
        for number, (values, lane_from, flat_to, width) in enumerate(pieces):
            low, high = max(flat_to - 128 * index, 0), min(flat_to + width - 128 * index, 128)
            if low >= high:
                continue
            if number not in rolled:
                shift = (flat_to - lane_from) % 128
                rolled[number] = pltpu.roll(values(), shift, 1) if shift else values()
            result = jnp.where((lane >= low) & (lane < high), rolled[number], result)
        yield index, result


def forward_kernel(
    member_ref, own_ref, top_ref, bottom_ref, left_ref, right_ref, above_ref, below_ref, gain_ref, valid_ref, mine_ref, w1_ref, w2_ref,
    forecast_ref, truth_ref, pre_ref, hidden_ref, window_ref, latent_ref,
    latent, normed, window, hidden, partial, truth, pre_kept, hidden_kept, semaphores,
):
    gain = gain_column(gain_ref)

    def side_of(row, near, rows):
        if row < near:
            return above_ref, row + ROWS
        if row < near + rows:
            return None, row
        return below_ref, row - ROWS

    scaled_sides = {}

    def side(ref, which, far):
        if ref is None:
            return (left_ref, right_ref)[which][...]
        if not far:
            return ref[which]
        if (id(ref), which) not in scaled_sides:
            centered, scale = centred(ref[which])
            scaled_sides[id(ref), which] = centered * scale * gain
        return scaled_sides[id(ref), which]

    pieces, truths = [], []
    for row in range(TALL):
        ref, place = side_of(row, RIM, ROWS)
        far = row < FAR or row >= TALL - FAR
        pieces.append((functools.partial(latent_row, own_ref, top_ref, bottom_ref, row), 0, PITCH * row + SIDE, COLS))
        for which, flat in ((0, PITCH * row), (1, PITCH * row + SIDE + COLS)):
            pieces.append((functools.partial(side, ref, which, far), SIDE * place, flat, SIDE))
    for row in range(ROWS + 2 * NEAR):
        ref, place = side_of(row, NEAR, ROWS)
        flat, lane = PITCH * (row + FAR) + SIDE, SIDE * TALL + BESIDE * place
        truths.append((functools.partial(truth_row, own_ref, top_ref, bottom_ref, row), 0, flat, COLS))
        truths.append((functools.partial(side, ref, 0, False), lane, flat - BESIDE, BESIDE))
        truths.append((functools.partial(side, ref, 1, False), lane, flat + COLS, BESIDE))
    lane = lanes_of(CP)
    inner_low, inner_high = PITCH * FAR, PITCH * (TALL - FAR)
    normed[CP:CI, :] = jnp.zeros((CI - CP, FLAT), f32)
    for index, values in flat_tiles(pieces, 0, TILES):
        latent[:, tile(index)] = values
        start = 128 * index
        if start < inner_high and start + 128 > inner_low:
            centered, scale = centred(values)
            scaled = centered * scale * gain
            if start < inner_low or start + 128 > inner_high:
                inside = (lane >= inner_low - start) & (lane < inner_high - start)
                scaled = jnp.where(inside, scaled, values)
            values = scaled
        normed[0:CP, tile(index)] = values * valid_ref[:, tile(index)]
    own = pl.ds(128 * OWN[0], 128 * (OWN[1] - OWN[0]))
    moves = started((latent.at[:, own], latent_ref), semaphores=semaphores)
    for index, values in flat_tiles(truths, *SPREAD):
        truth[pl.ds(CP * (index - SPREAD[0]), CP), :] = values
    filled = CP * (SPREAD[1] - SPREAD[0])
    truth[filled:, :] = jnp.zeros((MEMBERS * CHUNK - filled, 128), f32)
    truth_ref[...] = truth[pl.ds(pl.multiple_of(member_ref[0] * CHUNK, 8), CHUNK), :]

    for group in range(CI // 16):
        values = normed[16 * group : 16 * group + 16, :]
        for offset in range(9):
            shift = -step_of(offset) % FLAT
            moved = pltpu.roll(values, shift, 1) if shift else values
            window[CI * offset + 16 * group : CI * offset + 16 * group + 16, :] = moved.astype(bf16)
    moves += started((window.at[:, own], window_ref), semaphores=semaphores.at[1:2])

    for number, first in enumerate(range(0, TILES, 4)):
        last = min(first + 4, TILES)
        span = slice(128 * first, 128 * last)
        pre = jnp.dot(w1_ref[...], window[:, span], preferred_element_type=f32)
        low, high = max(first, OWN[0]), min(last, OWN[1])
        if low < high:
            kept = pl.ds(128 * (low - OWN[0]), 128 * (high - low))
            pre_kept[:, kept] = pre[:, 128 * (low - first) : 128 * (high - first)]
            moves += started((pre_kept.at[:, kept], pre_ref.at[:, kept]), semaphores=semaphores.at[number + 3 : number + 4])
        curve = jnp.tanh(GELU_A * (pre + GELU_B * (pre * pre * pre)))
        hidden[:, span] = (0.5 * pre * (1.0 + curve) * valid_ref[:, span]).astype(bf16)
        partial[:, span] = jnp.dot(w2_ref[...], hidden[:, span], preferred_element_type=f32)
    hidden_kept[...] = (hidden[:, 128 * OWN[0] : 128 * OWN[1]].astype(f32) * mine_ref[...]).astype(bf16)
    moves += started((hidden_kept, hidden_ref), semaphores=semaphores.at[2:3])

    for group in range(CP // 8):
        total = None
        for offset in range(9):
            start = CP * offset + 8 * group
            shift = -step_of(offset) % FLAT
            values = partial[start : start + 8, :]
            moved = pltpu.roll(values, shift, 1) if shift else values
            total = moved if total is None else total + moved
        for index in range(*SPREAD):
            start = CP * (index - SPREAD[0]) + 8 * group
            forecast_ref[start : start + 8, :] = (
                total[:, 128 * index : 128 * index + 128] + latent[8 * group : 8 * group + 8, tile(index)]
            )
    forecast_ref[filled:, :] = jnp.zeros((MEMBERS * CHUNK - filled, 128), f32)
    for move in moves:
        move.wait()


def soft_slope(values):
    return values * lax.rsqrt(values * values + soft_eps)


def score_kernel(forecast_ref, truth_ref, grad_ref, grads):
    def body(step, carry):
        span = pl.ds(pl.multiple_of(8 * step, 8), 8)
        truth = truth_ref[span, :]
        values = [forecast_ref[m, span, :] for m in range(MEMBERS)]
        totals = [jnp.zeros((8, 128), f32)] * MEMBERS
        for first in range(MEMBERS):
            for second in range(first):
                slope = soft_slope(values[first] - values[second])
                totals[first] = totals[first] + slope
                totals[second] = totals[second] - slope
        for m in range(MEMBERS):
            grads[m, span, :] = soft_slope(values[m] - truth) - totals[m] * (1.0 / (MEMBERS - 1))
        return carry

    lax.fori_loop(0, CHUNK // 8, body, 0)
    grad_ref[...] = grads[...].astype(bf16)


def flat_lanes(values, start, count):
    index, off = divmod(start - 128 * OWN[0], 128)
    near = pltpu.roll(values(index), 128 - off, 1)
    if index + 1 == count:
        return near
    far = pltpu.roll(values(index + 1), 128 - off, 1)
    return jnp.where(lanes_of(near.shape[0]) < 128 - off, near, far)


def backward_kernel(
    grad_ref, pre_far, hidden_far, window_far, valid_ref, mine_ref, wide_ref, w2_ref,
    grad_pre_ref, own_grad_ref, weights_ref, up_ref, down_ref,
    pre_ref, hidden_ref, window_ref, chunks, grad, window, grad_pre, packed, semaphores,
):
    moves = started((hidden_far, hidden_ref), (pre_far, pre_ref), (window_far, window_ref), semaphores=semaphores)
    for m in range(MEMBERS):
        chunks[CHUNK * m : CHUNK * m + CHUNK, :] = grad_ref[m].astype(f32)
    edge = 128 * SPREAD[0]
    grad[:, 0:edge] = jnp.zeros((CI, edge), f32)
    grad[:, 128 * SPREAD[1] :] = jnp.zeros((CI, FLAT - 128 * SPREAD[1]), f32)
    grad[CP:CI, :] = jnp.zeros((CI - CP, FLAT), f32)
    for index in range(*SPREAD):
        values = chunks[CP * (index - SPREAD[0]) : CP * (index - SPREAD[0]) + CP, :]
        grad[0:CP, tile(index)] = values * valid_ref[:, tile(index)]
    low, high = 128 * OWN[0], 128 * OWN[1]
    for group in range(CI // 16):
        values = grad[16 * group : 16 * group + 16, :]
        for offset in range(9):
            shift = step_of(offset) % FLAT
            moved = pltpu.roll(values, shift, 1) if shift else values
            window[CI * offset + 16 * group : CI * offset + 16 * group + 16, :] = moved[:, low:high].astype(bf16)
    own = pl.ds(low, high - low)
    later = started((grad.at[0:CP, own], own_grad_ref), semaphores=semaphores.at[3:4])
    moves[0].wait()
    across = (((1,), (1,)), ((), ()))
    grad_out = lax.dot_general(window[...], hidden_ref[...], across, preferred_element_type=f32)
    for k in range(9):
        values = grad_out[CI * k : CI * k + C, :]
        packed[C * (9 + k) : C * (10 + k), :] = values[:, 0:128]
        packed[C * (18 + k) : C * (19 + k), 64:128] = values[:, 128:192]
    moves[1].wait()
    for first in range(0, high - low, 512):
        span = slice(first, min(first + 512, high - low))
        grad_hidden = jnp.dot(w2_ref[...], window[:, span], preferred_element_type=f32)
        pre = pre_ref[:, span]
        square = pre * pre
        curve = jnp.tanh(GELU_A * (pre + GELU_B * (square * pre)))
        slope = 0.5 * (1.0 + curve) + 0.5 * pre * (1.0 - curve * curve) * (GELU_A * (1.0 + 3.0 * GELU_B * square))
        grad_pre[:, span] = (grad_hidden * slope * wide_ref[:, span]).astype(bf16)
    later += started((grad_pre, grad_pre_ref), semaphores=semaphores.at[4:5])
    own_pre = (grad_pre[...].astype(f32) * mine_ref[...]).astype(bf16)
    moves[2].wait()
    grad_in = lax.dot_general(window_ref[...], own_pre, across, preferred_element_type=f32)
    for k in range(9):
        values = grad_in[CI * k : CI * k + C, :]
        packed[C * k : C * (k + 1), :] = values[:, 0:128]
        packed[C * (18 + k) : C * (19 + k), 0:64] = values[:, 128:192]
    packed[27 * C :, :] = jnp.zeros((GROUPS * PIECE - 27 * C, 128), f32)
    for place in range(GROUPS):
        weights_ref[place] = packed[PIECE * place : PIECE * place + PIECE, :].astype(bf16)
    for row, sent_ref in ((0, up_ref), (ROWS - 1, down_ref)):
        start = PITCH * (row + RIM) + SIDE - 1
        for half in range(2):
            values = flat_lanes(lambda index: grad_pre[:, tile(index)].astype(f32), start + 128 * half, OWN[1] - OWN[0])
            sent_ref[:, tile(half)] = values.astype(bf16)
    for move in later:
        move.wait()


def states_kernel(
    grad_pre_far, grad_far, latent_far, gain_ref, w1_ref, top_ref, bottom_ref,
    states_ref,
    own_pre, grad, latent, grad_pre, partial, shifted, result, semaphores,
):
    moves = started((grad_pre_far, own_pre), (latent_far, latent), (grad_far, grad), semaphores=semaphores)
    span = 128 * (SPREAD[1] - SPREAD[0])
    inner = slice(128 * (OWN[0] - SPREAD[0]), 128 * (OWN[1] - SPREAD[0]))
    moves[0].wait()

    def base(index):
        if OWN[0] <= index < OWN[1]:
            return own_pre[:, tile(index - OWN[0])].astype(f32)
        return jnp.zeros((HID, 128), f32)

    pieces = []
    for row, strip_ref in ((RIM - 1, top_ref), (RIM + ROWS, bottom_ref)):
        for half, width in ((0, 128), (1, COLS + 2 - 128)):
            values = functools.partial(lambda ref, index: ref[:, tile(index)].astype(f32), strip_ref, half)
            pieces.append((values, 0, PITCH * row + SIDE - 1 + 128 * half, width))
    for index, values in flat_tiles(pieces, *SPREAD, HID, base):
        grad_pre[:, tile(index - SPREAD[0])] = values.astype(bf16)
    for first in range(0, span, 512):
        some = slice(first, min(first + 512, span))
        partial[:, some] = jnp.dot(w1_ref[...], grad_pre[:, some], preferred_element_type=f32)
    for group in range(CP // 8):
        total = None
        for offset in range(9):
            start = CP * offset + 8 * group
            shift = step_of(offset) % span
            values = partial[start : start + 8, :]
            moved = pltpu.roll(values, shift, 1) if shift else values
            total = moved if total is None else total + moved
        shifted[8 * group : 8 * group + 8, :] = total[:, inner]
    gain = gain_column(gain_ref)
    for move in moves[1:]:
        move.wait()
    for index in range(OWN[1] - OWN[0]):
        centered, scale = centred(latent[:, tile(index)])
        unit = centered * scale
        pull = shifted[:, tile(index)] * gain
        mean_pull = jnp.sum(pull, axis=0, keepdims=True) * (1.0 / C)
        mean_both = jnp.sum(pull * unit, axis=0, keepdims=True) * (1.0 / C)
        shifted[:, tile(index)] = grad[:, tile(index)] + scale * (pull - mean_pull - unit * mean_both)
    for row in range(ROWS):
        start = PITCH * (row + RIM) + SIDE
        values = flat_lanes(lambda index: shifted[:, tile(index)], start, OWN[1] - OWN[0])
        result[pl.ds(row, C, stride=ROWS), :] = values[0:C]
    states_ref[...] = result[...].astype(bf16)


def total_kernel(parts_ref, copies_ref):
    total = parts_ref[0].astype(f32)
    for index in range(1, parts_ref.shape[0]):
        total = total + parts_ref[index].astype(f32)
    total = total.astype(bf16)
    for index in range(copies_ref.shape[0]):
        copies_ref[index] = total


def weights_kernel(parts_ref, grad_in_ref, grad_out_ref, packed):
    scale = 1.0 / math.sqrt(MEMBERS * 32 * 512)
    for place in range(GROUPS):
        packed[PIECE * place : PIECE * place + PIECE, :] = parts_ref[place].astype(f32) * scale
    for k in range(9):
        first = packed[C * k : C * (k + 1), :]
        second = packed[C * (9 + k) : C * (10 + k), :]
        shared = packed[C * (18 + k) : C * (19 + k), :]
        grad_out_ref[k, :, 0:128] = second
        grad_out_ref[k, :, 128:192] = shared[:, 64:128]
        grad_in_ref[k, :, 0:128] = first
        grad_in_ref[k, :, 128:192] = shared[:, 0:64]


def neighbours(axis, periodic):
    count = lax.axis_size(axis)
    forward = [(i, i + 1) for i in range(count - 1)]
    if periodic:
        forward.append((count - 1, 0))
    return forward, [(target, source) for source, target in forward]


def swap(values, axes):
    return lax.all_to_all(values, axes, split_axis=0, concat_axis=0, tiled=True)


def on_device(
    embeddings,
    entry_perturbation,
    target,
    feature_scale_factor,
    first_stencil_kernel,
    second_stencil_kernel,
):
    def padded(weight, dim, size):
        pads = [(0, 0)] * 3
        pads[dim] = (0, size - weight.shape[dim])
        return jnp.pad(weight, pads)

    member_axes, plane = ("half", "ring"), ("half", "lat", "lon")
    gain = feature_scale_factor[None]
    block = (C, ROWS, COLS)
    rim = ((3 * NEAR + FAR, CP, 128), bf16)
    own, up, down, to_left, to_right = call(
        rows_kernel,
        6,
        [((2 * ROWS, CP, 128), f32), rim, rim, ((CP, 128), f32), ((CP, 128), f32)],
        [(block, bf16)] * 3 + [((C * ROWS, COLS), f32)] * 3,
        embeddings.reshape(block), entry_perturbation.reshape(block), target, gain,
        far=(0, 1, 2), home=(3,), copies=3,
    )
    forward, backward = neighbours("lat", False)
    top = lax.ppermute(down, "lat", forward)
    bottom = lax.ppermute(up, "lat", backward)
    to_below, to_above = forward, backward
    forward, backward = neighbours("lon", True)
    left = lax.ppermute(to_right, "lon", forward)
    right = lax.ppermute(to_left, "lon", backward)
    (both,) = call(columns_kernel, 6, [((2, CP, 128), f32)], [], left, right, close=(0, 1))
    above = lax.ppermute(both, "lat", to_below)
    below = lax.ppermute(both, "lat", to_above)

    place = jnp.arange(FLAT, dtype=jnp.int32)
    row, column = place // PITCH - RIM, place % PITCH - SIDE
    line = row + ROWS * lax.axis_index("lat")
    valid = ((line >= 0) & (line < ROWS * lax.axis_size("lat"))).astype(f32)[None]
    mine = ((row >= 0) & (row < ROWS) & (column >= 0) & (column < COLS)).astype(f32)[None]
    mine = mine[:, 128 * OWN[0] : 128 * OWN[1]]
    wide = ((row >= 0) & (row < ROWS) & (column >= -1) & (column <= COLS)).astype(f32)[None]
    wide = wide[:, 128 * OWN[0] : 128 * OWN[1]]
    w1_stack = padded(first_stencil_kernel, 2, CI).transpose(1, 0, 2).reshape(HID, 9 * CI)
    w2_stack = padded(second_stencil_kernel, 1, CP).reshape(9 * CP, HID)
    w2_turned = padded(second_stencil_kernel, 1, CI).transpose(2, 0, 1).reshape(HID, 9 * CI)
    w1_turned = padded(first_stencil_kernel.transpose(0, 2, 1), 1, CP).reshape(9 * CP, HID)

    member = lax.axis_index(member_axes).astype(jnp.int32)[None]
    own_lanes = OWN_LANES
    spread_lanes = 128 * (SPREAD[1] - SPREAD[0])
    forecast, truth, pre, hidden, window, latent = call(
        forward_kernel,
        26,
        [
            ((MEMBERS * CHUNK, 128), f32),
            ((CHUNK, 128), f32),
            ((HID, own_lanes), (f32,)),
            ((HID, own_lanes), (bf16,)),
            ((9 * CI, own_lanes), (bf16,)),
            ((CP, own_lanes), (f32,)),
        ],
        [
            ((CP, FLAT), f32),
            ((CI, FLAT), f32),
            ((9 * CI, FLAT), bf16),
            ((HID, FLAT), bf16),
            ((9 * CP, FLAT), f32),
            ((MEMBERS * CHUNK, 128), f32),
            ((HID, own_lanes), f32),
            ((HID, own_lanes), bf16),
        ],
        member, own, top, bottom, left, right, above, below, gain, valid, mine, w1_stack, w2_stack,
        smem=1, close=(1, 2, 3, 4, 5, 6, 7), copies=7,
    )
    spread = swap(forecast.reshape(MEMBERS, CHUNK, 128), member_axes)
    (grads,) = call(
        score_kernel,
        6,
        [((MEMBERS, CHUNK, 128), bf16)],
        [((MEMBERS, CHUNK, 128), f32)],
        spread, truth,
    )
    grads = swap(grads, member_axes)
    strip = ((HID, 256), bf16)
    grad_pre, own_grad, weights, up, down = call(
        backward_kernel,
        22,
        [
            ((HID, own_lanes), (bf16,)),
            ((CP, own_lanes), (f32,)),
            ((GROUPS, PIECE, 128), bf16),
            strip, strip,
        ],
        [
            ((HID, own_lanes), f32),
            ((HID, own_lanes), bf16),
            ((9 * CI, own_lanes), bf16),
            ((MEMBERS * CHUNK, 128), f32),
            ((CI, FLAT), f32),
            ((9 * CI, own_lanes), bf16),
            ((HID, own_lanes), bf16),
            ((GROUPS * PIECE, 128), f32),
        ],
        grads, pre, hidden, window, valid, mine, wide, w2_turned,
        far=(1, 2, 3), copies=5,
    )
    parts = swap(weights, plane)
    forward, backward = neighbours("lat", False)
    parts, top, bottom = lax.optimization_barrier(
        (parts, lax.ppermute(down, "lat", forward), lax.ppermute(up, "lat", backward))
    )
    piece = (PIECE, 128)
    (copies,) = call(total_kernel, 6, [((RING,) + piece, bf16)], [], parts)
    (copies,) = call(total_kernel, 6, [((GROUPS,) + piece, bf16)], [], swap(copies, "ring"))
    (states,) = call(
        states_kernel,
        16,
        [((C * ROWS, COLS), bf16)],
        [
            ((HID, own_lanes), bf16),
            ((CP, own_lanes), f32),
            ((CP, own_lanes), f32),
            ((HID, spread_lanes), bf16),
            ((9 * CP, spread_lanes), f32),
            ((CP, own_lanes), f32),
            ((C * ROWS, COLS), f32),
        ],
        grad_pre, own_grad, latent, gain, w1_turned, top, bottom,
        far=(0, 1, 2), copies=3,
    )
    grad_in, grad_out = call(
        weights_kernel,
        8,
        [((9, C, HID), f32), ((9, C, HID), f32)],
        [((GROUPS * PIECE, 128), f32)],
        swap(copies, plane),
    )
    grad_in = grad_in.transpose(0, 2, 1)
    return (states.reshape(embeddings.shape), grad_in, grad_out)


def solution(mesh):
    places = mesh.devices.reshape(MEMBERS // RING, RING, *mesh.devices.shape[1:])
    fine = jax.sharding.Mesh(places, ("half", "ring", "lat", "lon"))
    whole = P(("half", "ring"), None, "lat", "lon")
    return jax.shard_map(
        on_device,
        mesh=fine,
        in_specs=(whole, whole, P(None, "lat", "lon"), P(), P(), P()),
        out_specs=(whole, P(), P()),
        check_vma=False,
    )
```

```python
import functools
import math

import jax
import jax.numpy as jnp
from jax import lax
from jax.experimental import pallas as pl
from jax.experimental.pallas import tpu as pltpu
from jax.sharding import PartitionSpec as P

soft_eps = 0.01
norm_eps = 1e-05
C = 83
CP = 88
CI = 96
HID = 192
ROWS = 8
COLS = 128
NEAR = 1
FAR = 2
RIM = NEAR + FAR
SIDE = 4
BESIDE = 2
PITCH = COLS + 2 * SIDE
TALL = ROWS + 2 * RIM
TILES = -(-TALL * PITCH // 128)
FLAT = 128 * TILES
SPREAD = (2, 13)
OWN = (3, 12)
OWN_LANES = 128 * (OWN[1] - OWN[0])
MEMBERS = 16
GROUPS = 32
RING = 8
CHUNK = 64
PIECE = 72
f32 = jnp.float32
bf16 = jnp.bfloat16
GELU_A = math.sqrt(2.0 / math.pi)
GELU_B = 0.044715


def call(kernel, limit, outs, scratch, *operands, smem=0, far=(), close=(), home=(), copies=0):
    near = pl.BlockSpec(memory_space=pltpu.VMEM)
    away = pl.BlockSpec(memory_space=pltpu.HBM)
    specs = [pl.BlockSpec(memory_space=pltpu.SMEM)] * smem
    specs += [away if i in far else near for i in range(smem, len(operands))]
    kinds = [kind[0] if isinstance(kind, tuple) else kind for _, kind in outs]
    placed = {i: pltpu.VMEM for i in close} | {i: pltpu.HBM for i in (*far, *home)}
    operands = [
        pltpu.with_memory_space_constraint(operand, placed[i]) if i in placed else operand
        for i, operand in enumerate(operands)
    ]
    kept = [pltpu.VMEM(shape, kind) for shape, kind in scratch]
    return pl.pallas_call(
        kernel,
        out_shape=[
            (pltpu.HBM if isinstance(given, tuple) else jax.ShapeDtypeStruct)(shape, kind)
            for (shape, given), kind in zip(outs, kinds)
        ],
        in_specs=specs,
        out_specs=[away if isinstance(kind, tuple) else near for _, kind in outs],
        scratch_shapes=kept + ([pltpu.SemaphoreType.DMA((copies,))] if copies else []),
        compiler_params=pltpu.CompilerParams(vmem_limit_bytes=limit << 20),
    )(*operands)


def started(*pairs, semaphores):
    moves = [
        pltpu.make_async_copy(source, target, semaphores.at[i]) for i, (source, target) in enumerate(pairs)
    ]
    for move in moves:
        move.start()
    return moves


def gain_column(gain_ref):
    row = lax.broadcasted_iota(jnp.int32, (CP, C), 0)
    lane = lax.broadcasted_iota(jnp.int32, (CP, C), 1)
    spread = jnp.where(row == lane, jnp.broadcast_to(gain_ref[...], (CP, C)), 0.0)
    return jnp.sum(spread, axis=1, keepdims=True)


def centred(values):
    real = lax.broadcasted_iota(jnp.int32, (CP, 128), 0) < C
    average = jnp.sum(values, axis=0, keepdims=True) * (1.0 / C)
    centered = jnp.where(real, values - average, 0.0)
    variance = jnp.sum(centered * centered, axis=0, keepdims=True) * (1.0 / C)
    return centered, lax.rsqrt(variance + norm_eps)


def step_of(offset):
    return (offset // 3 - 1) * PITCH + offset % 3 - 1


def tile(index):
    return pl.ds(128 * index, 128)


def lanes_of(height):
    return lax.broadcasted_iota(jnp.int32, (height, 128), 1)


def rows_kernel(
    emb_ref, pert_ref, target_ref, gain_ref, own_ref, up_ref, down_ref, left_ref, right_ref, emb, pert, target, first, second, truth, semaphores,
):
    moves = started((emb_ref, emb), (pert_ref, pert), (target_ref, target), semaphores=semaphores)
    for move, source, wide in zip(moves, (emb, pert, target), (first, second, truth)):
        move.wait()
        wide[...] = source[...].astype(f32).reshape(C * ROWS, COLS)
    rest = jnp.zeros((CP - C, 128), f32)
    gain = gain_column(gain_ref)

    def row_of(source, r):
        return jnp.concatenate([source[pl.ds(r, C, stride=ROWS), :], rest], axis=0)

    lane = lanes_of(CP)
    left, right = jnp.zeros((CP, 128), f32), jnp.zeros((CP, 128), f32)
    for r in range(ROWS):
        parts = row_of(first, r), row_of(second, r)
        goal = row_of(truth, r)
        latent = parts[0] + parts[1]
        own_ref[r] = latent
        own_ref[ROWS + r] = goal
        sides = (latent, SIDE * (RIM + r), SIDE), (goal, SIDE * TALL + BESIDE * (NEAR + r), BESIDE)
        for values, start, width in sides:
            here = (lane >= start) & (lane < start + width)
            left = jnp.where(here, pltpu.roll(values, start % 128, 1), left)
            right = jnp.where(here, pltpu.roll(values, (start + width) % 128, 1), right)
        if RIM <= r < ROWS - RIM:
            continue
        sent, first_row = (up_ref, 0) if r < RIM else (down_ref, ROWS - RIM)
        if r < NEAR or r >= ROWS - NEAR:
            index = r - first_row if r < RIM else r - (ROWS - NEAR)
            sent[index] = parts[0].astype(bf16)
            sent[NEAR + index] = parts[1].astype(bf16)
            sent[2 * NEAR + FAR + index] = goal.astype(bf16)
        else:
            centered, scale = centred(latent)
            index = r - NEAR if r < RIM else r - first_row
            sent[2 * NEAR + index] = (centered * scale * gain).astype(bf16)
    left_ref[...] = left
    right_ref[...] = right


def latent_row(own_ref, top_ref, bottom_ref, row):
    def near(rim_ref, r):
        return rim_ref[r].astype(f32) + rim_ref[NEAR + r].astype(f32)

    if row < FAR:
        return top_ref[2 * NEAR + row].astype(f32)
    if row < RIM:
        return near(top_ref, row - FAR)
    if row < RIM + ROWS:
        return own_ref[row - RIM]
    if row < RIM + ROWS + NEAR:
        return near(bottom_ref, row - RIM - ROWS)
    return bottom_ref[2 * NEAR + row - RIM - ROWS - NEAR].astype(f32)


def truth_row(own_ref, top_ref, bottom_ref, row):
    base = 2 * NEAR + FAR
    if row < NEAR:
        return top_ref[base + row].astype(f32)
    if row < NEAR + ROWS:
        return own_ref[ROWS + row - NEAR]
    return bottom_ref[base + row - NEAR - ROWS].astype(f32)


def columns_kernel(left_ref, right_ref, both_ref):
    both_ref[0] = left_ref[...]
    both_ref[1] = right_ref[...]


def flat_tiles(pieces, first, last, height=CP, base=None):
    lane = lanes_of(height)
    rolled = {}
    for index in range(first, last):
        result = jnp.zeros((height, 128), f32) if base is None else base(index)
        for number, (values, lane_from, flat_to, width) in enumerate(pieces):
            low, high = max(flat_to - 128 * index, 0), min(flat_to + width - 128 * index, 128)
            if low >= high:
                continue
            if number not in rolled:
                shift = (flat_to - lane_from) % 128
                rolled[number] = pltpu.roll(values(), shift, 1) if shift else values()
            result = jnp.where((lane >= low) & (lane < high), rolled[number], result)
        yield index, result


def forward_kernel(
    member_ref, own_ref, top_ref, bottom_ref, left_ref, right_ref, above_ref, below_ref, gain_ref, valid_ref, mine_ref, w1_ref, w2_ref,
    forecast_ref, truth_ref, pre_ref, hidden_ref, window_ref, latent_ref,
    latent, normed, window, hidden, partial, truth, pre_kept, hidden_kept, semaphores,
):
    gain = gain_column(gain_ref)

    def side_of(row, near, rows):
        if row < near:
            return above_ref, row + ROWS
        if row < near + rows:
            return None, row
        return below_ref, row - ROWS

    scaled_sides = {}

    def side(ref, which, far):
        if ref is None:
            return (left_ref, right_ref)[which][...]
        if not far:
            return ref[which]
        if (id(ref), which) not in scaled_sides:
            centered, scale = centred(ref[which])
            scaled_sides[id(ref), which] = centered * scale * gain
        return scaled_sides[id(ref), which]

    pieces, truths = [], []
    for row in range(TALL):
        ref, place = side_of(row, RIM, ROWS)
        far = row < FAR or row >= TALL - FAR
        pieces.append((functools.partial(latent_row, own_ref, top_ref, bottom_ref, row), 0, PITCH * row + SIDE, COLS))
        for which, flat in ((0, PITCH * row), (1, PITCH * row + SIDE + COLS)):
            pieces.append((functools.partial(side, ref, which, far), SIDE * place, flat, SIDE))
    for row in range(ROWS + 2 * NEAR):
        ref, place = side_of(row, NEAR, ROWS)
        flat, lane = PITCH * (row + FAR) + SIDE, SIDE * TALL + BESIDE * place
        truths.append((functools.partial(truth_row, own_ref, top_ref, bottom_ref, row), 0, flat, COLS))
        truths.append((functools.partial(side, ref, 0, False), lane, flat - BESIDE, BESIDE))
        truths.append((functools.partial(side, ref, 1, False), lane, flat + COLS, BESIDE))
    lane = lanes_of(CP)
    inner_low, inner_high = PITCH * FAR, PITCH * (TALL - FAR)
    normed[CP:CI, :] = jnp.zeros((CI - CP, FLAT), f32)
    for index, values in flat_tiles(pieces, 0, TILES):
        latent[:, tile(index)] = values
        start = 128 * index
        if start < inner_high and start + 128 > inner_low:
            centered, scale = centred(values)
            scaled = centered * scale * gain
            if start < inner_low or start + 128 > inner_high:
                inside = (lane >= inner_low - start) & (lane < inner_high - start)
                scaled = jnp.where(inside, scaled, values)
            values = scaled
        normed[0:CP, tile(index)] = values * valid_ref[:, tile(index)]
    own = pl.ds(128 * OWN[0], 128 * (OWN[1] - OWN[0]))
    moves = started((latent.at[:, own], latent_ref), semaphores=semaphores)
    for index, values in flat_tiles(truths, *SPREAD):
        truth[pl.ds(CP * (index - SPREAD[0]), CP), :] = values
    filled = CP * (SPREAD[1] - SPREAD[0])
    truth[filled:, :] = jnp.zeros((MEMBERS * CHUNK - filled, 128), f32)
    truth_ref[...] = truth[pl.ds(pl.multiple_of(member_ref[0] * CHUNK, 8), CHUNK), :]

    for group in range(CI // 16):
        values = normed[16 * group : 16 * group + 16, :]
        for offset in range(9):
            shift = -step_of(offset) % FLAT
            moved = pltpu.roll(values, shift, 1) if shift else values
            window[CI * offset + 16 * group : CI * offset + 16 * group + 16, :] = moved.astype(bf16)
    moves += started((window.at[:, own], window_ref), semaphores=semaphores.at[1:2])

    for number, first in enumerate(range(0, TILES, 4)):
        last = min(first + 4, TILES)
        span = slice(128 * first, 128 * last)
        pre = jnp.dot(w1_ref[...], window[:, span], preferred_element_type=f32)
        low, high = max(first, OWN[0]), min(last, OWN[1])
        if low < high:
            kept = pl.ds(128 * (low - OWN[0]), 128 * (high - low))
            pre_kept[:, kept] = pre[:, 128 * (low - first) : 128 * (high - first)]
            moves += started((pre_kept.at[:, kept], pre_ref.at[:, kept]), semaphores=semaphores.at[number + 3 : number + 4])
        curve = jnp.tanh(GELU_A * (pre + GELU_B * (pre * pre * pre)))
        hidden[:, span] = (0.5 * pre * (1.0 + curve) * valid_ref[:, span]).astype(bf16)
        partial[:, span] = jnp.dot(w2_ref[...], hidden[:, span], preferred_element_type=f32)
    hidden_kept[...] = (hidden[:, 128 * OWN[0] : 128 * OWN[1]].astype(f32) * mine_ref[...]).astype(bf16)
    moves += started((hidden_kept, hidden_ref), semaphores=semaphores.at[2:3])

    for group in range(CP // 8):
        total = None
        for offset in range(9):
            start = CP * offset + 8 * group
            shift = -step_of(offset) % FLAT
            values = partial[start : start + 8, :]
            moved = pltpu.roll(values, shift, 1) if shift else values
            total = moved if total is None else total + moved
        for index in range(*SPREAD):
            start = CP * (index - SPREAD[0]) + 8 * group
            forecast_ref[start : start + 8, :] = (
                total[:, 128 * index : 128 * index + 128] + latent[8 * group : 8 * group + 8, tile(index)]
            )
    forecast_ref[filled:, :] = jnp.zeros((MEMBERS * CHUNK - filled, 128), f32)
    for move in moves:
        move.wait()


def soft_slope(values):
    return values * lax.rsqrt(values * values + soft_eps)


def score_kernel(forecast_ref, truth_ref, grad_ref, grads):
    def body(step, carry):
        span = pl.ds(pl.multiple_of(8 * step, 8), 8)
        truth = truth_ref[span, :]
        values = [forecast_ref[m, span, :] for m in range(MEMBERS)]
        totals = [jnp.zeros((8, 128), f32)] * MEMBERS
        for first in range(MEMBERS):
            for second in range(first):
                slope = soft_slope(values[first] - values[second])
                totals[first] = totals[first] + slope
                totals[second] = totals[second] - slope
        for m in range(MEMBERS):
            grads[m, span, :] = soft_slope(values[m] - truth) - totals[m] * (1.0 / (MEMBERS - 1))
        return carry

    lax.fori_loop(0, CHUNK // 8, body, 0)
    grad_ref[...] = grads[...].astype(bf16)


def flat_lanes(values, start, count):
    index, off = divmod(start - 128 * OWN[0], 128)
    near = pltpu.roll(values(index), 128 - off, 1)
    if index + 1 == count:
        return near
    far = pltpu.roll(values(index + 1), 128 - off, 1)
    return jnp.where(lanes_of(near.shape[0]) < 128 - off, near, far)


def backward_kernel(
    grad_ref, pre_far, hidden_far, window_far, valid_ref, mine_ref, wide_ref, w2_ref,
    grad_pre_ref, own_grad_ref, weights_ref, up_ref, down_ref,
    pre_ref, hidden_ref, window_ref, chunks, grad, window, grad_pre, packed, semaphores,
):
    moves = started((hidden_far, hidden_ref), (pre_far, pre_ref), (window_far, window_ref), semaphores=semaphores)
    for m in range(MEMBERS):
        chunks[CHUNK * m : CHUNK * m + CHUNK, :] = grad_ref[m].astype(f32)
    edge = 128 * SPREAD[0]
    grad[:, 0:edge] = jnp.zeros((CI, edge), f32)
    grad[:, 128 * SPREAD[1] :] = jnp.zeros((CI, FLAT - 128 * SPREAD[1]), f32)
    grad[CP:CI, :] = jnp.zeros((CI - CP, FLAT), f32)
    for index in range(*SPREAD):
        values = chunks[CP * (index - SPREAD[0]) : CP * (index - SPREAD[0]) + CP, :]
        grad[0:CP, tile(index)] = values * valid_ref[:, tile(index)]
    low, high = 128 * OWN[0], 128 * OWN[1]
    for group in range(CI // 16):
        values = grad[16 * group : 16 * group + 16, :]
        for offset in range(9):
            shift = step_of(offset) % FLAT
            moved = pltpu.roll(values, shift, 1) if shift else values
            window[CI * offset + 16 * group : CI * offset + 16 * group + 16, :] = moved[:, low:high].astype(bf16)
    own = pl.ds(low, high - low)
    later = started((grad.at[0:CP, own], own_grad_ref), semaphores=semaphores.at[3:4])
    moves[0].wait()
    across = (((1,), (1,)), ((), ()))
    grad_out = lax.dot_general(window[...], hidden_ref[...], across, preferred_element_type=f32)
    for k in range(9):
        values = grad_out[CI * k : CI * k + C, :]
        packed[C * (9 + k) : C * (10 + k), :] = values[:, 0:128]
        packed[C * (18 + k) : C * (19 + k), 64:128] = values[:, 128:192]
    moves[1].wait()
    for first in range(0, high - low, 512):
        span = slice(first, min(first + 512, high - low))
        grad_hidden = jnp.dot(w2_ref[...], window[:, span], preferred_element_type=f32)
        pre = pre_ref[:, span]
        square = pre * pre
        curve = jnp.tanh(GELU_A * (pre + GELU_B * (square * pre)))
        slope = 0.5 * (1.0 + curve) + 0.5 * pre * (1.0 - curve * curve) * (GELU_A * (1.0 + 3.0 * GELU_B * square))
        grad_pre[:, span] = (grad_hidden * slope * wide_ref[:, span]).astype(bf16)
    later += started((grad_pre, grad_pre_ref), semaphores=semaphores.at[4:5])
    own_pre = (grad_pre[...].astype(f32) * mine_ref[...]).astype(bf16)
    moves[2].wait()
    grad_in = lax.dot_general(window_ref[...], own_pre, across, preferred_element_type=f32)
    for k in range(9):
        values = grad_in[CI * k : CI * k + C, :]
        packed[C * k : C * (k + 1), :] = values[:, 0:128]
        packed[C * (18 + k) : C * (19 + k), 0:64] = values[:, 128:192]
    packed[27 * C :, :] = jnp.zeros((GROUPS * PIECE - 27 * C, 128), f32)
    for place in range(GROUPS):
        weights_ref[place] = packed[PIECE * place : PIECE * place + PIECE, :].astype(bf16)
    for row, sent_ref in ((0, up_ref), (ROWS - 1, down_ref)):
        start = PITCH * (row + RIM) + SIDE - 1
        for half in range(2):
            values = flat_lanes(lambda index: grad_pre[:, tile(index)].astype(f32), start + 128 * half, OWN[1] - OWN[0])
            sent_ref[:, tile(half)] = values.astype(bf16)
    for move in later:
        move.wait()


def states_kernel(
    grad_pre_far, grad_far, latent_far, gain_ref, w1_ref, top_ref, bottom_ref,
    states_ref,
    own_pre, grad, latent, grad_pre, partial, shifted, result, semaphores,
):
    moves = started((grad_pre_far, own_pre), (latent_far, latent), (grad_far, grad), semaphores=semaphores)
    span = 128 * (SPREAD[1] - SPREAD[0])
    inner = slice(128 * (OWN[0] - SPREAD[0]), 128 * (OWN[1] - SPREAD[0]))
    moves[0].wait()

    def base(index):
        if OWN[0] <= index < OWN[1]:
            return own_pre[:, tile(index - OWN[0])].astype(f32)
        return jnp.zeros((HID, 128), f32)

    pieces = []
    for row, strip_ref in ((RIM - 1, top_ref), (RIM + ROWS, bottom_ref)):
        for half, width in ((0, 128), (1, COLS + 2 - 128)):
            values = functools.partial(lambda ref, index: ref[:, tile(index)].astype(f32), strip_ref, half)
            pieces.append((values, 0, PITCH * row + SIDE - 1 + 128 * half, width))
    for index, values in flat_tiles(pieces, *SPREAD, HID, base):
        grad_pre[:, tile(index - SPREAD[0])] = values.astype(bf16)
    for first in range(0, span, 512):
        some = slice(first, min(first + 512, span))
        partial[:, some] = jnp.dot(w1_ref[...], grad_pre[:, some], preferred_element_type=f32)
    for group in range(CP // 8):
        total = None
        for offset in range(9):
            start = CP * offset + 8 * group
            shift = step_of(offset) % span
            values = partial[start : start + 8, :]
            moved = pltpu.roll(values, shift, 1) if shift else values
            total = moved if total is None else total + moved
        shifted[8 * group : 8 * group + 8, :] = total[:, inner]
    gain = gain_column(gain_ref)
    for move in moves[1:]:
        move.wait()
    for index in range(OWN[1] - OWN[0]):
        centered, scale = centred(latent[:, tile(index)])
        unit = centered * scale
        pull = shifted[:, tile(index)] * gain
        mean_pull = jnp.sum(pull, axis=0, keepdims=True) * (1.0 / C)
        mean_both = jnp.sum(pull * unit, axis=0, keepdims=True) * (1.0 / C)
        shifted[:, tile(index)] = grad[:, tile(index)] + scale * (pull - mean_pull - unit * mean_both)
    for row in range(ROWS):
        start = PITCH * (row + RIM) + SIDE
        values = flat_lanes(lambda index: shifted[:, tile(index)], start, OWN[1] - OWN[0])
        result[pl.ds(row, C, stride=ROWS), :] = values[0:C]
    states_ref[...] = result[...].astype(bf16)


def total_kernel(parts_ref, copies_ref):
    total = parts_ref[0].astype(f32)
    for index in range(1, parts_ref.shape[0]):
        total = total + parts_ref[index].astype(f32)
    total = total.astype(bf16)
    for index in range(copies_ref.shape[0]):
        copies_ref[index] = total


def weights_kernel(parts_ref, grad_in_ref, grad_out_ref, packed):
    scale = 1.0 / math.sqrt(MEMBERS * 32 * 512)
    for place in range(GROUPS):
        packed[PIECE * place : PIECE * place + PIECE, :] = parts_ref[place].astype(f32) * scale
    for k in range(9):
        first = packed[C * k : C * (k + 1), :]
        second = packed[C * (9 + k) : C * (10 + k), :]
        shared = packed[C * (18 + k) : C * (19 + k), :]
        grad_out_ref[k, :, 0:128] = second
        grad_out_ref[k, :, 128:192] = shared[:, 64:128]
        grad_in_ref[k, :, 0:128] = first
        grad_in_ref[k, :, 128:192] = shared[:, 0:64]


def neighbours(axis, periodic):
    count = lax.axis_size(axis)
    forward = [(i, i + 1) for i in range(count - 1)]
    if periodic:
        forward.append((count - 1, 0))
    return forward, [(target, source) for source, target in forward]


def swap(values, axes):
    return lax.all_to_all(values, axes, split_axis=0, concat_axis=0, tiled=True)


def on_device(
    embeddings,
    entry_perturbation,
    target,
    feature_scale_factor,
    first_stencil_kernel,
    second_stencil_kernel,
):
    def padded(weight, dim, size):
        pads = [(0, 0)] * 3
        pads[dim] = (0, size - weight.shape[dim])
        return jnp.pad(weight, pads)

    member_axes, plane = ("half", "ring"), ("half", "lat", "lon")
    gain = feature_scale_factor[None]
    block = (C, ROWS, COLS)
    rim = ((3 * NEAR + FAR, CP, 128), bf16)
    own, up, down, to_left, to_right = call(
        rows_kernel,
        6,
        [((2 * ROWS, CP, 128), f32), rim, rim, ((CP, 128), f32), ((CP, 128), f32)],
        [(block, bf16)] * 3 + [((C * ROWS, COLS), f32)] * 3,
        embeddings.reshape(block), entry_perturbation.reshape(block), target, gain,
        far=(0, 1, 2), home=(3,), copies=3,
    )
    forward, backward = neighbours("lat", False)
    top = lax.ppermute(down, "lat", forward)
    bottom = lax.ppermute(up, "lat", backward)
    to_below, to_above = forward, backward
    forward, backward = neighbours("lon", True)
    left = lax.ppermute(to_right, "lon", forward)
    right = lax.ppermute(to_left, "lon", backward)
    (both,) = call(columns_kernel, 6, [((2, CP, 128), f32)], [], left, right, close=(0, 1))
    above = lax.ppermute(both, "lat", to_below)
    below = lax.ppermute(both, "lat", to_above)

    place = jnp.arange(FLAT, dtype=jnp.int32)
    row, column = place // PITCH - RIM, place % PITCH - SIDE
    line = row + ROWS * lax.axis_index("lat")
    valid = ((line >= 0) & (line < ROWS * lax.axis_size("lat"))).astype(f32)[None]
    mine = ((row >= 0) & (row < ROWS) & (column >= 0) & (column < COLS)).astype(f32)[None]
    mine = mine[:, 128 * OWN[0] : 128 * OWN[1]]
    wide = ((row >= 0) & (row < ROWS) & (column >= -1) & (column <= COLS)).astype(f32)[None]
    wide = wide[:, 128 * OWN[0] : 128 * OWN[1]]
    w1_stack = padded(first_stencil_kernel, 2, CI).transpose(1, 0, 2).reshape(HID, 9 * CI)
    w2_stack = padded(second_stencil_kernel, 1, CP).reshape(9 * CP, HID)
    w2_turned = padded(second_stencil_kernel, 1, CI).transpose(2, 0, 1).reshape(HID, 9 * CI)
    w1_turned = padded(first_stencil_kernel.transpose(0, 2, 1), 1, CP).reshape(9 * CP, HID)

    member = lax.axis_index(member_axes).astype(jnp.int32)[None]
    own_lanes = OWN_LANES
    spread_lanes = 128 * (SPREAD[1] - SPREAD[0])
    forecast, truth, pre, hidden, window, latent = call(
        forward_kernel,
        26,
        [
            ((MEMBERS * CHUNK, 128), f32),
            ((CHUNK, 128), f32),
            ((HID, own_lanes), (f32,)),
            ((HID, own_lanes), (bf16,)),
            ((9 * CI, own_lanes), (bf16,)),
            ((CP, own_lanes), (f32,)),
        ],
        [
            ((CP, FLAT), f32),
            ((CI, FLAT), f32),
            ((9 * CI, FLAT), bf16),
            ((HID, FLAT), bf16),
            ((9 * CP, FLAT), f32),
            ((MEMBERS * CHUNK, 128), f32),
            ((HID, own_lanes), f32),
            ((HID, own_lanes), bf16),
        ],
        member, own, top, bottom, left, right, above, below, gain, valid, mine, w1_stack, w2_stack,
        smem=1, close=(1, 2, 3, 4, 5, 6, 7), copies=7,
    )
    spread = swap(forecast.reshape(MEMBERS, CHUNK, 128), member_axes)
    (grads,) = call(
        score_kernel,
        6,
        [((MEMBERS, CHUNK, 128), bf16)],
        [((MEMBERS, CHUNK, 128), f32)],
        spread, truth,
    )
    grads = swap(grads, member_axes)
    strip = ((HID, 256), bf16)
    grad_pre, own_grad, weights, up, down = call(
        backward_kernel,
        22,
        [
            ((HID, own_lanes), (bf16,)),
            ((CP, own_lanes), (f32,)),
            ((GROUPS, PIECE, 128), bf16),
            strip, strip,
        ],
        [
            ((HID, own_lanes), f32),
            ((HID, own_lanes), bf16),
            ((9 * CI, own_lanes), bf16),
            ((MEMBERS * CHUNK, 128), f32),
            ((CI, FLAT), f32),
            ((9 * CI, own_lanes), bf16),
            ((HID, own_lanes), bf16),
            ((GROUPS * PIECE, 128), f32),
        ],
        grads, pre, hidden, window, valid, mine, wide, w2_turned,
        far=(1, 2, 3), copies=5,
    )
    parts = swap(weights, plane)
    forward, backward = neighbours("lat", False)
    parts, top = lax.optimization_barrier((parts, lax.ppermute(down, "lat", forward)))
    bottom = lax.ppermute(up, "lat", backward)
    piece = (PIECE, 128)
    (copies,) = call(total_kernel, 6, [((RING,) + piece, bf16)], [], parts)
    parts, bottom = lax.optimization_barrier((swap(copies, "ring"), bottom))
    (copies,) = call(total_kernel, 6, [((GROUPS,) + piece, bf16)], [], parts)
    (states,) = call(
        states_kernel,
        16,
        [((C * ROWS, COLS), bf16)],
        [
            ((HID, own_lanes), bf16),
            ((CP, own_lanes), f32),
            ((CP, own_lanes), f32),
            ((HID, spread_lanes), bf16),
            ((9 * CP, spread_lanes), f32),
            ((CP, own_lanes), f32),
            ((C * ROWS, COLS), f32),
        ],
        grad_pre, own_grad, latent, gain, w1_turned, top, bottom,
        far=(0, 1, 2), copies=3,
    )
    grad_in, grad_out = call(
        weights_kernel,
        8,
        [((9, C, HID), f32), ((9, C, HID), f32)],
        [((GROUPS * PIECE, 128), f32)],
        swap(copies, plane),
    )
    grad_in = grad_in.transpose(0, 2, 1)
    return (states.reshape(embeddings.shape), grad_in, grad_out)


def solution(mesh):
    places = mesh.devices.reshape(MEMBERS // RING, RING, *mesh.devices.shape[1:])
    fine = jax.sharding.Mesh(places, ("half", "ring", "lat", "lon"))
    whole = P(("half", "ring"), None, "lat", "lon")
    return jax.shard_map(
        on_device,
        mesh=fine,
        in_specs=(whole, whole, P(None, "lat", "lon"), P(), P(), P()),
        out_specs=(whole, P(), P()),
        check_vma=False,
    )
```

```python
import functools
import math

import jax
import jax.numpy as jnp
from jax import lax
from jax.experimental import pallas as pl
from jax.experimental.pallas import tpu as pltpu
from jax.sharding import PartitionSpec as P

soft_eps = 0.01
norm_eps = 1e-05
C = 83
CP = 88
CI = 96
HID = 192
ROWS = 8
COLS = 128
NEAR = 1
FAR = 2
RIM = NEAR + FAR
SIDE = 4
BESIDE = 2
PITCH = COLS + 2 * SIDE
TALL = ROWS + 2 * RIM
TILES = -(-TALL * PITCH // 128)
FLAT = 128 * TILES
SPREAD = (2, 13)
OWN = (3, 12)
OWN_LANES = 128 * (OWN[1] - OWN[0])
MEMBERS = 16
GROUPS = 32
RING = 8
CHUNK = 64
PIECE = 72
f32 = jnp.float32
bf16 = jnp.bfloat16
GELU_A = math.sqrt(2.0 / math.pi)
GELU_B = 0.044715


def call(kernel, limit, outs, scratch, *operands, smem=0, far=(), close=(), home=(), copies=0):
    near = pl.BlockSpec(memory_space=pltpu.VMEM)
    away = pl.BlockSpec(memory_space=pltpu.HBM)
    specs = [pl.BlockSpec(memory_space=pltpu.SMEM)] * smem
    specs += [away if i in far else near for i in range(smem, len(operands))]
    kinds = [kind[0] if isinstance(kind, tuple) else kind for _, kind in outs]
    placed = {i: pltpu.VMEM for i in close} | {i: pltpu.HBM for i in (*far, *home)}
    operands = [
        pltpu.with_memory_space_constraint(operand, placed[i]) if i in placed else operand
        for i, operand in enumerate(operands)
    ]
    kept = [pltpu.VMEM(shape, kind) for shape, kind in scratch]
    return pl.pallas_call(
        kernel,
        out_shape=[
            (pltpu.HBM if isinstance(given, tuple) else jax.ShapeDtypeStruct)(shape, kind)
            for (shape, given), kind in zip(outs, kinds)
        ],
        in_specs=specs,
        out_specs=[away if isinstance(kind, tuple) else near for _, kind in outs],
        scratch_shapes=kept + ([pltpu.SemaphoreType.DMA((copies,))] if copies else []),
        compiler_params=pltpu.CompilerParams(vmem_limit_bytes=limit << 20),
    )(*operands)


def started(*pairs, semaphores):
    moves = [
        pltpu.make_async_copy(source, target, semaphores.at[i]) for i, (source, target) in enumerate(pairs)
    ]
    for move in moves:
        move.start()
    return moves


def gain_column(gain_ref):
    row = lax.broadcasted_iota(jnp.int32, (CP, C), 0)
    lane = lax.broadcasted_iota(jnp.int32, (CP, C), 1)
    spread = jnp.where(row == lane, jnp.broadcast_to(gain_ref[...], (CP, C)), 0.0)
    return jnp.sum(spread, axis=1, keepdims=True)


def centred(values):
    real = lax.broadcasted_iota(jnp.int32, (CP, 128), 0) < C
    average = jnp.sum(values, axis=0, keepdims=True) * (1.0 / C)
    centered = jnp.where(real, values - average, 0.0)
    variance = jnp.sum(centered * centered, axis=0, keepdims=True) * (1.0 / C)
    return centered, lax.rsqrt(variance + norm_eps)


def step_of(offset):
    return (offset // 3 - 1) * PITCH + offset % 3 - 1


def tile(index):
    return pl.ds(128 * index, 128)


def lanes_of(height):
    return lax.broadcasted_iota(jnp.int32, (height, 128), 1)


def rows_kernel(
    emb_ref, pert_ref, target_ref, gain_ref, own_ref, up_ref, down_ref, left_ref, right_ref, emb, pert, target, first, second, truth, semaphores,
):
    moves = started((emb_ref, emb), (pert_ref, pert), (target_ref, target), semaphores=semaphores)
    for move, source, wide in zip(moves, (emb, pert, target), (first, second, truth)):
        move.wait()
        wide[...] = source[...].astype(f32).reshape(C * ROWS, COLS)
    rest = jnp.zeros((CP - C, 128), f32)
    gain = gain_column(gain_ref)

    def row_of(source, r):
        return jnp.concatenate([source[pl.ds(r, C, stride=ROWS), :], rest], axis=0)

    lane = lanes_of(CP)
    left, right = jnp.zeros((CP, 128), f32), jnp.zeros((CP, 128), f32)
    for r in range(ROWS):
        parts = row_of(first, r), row_of(second, r)
        goal = row_of(truth, r)
        latent = parts[0] + parts[1]
        own_ref[r] = latent
        own_ref[ROWS + r] = goal
        sides = (latent, SIDE * (RIM + r), SIDE), (goal, SIDE * TALL + BESIDE * (NEAR + r), BESIDE)
        for values, start, width in sides:
            here = (lane >= start) & (lane < start + width)
            left = jnp.where(here, pltpu.roll(values, start % 128, 1), left)
            right = jnp.where(here, pltpu.roll(values, (start + width) % 128, 1), right)
        if RIM <= r < ROWS - RIM:
            continue
        sent, first_row = (up_ref, 0) if r < RIM else (down_ref, ROWS - RIM)
        if r < NEAR or r >= ROWS - NEAR:
            index = r - first_row if r < RIM else r - (ROWS - NEAR)
            sent[index] = parts[0].astype(bf16)
            sent[NEAR + index] = parts[1].astype(bf16)
            sent[2 * NEAR + FAR + index] = goal.astype(bf16)
        else:
            centered, scale = centred(latent)
            index = r - NEAR if r < RIM else r - first_row
            sent[2 * NEAR + index] = (centered * scale * gain).astype(bf16)
    left_ref[...] = left
    right_ref[...] = right


def latent_row(own_ref, top_ref, bottom_ref, row):
    def near(rim_ref, r):
        return rim_ref[r].astype(f32) + rim_ref[NEAR + r].astype(f32)

    if row < FAR:
        return top_ref[2 * NEAR + row].astype(f32)
    if row < RIM:
        return near(top_ref, row - FAR)
    if row < RIM + ROWS:
        return own_ref[row - RIM]
    if row < RIM + ROWS + NEAR:
        return near(bottom_ref, row - RIM - ROWS)
    return bottom_ref[2 * NEAR + row - RIM - ROWS - NEAR].astype(f32)


def truth_row(own_ref, top_ref, bottom_ref, row):
    base = 2 * NEAR + FAR
    if row < NEAR:
        return top_ref[base + row].astype(f32)
    if row < NEAR + ROWS:
        return own_ref[ROWS + row - NEAR]
    return bottom_ref[base + row - NEAR - ROWS].astype(f32)


def columns_kernel(left_ref, right_ref, both_ref):
    both_ref[0] = left_ref[...]
    both_ref[1] = right_ref[...]


def flat_tiles(pieces, first, last, height=CP, base=None):
    lane = lanes_of(height)
    rolled = {}
    for index in range(first, last):
        result = jnp.zeros((height, 128), f32) if base is None else base(index)
        for number, (values, lane_from, flat_to, width) in enumerate(pieces):
            low, high = max(flat_to - 128 * index, 0), min(flat_to + width - 128 * index, 128)
            if low >= high:
                continue
            if number not in rolled:
                shift = (flat_to - lane_from) % 128
                rolled[number] = pltpu.roll(values(), shift, 1) if shift else values()
            result = jnp.where((lane >= low) & (lane < high), rolled[number], result)
        yield index, result


def forward_kernel(
    own_ref, top_ref, bottom_ref, left_ref, right_ref, above_ref, below_ref, gain_ref, valid_ref, mine_ref, w1_ref, w2_ref,
    forecast_ref, pre_ref, hidden_ref, window_ref, latent_ref,
    latent, normed, window, hidden, partial, pre_kept, hidden_kept, semaphores,
):
    gain = gain_column(gain_ref)

    def side_of(row, near, rows):
        if row < near:
            return above_ref, row + ROWS
        if row < near + rows:
            return None, row
        return below_ref, row - ROWS

    scaled_sides = {}

    def side(ref, which, far):
        if ref is None:
            return (left_ref, right_ref)[which][...]
        if not far:
            return ref[which]
        if (id(ref), which) not in scaled_sides:
            centered, scale = centred(ref[which])
            scaled_sides[id(ref), which] = centered * scale * gain
        return scaled_sides[id(ref), which]

    pieces = []
    for row in range(TALL):
        ref, place = side_of(row, RIM, ROWS)
        far = row < FAR or row >= TALL - FAR
        pieces.append((functools.partial(latent_row, own_ref, top_ref, bottom_ref, row), 0, PITCH * row + SIDE, COLS))
        for which, flat in ((0, PITCH * row), (1, PITCH * row + SIDE + COLS)):
            pieces.append((functools.partial(side, ref, which, far), SIDE * place, flat, SIDE))
    lane = lanes_of(CP)
    inner_low, inner_high = PITCH * FAR, PITCH * (TALL - FAR)
    normed[CP:CI, :] = jnp.zeros((CI - CP, FLAT), f32)
    for index, values in flat_tiles(pieces, 0, TILES):
        latent[:, tile(index)] = values
        start = 128 * index
        if start < inner_high and start + 128 > inner_low:
            centered, scale = centred(values)
            scaled = centered * scale * gain
            if start < inner_low or start + 128 > inner_high:
                inside = (lane >= inner_low - start) & (lane < inner_high - start)
                scaled = jnp.where(inside, scaled, values)
            values = scaled
        normed[0:CP, tile(index)] = values * valid_ref[:, tile(index)]
    own = pl.ds(128 * OWN[0], 128 * (OWN[1] - OWN[0]))
    moves = started((latent.at[:, own], latent_ref), semaphores=semaphores)
    filled = CP * (SPREAD[1] - SPREAD[0])

    for group in range(CI // 16):
        values = normed[16 * group : 16 * group + 16, :]
        for offset in range(9):
            shift = -step_of(offset) % FLAT
            moved = pltpu.roll(values, shift, 1) if shift else values
            window[CI * offset + 16 * group : CI * offset + 16 * group + 16, :] = moved.astype(bf16)
    moves += started((window.at[:, own], window_ref), semaphores=semaphores.at[1:2])

    for number, first in enumerate(range(0, TILES, 4)):
        last = min(first + 4, TILES)
        span = slice(128 * first, 128 * last)
        pre = jnp.dot(w1_ref[...], window[:, span], preferred_element_type=f32)
        low, high = max(first, OWN[0]), min(last, OWN[1])
        if low < high:
            kept = pl.ds(128 * (low - OWN[0]), 128 * (high - low))
            pre_kept[:, kept] = pre[:, 128 * (low - first) : 128 * (high - first)]
            moves += started((pre_kept.at[:, kept], pre_ref.at[:, kept]), semaphores=semaphores.at[number + 3 : number + 4])
        curve = jnp.tanh(GELU_A * (pre + GELU_B * (pre * pre * pre)))
        hidden[:, span] = (0.5 * pre * (1.0 + curve) * valid_ref[:, span]).astype(bf16)
        partial[:, span] = jnp.dot(w2_ref[...], hidden[:, span], preferred_element_type=f32)
    hidden_kept[...] = (hidden[:, 128 * OWN[0] : 128 * OWN[1]].astype(f32) * mine_ref[...]).astype(bf16)
    moves += started((hidden_kept, hidden_ref), semaphores=semaphores.at[2:3])

    for group in range(CP // 8):
        total = None
        for offset in range(9):
            start = CP * offset + 8 * group
            shift = -step_of(offset) % FLAT
            values = partial[start : start + 8, :]
            moved = pltpu.roll(values, shift, 1) if shift else values
            total = moved if total is None else total + moved
        for index in range(*SPREAD):
            start = CP * (index - SPREAD[0]) + 8 * group
            forecast_ref[start : start + 8, :] = (
                total[:, 128 * index : 128 * index + 128] + latent[8 * group : 8 * group + 8, tile(index)]
            )
    forecast_ref[filled:, :] = jnp.zeros((MEMBERS * CHUNK - filled, 128), f32)
    for move in moves:
        move.wait()


def truth_kernel(
    member_ref, own_ref, top_ref, bottom_ref, left_ref, right_ref, above_ref, below_ref, truth_ref, truth,
):
    pieces = []
    for row in range(ROWS + 2 * NEAR):
        sides, place = (left_ref, right_ref), row
        if row < NEAR:
            sides, place = (above_ref.at[0], above_ref.at[1]), row + ROWS
        elif row >= NEAR + ROWS:
            sides, place = (below_ref.at[0], below_ref.at[1]), row - ROWS
        flat, lane = PITCH * (row + FAR) + SIDE, SIDE * TALL + BESIDE * place
        pieces.append((functools.partial(truth_row, own_ref, top_ref, bottom_ref, row), 0, flat, COLS))
        for ref, flat_side in zip(sides, (flat - BESIDE, flat + COLS)):
            pieces.append((functools.partial(lambda ref: ref[...], ref), lane, flat_side, BESIDE))
    for index, values in flat_tiles(pieces, *SPREAD):
        truth[pl.ds(CP * (index - SPREAD[0]), CP), :] = values
    filled = CP * (SPREAD[1] - SPREAD[0])
    truth[filled:, :] = jnp.zeros((MEMBERS * CHUNK - filled, 128), f32)
    truth_ref[...] = truth[pl.ds(pl.multiple_of(member_ref[0] * CHUNK, 8), CHUNK), :]


def soft_slope(values):
    return values * lax.rsqrt(values * values + soft_eps)


def score_kernel(forecast_ref, truth_ref, grad_ref, grads):
    def body(step, carry):
        span = pl.ds(pl.multiple_of(8 * step, 8), 8)
        truth = truth_ref[span, :]
        values = [forecast_ref[m, span, :] for m in range(MEMBERS)]
        totals = [jnp.zeros((8, 128), f32)] * MEMBERS
        for first in range(MEMBERS):
            for second in range(first):
                slope = soft_slope(values[first] - values[second])
                totals[first] = totals[first] + slope
                totals[second] = totals[second] - slope
        for m in range(MEMBERS):
            grads[m, span, :] = soft_slope(values[m] - truth) - totals[m] * (1.0 / (MEMBERS - 1))
        return carry

    lax.fori_loop(0, CHUNK // 8, body, 0)
    grad_ref[...] = grads[...].astype(bf16)


def flat_lanes(values, start, count):
    index, off = divmod(start - 128 * OWN[0], 128)
    near = pltpu.roll(values(index), 128 - off, 1)
    if index + 1 == count:
        return near
    far = pltpu.roll(values(index + 1), 128 - off, 1)
    return jnp.where(lanes_of(near.shape[0]) < 128 - off, near, far)


def backward_kernel(
    grad_ref, pre_far, hidden_far, window_far, valid_ref, mine_ref, wide_ref, w2_ref,
    grad_pre_ref, own_grad_ref, weights_ref, up_ref, down_ref,
    pre_ref, hidden_ref, window_ref, chunks, grad, window, grad_pre, packed, semaphores,
):
    moves = started((hidden_far, hidden_ref), (pre_far, pre_ref), (window_far, window_ref), semaphores=semaphores)
    for m in range(MEMBERS):
        chunks[CHUNK * m : CHUNK * m + CHUNK, :] = grad_ref[m].astype(f32)
    edge = 128 * SPREAD[0]
    grad[:, 0:edge] = jnp.zeros((CI, edge), f32)
    grad[:, 128 * SPREAD[1] :] = jnp.zeros((CI, FLAT - 128 * SPREAD[1]), f32)
    grad[CP:CI, :] = jnp.zeros((CI - CP, FLAT), f32)
    for index in range(*SPREAD):
        values = chunks[CP * (index - SPREAD[0]) : CP * (index - SPREAD[0]) + CP, :]
        grad[0:CP, tile(index)] = values * valid_ref[:, tile(index)]
    low, high = 128 * OWN[0], 128 * OWN[1]
    for group in range(CI // 16):
        values = grad[16 * group : 16 * group + 16, :]
        for offset in range(9):
            shift = step_of(offset) % FLAT
            moved = pltpu.roll(values, shift, 1) if shift else values
            window[CI * offset + 16 * group : CI * offset + 16 * group + 16, :] = moved[:, low:high].astype(bf16)
    own = pl.ds(low, high - low)
    later = started((grad.at[0:CP, own], own_grad_ref), semaphores=semaphores.at[3:4])
    moves[0].wait()
    across = (((1,), (1,)), ((), ()))
    grad_out = lax.dot_general(window[...], hidden_ref[...], across, preferred_element_type=f32)
    for k in range(9):
        values = grad_out[CI * k : CI * k + C, :]
        packed[C * (9 + k) : C * (10 + k), :] = values[:, 0:128]
        packed[C * (18 + k) : C * (19 + k), 64:128] = values[:, 128:192]
    moves[1].wait()
    for first in range(0, high - low, 512):
        span = slice(first, min(first + 512, high - low))
        grad_hidden = jnp.dot(w2_ref[...], window[:, span], preferred_element_type=f32)
        pre = pre_ref[:, span]
        square = pre * pre
        curve = jnp.tanh(GELU_A * (pre + GELU_B * (square * pre)))
        slope = 0.5 * (1.0 + curve) + 0.5 * pre * (1.0 - curve * curve) * (GELU_A * (1.0 + 3.0 * GELU_B * square))
        grad_pre[:, span] = (grad_hidden * slope * wide_ref[:, span]).astype(bf16)
    later += started((grad_pre, grad_pre_ref), semaphores=semaphores.at[4:5])
    own_pre = (grad_pre[...].astype(f32) * mine_ref[...]).astype(bf16)
    moves[2].wait()
    grad_in = lax.dot_general(window_ref[...], own_pre, across, preferred_element_type=f32)
    for k in range(9):
        values = grad_in[CI * k : CI * k + C, :]
        packed[C * k : C * (k + 1), :] = values[:, 0:128]
        packed[C * (18 + k) : C * (19 + k), 0:64] = values[:, 128:192]
    packed[27 * C :, :] = jnp.zeros((GROUPS * PIECE - 27 * C, 128), f32)
    for place in range(GROUPS):
        weights_ref[place] = packed[PIECE * place : PIECE * place + PIECE, :].astype(bf16)
    for row, sent_ref in ((0, up_ref), (ROWS - 1, down_ref)):
        start = PITCH * (row + RIM) + SIDE - 1
        for half in range(2):
            values = flat_lanes(lambda index: grad_pre[:, tile(index)].astype(f32), start + 128 * half, OWN[1] - OWN[0])
            sent_ref[:, tile(half)] = values.astype(bf16)
    for move in later:
        move.wait()


def states_kernel(
    grad_pre_far, grad_far, latent_far, gain_ref, w1_ref, top_ref, bottom_ref,
    states_ref,
    own_pre, grad, latent, grad_pre, partial, shifted, result, semaphores,
):
    moves = started((grad_pre_far, own_pre), (latent_far, latent), (grad_far, grad), semaphores=semaphores)
    span = 128 * (SPREAD[1] - SPREAD[0])
    inner = slice(128 * (OWN[0] - SPREAD[0]), 128 * (OWN[1] - SPREAD[0]))
    moves[0].wait()

    def base(index):
        if OWN[0] <= index < OWN[1]:
            return own_pre[:, tile(index - OWN[0])].astype(f32)
        return jnp.zeros((HID, 128), f32)

    pieces = []
    for row, strip_ref in ((RIM - 1, top_ref), (RIM + ROWS, bottom_ref)):
        for half, width in ((0, 128), (1, COLS + 2 - 128)):
            values = functools.partial(lambda ref, index: ref[:, tile(index)].astype(f32), strip_ref, half)
            pieces.append((values, 0, PITCH * row + SIDE - 1 + 128 * half, width))
    for index, values in flat_tiles(pieces, *SPREAD, HID, base):
        grad_pre[:, tile(index - SPREAD[0])] = values.astype(bf16)
    for first in range(0, span, 512):
        some = slice(first, min(first + 512, span))
        partial[:, some] = jnp.dot(w1_ref[...], grad_pre[:, some], preferred_element_type=f32)
    for group in range(CP // 8):
        total = None
        for offset in range(9):
            start = CP * offset + 8 * group
            shift = step_of(offset) % span
            values = partial[start : start + 8, :]
            moved = pltpu.roll(values, shift, 1) if shift else values
            total = moved if total is None else total + moved
        shifted[8 * group : 8 * group + 8, :] = total[:, inner]
    gain = gain_column(gain_ref)
    for move in moves[1:]:
        move.wait()
    for index in range(OWN[1] - OWN[0]):
        centered, scale = centred(latent[:, tile(index)])
        unit = centered * scale
        pull = shifted[:, tile(index)] * gain
        mean_pull = jnp.sum(pull, axis=0, keepdims=True) * (1.0 / C)
        mean_both = jnp.sum(pull * unit, axis=0, keepdims=True) * (1.0 / C)
        shifted[:, tile(index)] = grad[:, tile(index)] + scale * (pull - mean_pull - unit * mean_both)
    for row in range(ROWS):
        start = PITCH * (row + RIM) + SIDE
        values = flat_lanes(lambda index: shifted[:, tile(index)], start, OWN[1] - OWN[0])
        result[pl.ds(row, C, stride=ROWS), :] = values[0:C]
    states_ref[...] = result[...].astype(bf16)


def total_kernel(parts_ref, copies_ref):
    total = parts_ref[0].astype(f32)
    for index in range(1, parts_ref.shape[0]):
        total = total + parts_ref[index].astype(f32)
    total = total.astype(bf16)
    for index in range(copies_ref.shape[0]):
        copies_ref[index] = total


def weights_kernel(parts_ref, grad_in_ref, grad_out_ref, packed):
    scale = 1.0 / math.sqrt(MEMBERS * 32 * 512)
    for place in range(GROUPS):
        packed[PIECE * place : PIECE * place + PIECE, :] = parts_ref[place].astype(f32) * scale
    for k in range(9):
        first = packed[C * k : C * (k + 1), :]
        second = packed[C * (9 + k) : C * (10 + k), :]
        shared = packed[C * (18 + k) : C * (19 + k), :]
        grad_out_ref[k, :, 0:128] = second
        grad_out_ref[k, :, 128:192] = shared[:, 64:128]
        grad_in_ref[k, :, 0:128] = first
        grad_in_ref[k, :, 128:192] = shared[:, 0:64]


def neighbours(axis, periodic):
    count = lax.axis_size(axis)
    forward = [(i, i + 1) for i in range(count - 1)]
    if periodic:
        forward.append((count - 1, 0))
    return forward, [(target, source) for source, target in forward]


def swap(values, axes):
    return lax.all_to_all(values, axes, split_axis=0, concat_axis=0, tiled=True)


def on_device(
    embeddings,
    entry_perturbation,
    target,
    feature_scale_factor,
    first_stencil_kernel,
    second_stencil_kernel,
):
    def padded(weight, dim, size):
        pads = [(0, 0)] * 3
        pads[dim] = (0, size - weight.shape[dim])
        return jnp.pad(weight, pads)

    member_axes, plane = ("half", "ring"), ("half", "lat", "lon")
    gain = feature_scale_factor[None]
    block = (C, ROWS, COLS)
    rim = ((3 * NEAR + FAR, CP, 128), bf16)
    own, up, down, to_left, to_right = call(
        rows_kernel,
        6,
        [((2 * ROWS, CP, 128), f32), rim, rim, ((CP, 128), f32), ((CP, 128), f32)],
        [(block, bf16)] * 3 + [((C * ROWS, COLS), f32)] * 3,
        embeddings.reshape(block), entry_perturbation.reshape(block), target, gain,
        far=(0, 1, 2), home=(3,), copies=3,
    )
    forward, backward = neighbours("lat", False)
    top = lax.ppermute(down, "lat", forward)
    bottom = lax.ppermute(up, "lat", backward)
    to_below, to_above = forward, backward
    forward, backward = neighbours("lon", True)
    left = lax.ppermute(to_right, "lon", forward)
    right = lax.ppermute(to_left, "lon", backward)
    (both,) = call(columns_kernel, 6, [((2, CP, 128), f32)], [], left, right, close=(0, 1))
    above = lax.ppermute(both, "lat", to_below)
    below = lax.ppermute(both, "lat", to_above)

    place = jnp.arange(FLAT, dtype=jnp.int32)
    row, column = place // PITCH - RIM, place % PITCH - SIDE
    line = row + ROWS * lax.axis_index("lat")
    valid = ((line >= 0) & (line < ROWS * lax.axis_size("lat"))).astype(f32)[None]
    mine = ((row >= 0) & (row < ROWS) & (column >= 0) & (column < COLS)).astype(f32)[None]
    mine = mine[:, 128 * OWN[0] : 128 * OWN[1]]
    wide = ((row >= 0) & (row < ROWS) & (column >= -1) & (column <= COLS)).astype(f32)[None]
    wide = wide[:, 128 * OWN[0] : 128 * OWN[1]]
    w1_stack = padded(first_stencil_kernel, 2, CI).transpose(1, 0, 2).reshape(HID, 9 * CI)
    w2_stack = padded(second_stencil_kernel, 1, CP).reshape(9 * CP, HID)
    w2_turned = padded(second_stencil_kernel, 1, CI).transpose(2, 0, 1).reshape(HID, 9 * CI)
    w1_turned = padded(first_stencil_kernel.transpose(0, 2, 1), 1, CP).reshape(9 * CP, HID)

    member = lax.axis_index(member_axes).astype(jnp.int32)[None]
    own_lanes = OWN_LANES
    spread_lanes = 128 * (SPREAD[1] - SPREAD[0])
    forecast, pre, hidden, window, latent = call(
        forward_kernel,
        26,
        [
            ((MEMBERS * CHUNK, 128), f32),
            ((HID, own_lanes), (f32,)),
            ((HID, own_lanes), (bf16,)),
            ((9 * CI, own_lanes), (bf16,)),
            ((CP, own_lanes), (f32,)),
        ],
        [
            ((CP, FLAT), f32),
            ((CI, FLAT), f32),
            ((9 * CI, FLAT), bf16),
            ((HID, FLAT), bf16),
            ((9 * CP, FLAT), f32),
            ((HID, own_lanes), f32),
            ((HID, own_lanes), bf16),
        ],
        own, top, bottom, left, right, above, below, gain, valid, mine, w1_stack, w2_stack,
        close=(0, 1, 2, 3, 4, 5, 6), copies=7,
    )
    (truth,) = call(
        truth_kernel,
        8,
        [((CHUNK, 128), f32)],
        [((MEMBERS * CHUNK, 128), f32)],
        member, own, top, bottom, left, right, above, below,
        smem=1,
    )
    spread = swap(forecast.reshape(MEMBERS, CHUNK, 128), member_axes)
    (grads,) = call(
        score_kernel,
        6,
        [((MEMBERS, CHUNK, 128), bf16)],
        [((MEMBERS, CHUNK, 128), f32)],
        spread, truth,
    )
    grads = swap(grads, member_axes)
    strip = ((HID, 256), bf16)
    grad_pre, own_grad, weights, up, down = call(
        backward_kernel,
        22,
        [
            ((HID, own_lanes), (bf16,)),
            ((CP, own_lanes), (f32,)),
            ((GROUPS, PIECE, 128), bf16),
            strip, strip,
        ],
        [
            ((HID, own_lanes), f32),
            ((HID, own_lanes), bf16),
            ((9 * CI, own_lanes), bf16),
            ((MEMBERS * CHUNK, 128), f32),
            ((CI, FLAT), f32),
            ((9 * CI, own_lanes), bf16),
            ((HID, own_lanes), bf16),
            ((GROUPS * PIECE, 128), f32),
        ],
        grads, pre, hidden, window, valid, mine, wide, w2_turned,
        far=(1, 2, 3), copies=5,
    )
    parts = swap(weights, plane)
    forward, backward = neighbours("lat", False)
    parts, top, bottom = lax.optimization_barrier(
        (parts, lax.ppermute(down, "lat", forward), lax.ppermute(up, "lat", backward))
    )
    piece = (PIECE, 128)
    (copies,) = call(total_kernel, 6, [((RING,) + piece, bf16)], [], parts)
    (copies,) = call(total_kernel, 6, [((GROUPS,) + piece, bf16)], [], swap(copies, "ring"))
    (states,) = call(
        states_kernel,
        16,
        [((C * ROWS, COLS), bf16)],
        [
            ((HID, own_lanes), bf16),
            ((CP, own_lanes), f32),
            ((CP, own_lanes), f32),
            ((HID, spread_lanes), bf16),
            ((9 * CP, spread_lanes), f32),
            ((CP, own_lanes), f32),
            ((C * ROWS, COLS), f32),
        ],
        grad_pre, own_grad, latent, gain, w1_turned, top, bottom,
        far=(0, 1, 2), copies=3,
    )
    grad_in, grad_out = call(
        weights_kernel,
        8,
        [((9, C, HID), f32), ((9, C, HID), f32)],
        [((GROUPS * PIECE, 128), f32)],
        swap(copies, plane),
    )
    grad_in = grad_in.transpose(0, 2, 1)
    return (states.reshape(embeddings.shape), grad_in, grad_out)


def solution(mesh):
    places = mesh.devices.reshape(MEMBERS // RING, RING, *mesh.devices.shape[1:])
    fine = jax.sharding.Mesh(places, ("half", "ring", "lat", "lon"))
    whole = P(("half", "ring"), None, "lat", "lon")
    return jax.shard_map(
        on_device,
        mesh=fine,
        in_specs=(whole, whole, P(None, "lat", "lon"), P(), P(), P()),
        out_specs=(whole, P(), P()),
        check_vma=False,
    )
```
